32 devices in a mesh: batch: 8 (over z, y), head: 4 (over x, core).
Axes of the slice: x: 2, y: 2, z: 4, core: 2. Of those that a mesh axis runs over, the one named last changes fastest.
Arguments:
- post_stream: bfloat16 [32768, 512], P(('batch', 'head')), may hold values from -6 to 6
- dual_stream: float32 [32768, 512], P(('batch', 'head')), may hold values from -12 to 12
- post_cotangent: bfloat16 [32768, 512], P(('batch', 'head')), may hold values from -6 to 6
- dual_cotangent: bfloat16 [32768, 512], P(('batch', 'head')), may hold values from -6 to 6
- seq_lengths: int32 [32], P('batch'), may hold values from 64 to 1024, as said below
- owner_slots: int32 [8], replicated, may hold values from 0 to 7, each once
- weights: float32 [512, 6144], P('batch', 'head')
- first_moment: float32 [512, 6144], P('batch', 'head'), as said below
- second_moment: float32 [512, 6144], P('batch', 'head'), as said below
- norm_gain: float32 [2, 512], replicated, may hold values from 0.5 to 1.5
- norm_bias: float32 [2, 512], replicated, may hold values from -2 to 2
- norm_first: float32 [4, 512], replicated, may hold values from -80 to 80
- norm_second: float32 [4, 512], replicated, may hold values from 19.6608 to 78.6432
Outputs:
- post_out: bfloat16 [32768, 512], P(('batch', 'head'))
- dual_out: float32 [32768, 512], P(('batch', 'head'))
- post_grad: float32 [32768, 512], P(('batch', 'head'))
- new_first: float32 [512, 6144], P('batch', 'head')
- new_second: float32 [512, 6144], P('batch', 'head')
- new_weights: float32 [512, 6144], P('batch', 'head')
- norm_first_out: float32 [4, 512], replicated
- norm_second_out: float32 [4, 512], replicated
- norm_out: float32 [4, 512], replicated
The draws below stay inside these ranges and needn't reach their ends.
Inputs may be any that keep to these rules, and one draw needn't show every extreme that they name: `seq_lengths`: in each aligned group of 4 sequences (those of one batch index) one sequence has all 1024 tokens valid. `owner_slots`: each row block owned by exactly one batch index. `first_moment`: entries of both signs. `second_moment`: entries positive.
All inputs are finite; a program needn't handle non-finite values.
Results may differ from the reference program's by a relative error of at most 0.023.
Values may be sent and summed in bfloat16 or wider, within the bound.
A program may use at most 192 MiB of HBM per device.

```python
import math
import jax
import jax.numpy as jnp
from jax import lax

D = 512
FF = 2048
NHEADS = 8
DH = 64
SEQ_LEN = 1024
STEP = 10
GROUPW = 768
TOKENS = 32768
SEQS = 32
SEQS_G = 4
N_BATCH = 8


def draw_seq_lengths(key, part):
    key = jax.random.fold_in(key, 1)
    first_key, second_key = jax.random.split(key)
    groups = SEQS // SEQS_G
    base_lengths = jax.random.randint(first_key, (groups, SEQS_G), SEQ_LEN // 16, SEQ_LEN + 1)
    chosen = jax.random.randint(second_key, (groups, 1), 0, SEQS_G)
    column_ids = jnp.arange(SEQS_G, dtype=jnp.int32)[None, :]
    full_lengths = jnp.where(column_ids == chosen, SEQ_LEN, base_lengths)
    return full_lengths.reshape(SEQS).astype(jnp.int32)


def draw_weights(key, part):
    key = jax.random.fold_in(key, 2)
    values = jnp.clip(jax.random.normal(key, (D, NHEADS * GROUPW), jnp.float32), -6.0, 6.0)
    column = jnp.arange(NHEADS * GROUPW) % GROUPW
    scale_in = D ** (-0.5)
    scale_out = (SEQ_LEN / 4.0) ** 0.5 * D ** (-0.5)
    scale_down = FF ** (-0.5)
    scales = jnp.where(column < 3 * DH, scale_in, jnp.where(column < 4 * DH, scale_out, jnp.where(column < 4 * DH + FF // NHEADS, scale_in, scale_down)))
    return (values * scales[None, :]).astype(jnp.float32)


def gradient_sizes():
    column = jnp.arange(NHEADS * GROUPW) % GROUPW
    size_qkv = 0.9
    size_out = 1.9 * SEQ_LEN ** (-0.5)
    size_up = 0.3
    size_down = 0.6
    sizes = jnp.where(column < 3 * DH, size_qkv, jnp.where(column < 4 * DH, size_out, jnp.where(column < 4 * DH + FF // NHEADS, size_up, size_down)))
    return (sizes * TOKENS ** 0.5).astype(jnp.float32)


def draw_first_moment(key, part):
    key = jax.random.fold_in(key, 3)
    values = jnp.clip(jax.random.normal(key, (D, NHEADS * GROUPW), jnp.float32), -6.0, 6.0)
    return (values * (0.111 * gradient_sizes())[None, :]).astype(jnp.float32)


def draw_second_moment(key, part):
    key = jax.random.fold_in(key, 4)
    factor = jnp.exp(jax.random.uniform(key, (D, NHEADS * GROUPW), jnp.float32, 0.0, jnp.log(4.0)))
    sizes = gradient_sizes()
    return (factor * (0.001 * sizes * sizes)[None, :]).astype(jnp.float32)


def level_of(key, extent, cuts, least, top_value):
    def one(position, parts):
        steps = jax.random.uniform(jax.random.fold_in(jax.random.fold_in(key, 6), position), (parts,), jnp.float32, least / len(cuts), top_value / len(cuts))
        return jnp.repeat(jnp.exp(steps), extent[position] // parts).reshape((-1,) + (1,) * (len(extent) - position - 1))

    level = one(*cuts[0])
    for cut in cuts[1:]:
        level = level * one(*cut)
    return level


def bell_draw(key, dims, spread, most, cuts=(), held_as=jnp.bfloat16):
    gain = level_of(key, dims, cuts, -0.22, 0.18) if cuts else 1.0
    array = jax.random.normal(key, dims, jnp.float32) * spread * gain
    return jnp.minimum(jnp.maximum(array, -most), most).astype(held_as)


def setup_inputs(seed: int = 0) -> dict:
    key_list = jax.random.split(jax.random.key(seed), 14)
    return {
        "post_stream": bell_draw(key_list[0], (TOKENS, D), 1.0, 6.0, ((0, 32),)),
        "dual_stream": bell_draw(key_list[1], (TOKENS, D), 2.0, 12.0, ((0, 32),), jnp.float32),
        "post_cotangent": bell_draw(key_list[2], (TOKENS, D), 1.0, 6.0, ((0, 32),)),
        "dual_cotangent": bell_draw(key_list[3], (TOKENS, D), 1.0, 6.0, ((0, 32),)),
        "seq_lengths": draw_seq_lengths(jax.random.fold_in(key_list[13], 71), 0),
        "owner_slots": jax.random.permutation(key_list[5], N_BATCH).astype(jnp.int32),
        "weights": draw_weights(jax.random.fold_in(key_list[13], 71), 0),
        "first_moment": draw_first_moment(jax.random.fold_in(key_list[13], 71), 0),
        "second_moment": draw_second_moment(jax.random.fold_in(key_list[13], 71), 0),
        "norm_gain": jnp.clip(1.0 + 0.1 * jax.random.normal(key_list[9], (2, D), jnp.float32), 0.5, 1.5),
        "norm_bias": bell_draw(key_list[10], (2, D), 0.3, 2.0, (), jnp.float32),
        "norm_first": bell_draw(key_list[11], (4, D), (0.08 * TOKENS ** 0.5), 80.0, (), jnp.float32),
        "norm_second": jnp.clip(jnp.exp(jax.random.uniform(key_list[12], (4, D), jnp.float32, math.log(19.6608), math.log(78.6432))), 19.6608, 78.6432),
    }


@jax.custom_vjp
def low(v):
    return lax.optimization_barrier(v.astype(jnp.bfloat16)).astype(jnp.float32)

@jax.custom_vjp
def low_back(v):
    return v

def low_keep(v):
    return (low(v), None)

def low_pass(kept, grad):
    return (grad,)

def back_keep(v):
    return (v, None)

def back_low(kept, grad):
    return (low(grad),)
low.defvjp(low_keep, low_pass)
low_back.defvjp(back_keep, back_low)
HIGHEST = lax.Precision.HIGHEST
BETA_FIRST = 0.9
BETA_SECOND = 0.999
ADAM_EPSILON = 1e-08
WEIGHT_DECAY = 0.1
WEIGHT_RATE = 0.2
NORM_RATE = 0.2
NORM_EPSILON = 1e-05
MASK_VALUE = -1000000000.0

def rounded(value):
    return low(low_back(value))

def layer_norm(value, gain_row, bias_row):
    average = lax.optimization_barrier(jnp.mean(value, axis=-1, keepdims=True))
    centred = value - average
    variance = lax.optimization_barrier(jnp.mean(centred * centred, axis=-1, keepdims=True))
    return centred * lax.rsqrt(variance + NORM_EPSILON) * gain_row + bias_row

def slot_inverse(owner_slots):
    slot_ids = jnp.arange(N_BATCH, dtype=jnp.int32)
    matches = owner_slots[None, :] == slot_ids[:, None]
    return lax.optimization_barrier(jnp.sum(jnp.where(matches, slot_ids[None, :], 0), axis=1)).astype(jnp.int32)

def attend(sequence_block):
    queries, key_rows, value_rows, length = sequence_block
    scores = jnp.einsum('qhd,khd->hqk', queries, key_rows, precision=HIGHEST) * DH ** (-0.5)
    scores = low_back(scores)
    kept_keys = jnp.arange(SEQ_LEN, dtype=jnp.int32) < length
    scores = jnp.where(kept_keys[None, None, :], scores, MASK_VALUE)
    soft_weights = low(jax.nn.softmax(scores, axis=-1))
    return jnp.einsum('hqk,khd->qhd', soft_weights, value_rows, precision=HIGHEST)

def adam_update(param, grad, first, second, rate, decay):
    first_new = BETA_FIRST * first + (1.0 - BETA_FIRST) * grad
    second_new = BETA_SECOND * second + (1.0 - BETA_SECOND) * grad * grad
    first_hat = first_new / (1.0 - BETA_FIRST ** STEP)
    second_hat = second_new / (1.0 - BETA_SECOND ** STEP)
    param_new = param - rate * (first_hat / (jnp.sqrt(second_hat) + ADAM_EPSILON) + decay * param)
    return (first_new, second_new, param_new)

def reference(post_stream, dual_stream, post_cotangent, dual_cotangent, seq_lengths, owner_slots, weights, first_moment, second_moment, norm_gain, norm_bias, norm_first, norm_second):
    inverse = slot_inverse(owner_slots)
    hidden_group = FF // NHEADS

    def forward(post_in, dual_in, weight_in, gain_in, bias_in):
        blocks = low(weight_in).reshape(N_BATCH, D // N_BATCH, NHEADS * GROUPW)
        full_table = jnp.take(blocks, inverse, axis=0).reshape(D, NHEADS, GROUPW)
        w_qkv = full_table[:, :, :3 * DH]
        w_out = full_table[:, :, 3 * DH:4 * DH].reshape(D, D)
        w_up = full_table[:, :, 4 * DH:4 * DH + hidden_group].reshape(D, FF)
        w_down = full_table[:, :, 4 * DH + hidden_group:].reshape(D, FF)
        projected = rounded(jnp.einsum('td,dhc->thc', post_in, w_qkv, precision=HIGHEST))
        seq_shape = (SEQS, SEQ_LEN, NHEADS, DH)
        queries = projected[:, :, :DH].reshape(seq_shape)
        key_rows = projected[:, :, DH:2 * DH].reshape(seq_shape)
        value_rows = projected[:, :, 2 * DH:].reshape(seq_shape)
        attended = lax.map(jax.checkpoint(attend), (queries, key_rows, value_rows, seq_lengths))
        attended = rounded(attended.reshape(TOKENS, D))
        branch = low_back(jnp.einsum('tc,dc->td', attended, w_out, precision=HIGHEST))
        middle = layer_norm(post_in + branch, gain_in[0], bias_in[0])
        dual_middle = dual_in + branch
        hidden_pre = low_back(jnp.einsum('td,df->tf', low(middle), w_up, precision=HIGHEST))
        hidden = low(jax.nn.gelu(hidden_pre, approximate=False))
        feed = low_back(jnp.einsum('tf,df->td', hidden, w_down, precision=HIGHEST))
        post_new = layer_norm(middle + feed, gain_in[1], bias_in[1])
        return (post_new, dual_middle + feed)
    positions = jnp.arange(TOKENS, dtype=jnp.int32)
    length_row = jnp.take(seq_lengths, positions // SEQ_LEN)
    valid = (positions % SEQ_LEN < length_row).astype(jnp.float32)[:, None]
    outputs, pullback = jax.vjp(forward, post_stream.astype(jnp.float32), dual_stream, weights, norm_gain, norm_bias)
    post_new, dual_new = outputs
    grads = pullback((post_cotangent.astype(jnp.float32) * valid, dual_cotangent.astype(jnp.float32) * valid))
    post_grad, dual_unused, weight_grad, gain_grad, bias_grad = grads
    new_first, new_second, new_weights = adam_update(weights, weight_grad, first_moment, second_moment, WEIGHT_RATE, WEIGHT_DECAY)
    norm_params = jnp.concatenate([norm_gain, norm_bias], axis=0)
    norm_grads = jnp.concatenate([gain_grad, bias_grad], axis=0)
    norm_first_out, norm_second_out, norm_out = adam_update(norm_params, norm_grads, norm_first, norm_second, NORM_RATE, 0.0)
    return (post_new.astype(jnp.bfloat16), dual_new, post_grad, new_first, new_second, new_weights, norm_first_out, norm_second_out, norm_out)
```

```python
import functools
import math

import jax
import jax.numpy as jnp
from jax import lax
from jax.experimental import pallas as pl
from jax.experimental.pallas import tpu as pltpu
from jax.sharding import PartitionSpec as P

D = 512
FF = 2048
NHEADS = 8
DH = 64
SEQ_LEN = 1024
STEP = 10
GROUPW = 768
PART = 256

BETA_FIRST = 0.9
BETA_SECOND = 0.999
ADAM_EPSILON = 1e-08
WEIGHT_DECAY = 0.1
WEIGHT_RATE = 0.2
NORM_RATE = 0.2
NORM_EPSILON = 1e-05
MASK_VALUE = -1000000000.0

MESH = pl.DeviceIdType.MESH
F32 = jnp.float32
BF = jnp.bfloat16
VMEM_BYTES = 60 << 20


def dot(a, b, ca, cb):
    return lax.dot_general(a, b, (((ca,), (cb,)), ((), ())), preferred_element_type=F32)


class Place:
    def __init__(self, batches, heads):
        self.X = self.Y = heads // 2
        self.Z = batches // self.Y
        self.batches, self.heads = batches, heads
        batch, head = lax.axis_index("batch"), lax.axis_index("head")
        self.j = batch
        self.z, self.y = batch // self.Y, batch % self.Y
        self.x, self.c = head // 2, head % 2
        self.xs = [lax.rem(self.x + d, self.X) for d in range(1, self.X)]
        self.ys = [lax.rem(self.y + d, self.Y) for d in range(1, self.Y)]
        self.zs = [lax.rem(self.z + d, self.Z) for d in range(1, self.Z)]

    def dev(self, z=None, y=None, x=None, c=None):
        z = self.z if z is None else z
        y = self.y if y is None else y
        x = self.x if x is None else x
        c = self.c if c is None else c
        return (z * self.Y + y, x * 2 + c)

    def greet(self, devices):
        barrier = pltpu.get_barrier_semaphore()
        for device in devices:
            pl.semaphore_signal(barrier, inc=1, device_id=device, device_id_type=MESH)
        pl.semaphore_wait(barrier, len(devices))

    def batch_peers(self):
        return [(lax.rem(self.j + d, self.batches), self.x * 2 + self.c) for d in range(1, self.batches)]


class Sends:
    def __init__(self, sems):
        self.sems, self.count, self.made = sems, 0, []

    def push(self, src, dst, recv, device, like, cond=None):
        copy = pltpu.make_async_remote_copy(
            src_ref=src, dst_ref=dst, send_sem=self.sems.at[self.count], recv_sem=recv,
            device_id=device, device_id_type=MESH,
        )
        if cond is None:
            copy.start()
        else:
            pl.when(cond())(lambda: copy.start())
        self.made.append((self.count, like, cond))
        self.count += 1

    def drain(self, place):
        for k, like, cond in self.made:
            sent = pltpu.make_async_remote_copy(
                src_ref=like(), dst_ref=like(), send_sem=self.sems.at[k], recv_sem=self.sems.at[k],
                device_id=place.dev(), device_id_type=MESH,
            )
            if cond is None:
                sent.wait_send()
            else:
                pl.when(cond())(lambda sent=sent: sent.wait_send())


def arrived(place, ref, recv, send):
    pltpu.make_async_remote_copy(
        src_ref=ref, dst_ref=ref, send_sem=send, recv_sem=recv, device_id=place.dev(), device_id_type=MESH
    ).wait_recv()


def forward_sends(X, Y, Z):
    part_a = (Z * Y - 1) + (X - 1) + 1 + (Z * Y - 1) * (X - 1 + 1) + (X - 1) * Z * Y
    part_b = (X - 1) + (Y - 1) + (Z - 1) + 1 + (Z - 1) * (X + Y - 1) + Z * (
        2 * (X - 1) * (Y - 1) + (X - 1) + (Y - 1) + (X - 1) * (Y - 1)
    )
    return part_a + part_b


def forward_kernel(
    batches, heads, owner_ref, length_ref, post_ref, weight_ref,
    qk_ref, vx_ref, p_ref, linv_ref, at_ref, xst_ref, ga_out, gb_ref,
    xs_ref, own_ref, ga_ref, recv_a, recv_b, send_sems, own_sem, out_sem,
):
    place = Place(batches, heads)
    groups, rows = NHEADS // heads, D // batches
    X, Y, Z = place.X, place.Y, place.Z
    step = pl.program_id(0)
    sends = Sends(send_sems)
    c, x, j = place.c, place.x, place.j
    dummy = send_sems.at[0]

    def got_a(cc, xx, jj):
        arrived(place, ga_ref.at[cc, xx, jj], recv_a.at[cc, xx, jj], dummy)

    def push_a(cc, xx, jj, device):
        ref = ga_ref.at[cc, xx, jj]
        sends.push(ref, ref, recv_a.at[cc, xx, jj], device, lambda: ga_ref.at[0, 0, 0])

    def got_b(block):
        cc, xx, jj = block
        arrived(place, gb_ref.at[cc, xx, jj], recv_b.at[cc, xx, jj], dummy)

    def push_b(block, device, cond=None, src=None):
        cc, xx, jj = block
        ref = gb_ref.at[cc, xx, jj]
        sends.push(ref if src is None else src, ref, recv_b.at[cc, xx, jj], device, lambda: gb_ref.at[0, 0, 0], cond)

    def at(z=None, y=None, x=None, c=None):
        jj, hh = place.dev(z, y, x, c)
        return (hh % 2, hh // 2, jj)

    def side(offset):
        zo = lax.rem(place.z + offset, Z)
        low = lambda: lax.rem(place.z + offset, Z) < (3 * Z) // 4
        for xx in place.xs:
            got_b(at(z=zo, x=xx))
            for yy in place.ys:
                push_b(at(z=zo, x=xx), place.dev(y=yy), low)
            push_b(at(z=zo, x=xx), place.dev(c=1 - c))
        for yy in place.ys:
            got_b(at(z=zo, y=yy))
            for xx in place.xs:
                push_b(at(z=zo, y=yy), place.dev(x=xx), lambda: jnp.logical_not(low()))
            push_b(at(z=zo, y=yy), place.dev(c=1 - c))

    def own_copy():
        return pltpu.make_async_copy(own_ref, gb_ref.at[c, x, j], own_sem)

    @pl.when(step == 0)
    def _():
        weight = weight_ref[...]
        for g in range(groups):
            ga_ref[c, x, j, g] = weight[:, g * GROUPW : g * GROUPW + PART].astype(BF)
        peers = place.batch_peers()
        place.greet(peers + [place.dev(x=xx) for xx in place.xs] + [place.dev(c=1 - c)])
        for peer in peers:
            push_a(c, x, j, peer)
        for xx in place.xs:
            push_a(c, x, j, place.dev(x=xx))
        push_a(c, x, j, place.dev(c=1 - c))
        for g in range(groups):
            for k in range(2):
                low = g * GROUPW + (k + 1) * PART
                own_ref[g, k] = weight[:, low : low + PART].astype(BF)
        own_copy().start()
        lane = lax.broadcasted_iota(jnp.int32, (1, D), 1)
        source = lane % rows
        for b in range(batches):
            source = jnp.where(lane // rows == b, source + owner_ref[b] * rows, source)
        pick = (lax.broadcasted_iota(jnp.int32, (D, D), 0) == source).astype(F32).astype(BF)
        ordered = dot(post_ref[...], pick, 1, 0).astype(BF)
        xs_ref[...] = ordered
        xst_ref[...] = ordered.T
        for jj, _ in peers:
            got_a(c, x, jj)
            for xx in place.xs:
                push_a(c, x, jj, place.dev(x=xx))
            push_a(c, x, jj, place.dev(c=1 - c))
        for xx in place.xs:
            push_b((c, x, j), place.dev(x=xx), src=own_ref)
        for yy in place.ys:
            push_b((c, x, j), place.dev(y=yy), src=own_ref)
        for zz in place.zs:
            push_b((c, x, j), place.dev(z=zz), src=own_ref)
        push_b((c, x, j), place.dev(c=1 - c), src=own_ref)

    for q in range(1, heads):

        @pl.when(step == q * groups)
        def _(q=q):
            xx = lax.rem(x + q // 2, X)
            for jj in range(batches):
                got_a((c + q) % 2, xx, jj)
            if q % 2 == 0:
                for jj in range(batches):
                    push_a(c, xx, jj, place.dev(c=1 - c))

    @pl.when(step == 3)
    def _():
        own_copy().wait()
        for zz in place.zs:
            got_b(at(z=zz))
            for xx in place.xs:
                push_b(at(z=zz), place.dev(x=xx))
            for yy in place.ys:
                push_b(at(z=zz), place.dev(y=yy))
            push_b(at(z=zz), place.dev(c=1 - c))
        side(0)

    @pl.when(step == 6)
    def _():
        for offset in range(1, Z):
            side(offset)

    @pl.when(step == NHEADS - 1)
    def _():
        pltpu.make_async_copy(ga_ref, ga_out, out_sem).start()

    q, g = step // groups, step % groups
    cc, xx = (c + q) % 2, lax.rem(x + q // 2, X)
    head = (xx * 2 + cc) * groups + g
    w = ga_ref[cc, xx, :, g].reshape(D, PART)
    proj = dot(xs_ref[...], w, 1, 0)
    lane = lax.broadcasted_iota(jnp.int32, (SEQ_LEN, 128), 1)
    qk = proj[:, :128].astype(BF)
    qk = jnp.where(lane < DH, qk * BF(DH**-0.5), qk)
    v = proj[:, 128:].astype(BF)
    vx = jnp.where(lane < DH, v, jnp.where(lane < DH + 2, BF(1), BF(0)))
    qk_ref[0] = qk
    vx_ref[0] = vx
    q_only = jnp.where(lane < DH, qk, BF(0))
    kq = jnp.concatenate([qk[:, DH:], qk[:, :DH]], axis=1)
    vxt = vx.T[: DH + 8]
    keep = lax.broadcasted_iota(jnp.int32, (SEQ_LEN, 1), 0) < length_ref[0]
    s = dot(kq, q_only, 1, 1)
    s = jnp.where(keep, s, F32(MASK_VALUE))
    m = jnp.max(s, axis=0, keepdims=True)
    p = jnp.exp(s - m).astype(BF)
    p_ref[0] = p
    o = dot(vxt, p, 1, 0)
    r = 1.0 / o[DH : DH + 1]
    linv_ref[head] = r
    at_ref[head] = (o[:DH] * r).astype(BF)

    @pl.when(step == NHEADS - 1)
    def _():
        pltpu.make_async_copy(ga_ref, ga_out, out_sem).wait()
        for zz in [place.z] + place.zs:
            for yy in place.ys:
                for xx in place.xs:
                    got_b(at(z=zz, y=yy, x=xx))
                    push_b(at(z=zz, y=yy, x=xx), place.dev(c=1 - c))
        for jj in range(batches):
            for xx in [x] + place.xs:
                got_b((1 - c, xx, jj))
        sends.drain(place)


def forward_call(owner, length, post, weights, batches, heads):
    groups, rows = NHEADS // heads, D // batches
    X, Y = heads // 2, heads // 2
    Z = batches // Y
    tokens = post.shape[0]
    whole = lambda shape: pl.BlockSpec(shape, lambda i: (0,) * len(shape), pipeline_mode=pl.Buffered(1))
    per_head = lambda *shape: pl.BlockSpec((1,) + shape, lambda i: (i, 0, 0))
    shapes = [
        ((NHEADS, tokens, 128), BF),
        ((NHEADS, tokens, 128), BF),
        ((NHEADS, tokens, tokens), BF),
        ((NHEADS, 1, tokens), F32),
        ((NHEADS, DH, tokens), BF),
        ((D, tokens), BF),
        ((2, X, batches, groups, rows, PART), BF),
        ((2, X, batches, groups, 2, rows, PART), BF),
    ]
    return pl.pallas_call(
        functools.partial(forward_kernel, batches, heads),
        grid=(NHEADS,),
        in_specs=[
            pl.BlockSpec(memory_space=pltpu.SMEM),
            pl.BlockSpec(memory_space=pltpu.SMEM),
            whole(post.shape),
            whole(weights.shape),
        ],
        out_specs=[
            per_head(tokens, 128),
            per_head(tokens, 128),
            per_head(tokens, tokens),
            whole(shapes[3][0]),
            whole(shapes[4][0]),
            whole(shapes[5][0]),
            pl.BlockSpec(memory_space=pl.ANY),
            pl.BlockSpec(memory_space=pl.ANY),
        ],
        out_shape=[jax.ShapeDtypeStruct(*s) for s in shapes],
        scratch_shapes=[
            pltpu.VMEM((tokens, D), BF),
            pltpu.VMEM((groups, 2, rows, PART), BF),
            pltpu.VMEM(shapes[6][0], BF),
            pltpu.SemaphoreType.DMA((2, X, batches)),
            pltpu.SemaphoreType.DMA((2, X, batches)),
            pltpu.SemaphoreType.DMA((forward_sends(X, Y, Z),)),
            pltpu.SemaphoreType.DMA,
            pltpu.SemaphoreType.DMA,
        ],
        name="attend_forward",
        compiler_params=pltpu.CompilerParams(
            collective_id=1, has_side_effects=True, vmem_limit_bytes=VMEM_BYTES
        ),
    )(owner, length, post, weights)


def norm_forward(u, gain, bias):
    centred = u - jnp.mean(u, axis=-1, keepdims=True)
    recip = lax.rsqrt(jnp.mean(centred * centred, axis=-1, keepdims=True) + NORM_EPSILON)
    normed = centred * recip
    return normed * gain + bias, normed, recip


def norm_back(grad, normed, recip, gain):
    e = grad * gain
    slope = jnp.mean(e * normed, axis=-1, keepdims=True)
    return recip * (e - jnp.mean(e, axis=-1, keepdims=True) - normed * slope)


def middle_kernel(
    batches, heads, block, owner_ref, length_ref, at_ref, post_ref, dual_ref, pc_ref, dc_ref, gain_ref, bias_ref,
    ga_ref, gb_ref, post_out, dual_out, dmid_ref, dat_ref, wq_ref, dff_ref, dwo_ref, norm_ref,
    wo, w1, w2, a1, a2, ao,
):
    groups, rows = NHEADS // heads, D // batches
    step = pl.program_id(0)

    def seat(h):
        return h % groups, (h // groups) // 2, (h // groups) % 2

    @pl.when(step == 0)
    def _():
        for j in range(batches):
            there = pl.ds(pl.multiple_of(owner_ref[j] * rows, rows), rows)
            for h in range(NHEADS):
                g, x, c = seat(h)
                held = ga_ref[c, x, j, g]
                wq_ref[there, h * PART : (h + 1) * PART] = held
                wo[there, h * DH : (h + 1) * DH] = held[:, 3 * DH :]
                w1[there, h * PART : (h + 1) * PART] = gb_ref[c, x, j, g, 0]
                w2[there, h * PART : (h + 1) * PART] = gb_ref[c, x, j, g, 1]
        a1[...] = jnp.zeros_like(a1)
        a2[...] = jnp.zeros_like(a2)
        ao[...] = jnp.zeros_like(ao)
        norm_ref[...] = jnp.zeros_like(norm_ref)

    at = at_ref[...].reshape(D, block)
    gain, bias = gain_ref[...], bias_ref[...]
    branch = dot(at, wo[...], 0, 1)
    middle, n1, r1 = norm_forward(post_ref[...].astype(F32) + branch, gain[0:1], bias[0:1])
    middle_low = middle.astype(BF)
    pre = dot(middle_low, w1[...], 1, 0)
    cdf = 0.5 + 0.5 * lax.erf(pre * F32(math.sqrt(0.5)))
    density = jnp.exp(pre * pre * F32(-0.5)) * F32(1.0 / math.sqrt(2.0 * math.pi))
    hidden = (pre * cdf).astype(BF)
    slope = cdf + pre * density
    feed = dot(hidden, w2[...], 1, 1)
    out, n2, r2 = norm_forward(middle + feed, gain[1:2], bias[1:2])
    post_out[...] = out.astype(BF)
    dual_out[...] = dual_ref[...] + branch + feed
    keep = step * block + lax.broadcasted_iota(jnp.int32, (block, 1), 0) < length_ref[0]
    d_out = jnp.where(keep, pc_ref[...].astype(F32), 0.0)
    d_dual = jnp.where(keep, dc_ref[...].astype(F32), 0.0)
    d_pre = norm_back(d_out, n2, r2, gain[1:2])
    d_feed = (d_pre + d_dual).astype(BF)
    a2[...] += dot(d_feed, hidden, 0, 0)
    d_hidden = dot(d_feed, w2[...], 1, 0)
    d_hidden_pre = (d_hidden * slope).astype(BF)
    a1[...] += dot(middle_low, d_hidden_pre, 0, 0)
    d_middle = d_pre + dot(d_hidden_pre, w1[...], 1, 1)
    d_mid = norm_back(d_middle, n1, r1, gain[0:1])
    dmid_ref[...] = d_mid
    d_branch = (d_mid + d_dual).astype(BF)
    ao[...] += dot(d_branch, at, 0, 1)
    dat_ref[...] = dot(wo[...], d_branch, 0, 1).astype(BF).reshape(NHEADS, DH, block)
    sums = [jnp.sum(v, axis=0, keepdims=True) for v in (d_middle * n1, d_out * n2, d_middle, d_out)]
    norm_ref[...] += jnp.concatenate(sums, axis=0)

    @pl.when(step == pl.num_programs(0) - 1)
    def _():
        empty = jnp.zeros((rows, DH), BF)
        for j in range(batches):
            there = pl.ds(pl.multiple_of(owner_ref[j] * rows, rows), rows)
            for h in range(NHEADS):
                g, x, c = seat(h)
                dff_ref[g * 2, c, x, j] = a1[there, h * PART : (h + 1) * PART].astype(BF)
                dff_ref[g * 2 + 1, c, x, j] = a2[there, h * PART : (h + 1) * PART].astype(BF)
                dwo = ao[there, h * DH : (h + 1) * DH].astype(BF)
                dwo_ref[h, j * rows : (j + 1) * rows] = jnp.concatenate([empty, dwo], axis=1)


def middle_call(owner, length, at, post, dual, pc, dc, gain, bias, ga, gb, batches, heads):
    groups, rows, X = NHEADS // heads, D // batches, heads // 2
    tokens, block = post.shape[0], 256
    whole = lambda shape: pl.BlockSpec(shape, lambda i, *_: (0,) * len(shape), pipeline_mode=pl.Buffered(1))
    token = pl.BlockSpec((block, D), lambda i, *_: (i, 0))
    across = pl.BlockSpec((NHEADS, DH, block), lambda i, *_: (0, 0, i))
    shapes = [
        ((tokens, D), BF),
        ((tokens, D), F32),
        ((tokens, D), F32),
        ((NHEADS, DH, tokens), BF),
        ((D, NHEADS * PART), BF),
        ((2 * groups, 2, X, batches, rows, PART), BF),
        ((NHEADS, D, 128), BF),
        ((4, D), F32),
    ]
    return pl.pallas_call(
        functools.partial(middle_kernel, batches, heads, block),
        grid_spec=pltpu.PrefetchScalarGridSpec(
            num_scalar_prefetch=2,
            grid=(tokens // block,),
            in_specs=[across, token, token, token, token]
            + [whole(a.shape) for a in (gain, bias, ga, gb)],
            out_specs=[token, token, token, across] + [whole(s[0]) for s in shapes[4:]],
            scratch_shapes=[
                pltpu.VMEM((D, D), BF),
                pltpu.VMEM((D, FF), BF),
                pltpu.VMEM((D, FF), BF),
                pltpu.VMEM((D, FF), F32),
                pltpu.VMEM((D, FF), F32),
                pltpu.VMEM((D, D), F32),
            ],
        ),
        out_shape=[jax.ShapeDtypeStruct(*s) for s in shapes],
        name="middle",
        compiler_params=pltpu.CompilerParams(vmem_limit_bytes=VMEM_BYTES),
    )(owner, length, at, post, dual, pc, dc, gain, bias, ga, gb)


def adam_update(param, grad, first, second, rate, decay):
    first_new = BETA_FIRST * first + (1.0 - BETA_FIRST) * grad
    second_new = BETA_SECOND * second + (1.0 - BETA_SECOND) * grad * grad
    first_hat = first_new * (1.0 / (1.0 - BETA_FIRST**STEP))
    second_hat = second_new * (1.0 / (1.0 - BETA_SECOND**STEP))
    param_new = param - rate * (first_hat / (jnp.sqrt(second_hat) + ADAM_EPSILON) + decay * param)
    return first_new, second_new, param_new


def bits(n):
    return [1 << k for k in range(n.bit_length() - 1)]


class Reduce:
    def __init__(self, place, piece, source, x_first, bufs, recv, sends):
        self.place, self.piece, self.source, self.x_first = place, piece, source, x_first
        self.r1, self.r2, self.r3, self.r4, self.s1, self.s2, self.s3, self.final = (
            b[0 if x_first else 1] if isinstance(b, tuple) else b for b in bufs
        )
        self.recv, self.sends = recv.at[piece], sends

    def got(self, ref, k):
        arrived(self.place, ref, self.recv.at[k], self.sends.sems.at[0])

    def across(self, axis):
        p = self.place
        return (p.X, p.x, lambda v: p.dev(x=v)) if axis == "x" else (p.Y, p.y, lambda v: p.dev(y=v))

    def hop0(self):
        p, k = self.place, self.piece
        self.sends.push(self.source.at[1 - p.c], self.r1.at[k], self.recv.at[0], p.dev(c=1 - p.c), lambda: self.r1.at[k])

    def hop1(self):
        p, k = self.place, self.piece
        self.got(self.r1.at[k], 0)
        self.s1[k] = (self.source[p.c].astype(F32) + self.r1[k].astype(F32)).astype(BF)
        size, me, dev = self.across("x" if self.x_first else "y")
        for d in range(1, size):
            to = lax.rem(me + d, size)
            src = self.s1.at[k, to] if self.x_first else self.s1.at[k, :, :, to]
            self.sends.push(src, self.r2.at[k, d - 1], self.recv.at[d], dev(to), lambda: self.r2.at[k, 0])

    def hop2(self):
        p, k = self.place, self.piece
        size, me, _ = self.across("x" if self.x_first else "y")
        own = self.s1[k, me] if self.x_first else self.s1[k, :, :, me]
        total = own.astype(F32)
        for d in range(1, size):
            self.got(self.r2.at[k, d - 1], d)
            total = total + self.r2[k, d - 1].astype(F32)
        self.s2[k] = total.astype(BF)
        size, me, dev = self.across("y" if self.x_first else "x")
        for d in range(1, size):
            to = lax.rem(me + d, size)
            src = self.s2.at[k, :, to] if self.x_first else self.s2.at[k, to]
            self.sends.push(src, self.r3.at[k, d - 1], self.recv.at[p.X + d], dev(to), lambda: self.r3.at[k, 0])

    def hop3(self):
        p, k = self.place, self.piece
        size, me, _ = self.across("y" if self.x_first else "x")
        own = self.s2[k, :, me] if self.x_first else self.s2[k, me]
        total = own.astype(F32)
        for d in range(1, size):
            self.got(self.r3.at[k, d - 1], p.X + d)
            total = total + self.r3[k, d - 1].astype(F32)
        self.s3[k] = total.astype(BF)
        for d in range(1, p.Z):
            to = lax.rem(p.z + d, p.Z)
            self.sends.push(self.s3.at[k, to], self.r4.at[k, d - 1], self.recv.at[2 * p.X + d], p.dev(z=to), lambda: self.r4.at[k, 0])

    def hop4(self):
        p, k = self.place, self.piece
        total = self.s3[k, p.z].astype(F32)
        for d in range(1, p.Z):
            self.got(self.r4.at[k, d - 1], 2 * p.X + d)
            total = total + self.r4[k, d - 1].astype(F32)
        self.final[k] = total


def backward_kernel(
    batches, heads, qk_ref, vx_ref, p_ref, linv_ref, at_ref, dat_ref, xst_ref, wq_ref, dmid_ref, dff_ref, dwo_ref,
    norm_ref, weight_ref, first_ref, second_ref, nparam_ref, nfirst_ref, nsecond_ref,
    grad_ref, first_out, second_out, weight_out, nfirst_out, nsecond_out, nparam_out,
    dp_ref, dqkv_ref, r1, r2x, r2y, r3, r4, s1, s2x, s2y, s3, final, norm_send, norm_recv, recv_sems, norm_sems, send_sems,
):
    place = Place(batches, heads)
    groups = NHEADS // heads
    X, Y, Z = place.X, place.Y, place.Z
    c, x = place.c, place.x
    step = pl.program_id(0)
    sends = Sends(send_sems)
    bufs = (r1, (r2x, r2y), r3, r4, s1, (s2x, s2y), s3, final)
    pieces = [Reduce(place, k, dff_ref.at[k], k % 2 == 0, bufs, recv_sems, sends) for k in range(2 * groups)]
    pieces += [
        Reduce(place, 2 * groups + g, dqkv_ref.at[g], g % 2 == 0, bufs, recv_sems, sends) for g in range(groups)
    ]
    partners = [place.dev(c=1 - c)]
    flip = lambda v, b: v + b - 2 * b * ((v // b) % 2)
    partners += [place.dev(x=flip(x, b)) for b in bits(X)]
    partners += [place.dev(y=flip(place.y, b)) for b in bits(Y)]
    partners += [place.dev(z=flip(place.z, b)) for b in bits(Z)]

    def norm_push(k):
        sends.push(norm_send.at[k], norm_recv.at[k], norm_sems.at[k], partners[k], lambda: norm_send.at[0])

    def norm_pull(k):
        arrived(place, norm_recv.at[k], norm_sems.at[k], send_sems.at[0])
        norm_send[k + 1] = norm_send[k] + norm_recv[k]

    @pl.when(step == 0)
    def _():
        norm_send[0] = norm_ref[...]
        place.greet(
            [place.dev(c=1 - c)]
            + [place.dev(x=v) for v in place.xs]
            + [place.dev(y=v) for v in place.ys]
            + [place.dev(z=v) for v in place.zs]
        )
        for k in range(2 * groups):
            pieces[k].hop0()
        norm_push(0)

    q, g = step % heads, step // heads
    cc, xx = (c + q) % 2, lax.rem(x + q // 2, X)
    head = (xx * 2 + cc) * groups + g
    lane = lax.broadcasted_iota(jnp.int32, (SEQ_LEN, 128), 1)
    row = lax.broadcasted_iota(jnp.int32, (DH, SEQ_LEN), 0)
    qk, vx = qk_ref[0], vx_ref[0]
    do = dat_ref[head].astype(F32) * linv_ref[head]
    inner = -jnp.sum(do * at_ref[head].astype(F32), axis=0, keepdims=True)
    coarse = inner.astype(BF).astype(F32)
    tail = jnp.where(row == 0, coarse, jnp.where(row == 1, inner - coarse, 0.0))
    et = jnp.concatenate([do, tail], axis=0).astype(BF)
    e = et.T
    kt = qk.T[DH:]
    kq = jnp.concatenate([qk[:, DH:], qk[:, :DH]], axis=1)
    dk = jnp.zeros((SEQ_LEN, 128), F32)
    dv = jnp.zeros((SEQ_LEN, 128), F32)
    dqs = []
    for b in range(2):
        sl = slice(b * (SEQ_LEN // 2), (b + 1) * (SEQ_LEN // 2))
        p = p_ref[0, :, sl]
        ds = (p.astype(F32) * dot(vx, et[:, sl], 1, 0)).astype(BF)
        dv = dv + dot(p, e[sl], 1, 0)
        dk = dk + dot(ds, kq[sl], 1, 0)
        dqs.append(dot(kt, ds, 1, 0))
    dqt = jnp.concatenate(dqs, axis=1) * F32(DH**-0.5)
    dq = jnp.concatenate([dqt, jnp.zeros_like(dqt)], axis=0).T
    d_proj = jnp.concatenate([jnp.where(lane < DH, dq, dk), jnp.where(lane < DH, dv, 0.0)], axis=1).astype(BF)
    dp_ref[head] = d_proj
    dw = dot(xst_ref[...], d_proj, 1, 0)
    dw = jnp.concatenate([dw[:, :128], dw[:, 128:] + dwo_ref[head].astype(F32)], axis=1).astype(BF)
    dqkv_ref[g, cc, xx] = dw.reshape(dqkv_ref.shape[3:])

    def at_step(k):
        return pl.when(step == k)

    half = len(pieces[: 2 * groups]) // 2
    early, late = pieces[:half], pieces[half : 2 * groups]

    for t, todo in enumerate(
        [
            [p.hop1 for p in early] + [lambda: norm_pull(0), lambda: norm_push(1)],
            [p.hop2 for p in early] + [lambda: norm_pull(1), lambda: norm_push(2)],
            [p.hop1 for p in late] + [p.hop3 for p in early],
            ([pieces[2 * groups].hop0] if groups > 1 else [])
            + [p.hop4 for p in early]
            + [p.hop2 for p in late]
            + [lambda: norm_pull(2), lambda: norm_push(3)],
            [p.hop3 for p in late] + ([pieces[2 * groups].hop1] if groups > 1 else []),
            [p.hop4 for p in late] + [lambda: norm_pull(3), lambda: norm_push(4)],
            ([pieces[2 * groups].hop2] if groups > 1 else []),
        ]
    ):

        @at_step(t)
        def _(todo=todo):
            for act in todo:
                act()

    @at_step(NHEADS - 1)
    def _():
        last = pieces[2 * groups + groups - 1]
        last.hop0()
        if groups > 1:
            pieces[2 * groups].hop3()
        for k in range(4, len(partners)):
            norm_pull(k)
            if k + 1 < len(partners):
                norm_push(k + 1)
        last.hop1()
        if groups > 1:
            pieces[2 * groups].hop4()
        total = dmid_ref[...]
        for h in range(NHEADS):
            total = total + dot(dp_ref[h], wq_ref[:, h * PART : (h + 1) * PART], 1, 1)
        grad_ref[...] = total
        last.hop2()
        last.hop3()
        norm_new = adam_update(
            nparam_ref[...], norm_send[len(partners)], nfirst_ref[...], nsecond_ref[...], NORM_RATE, 0.0
        )
        nfirst_out[...], nsecond_out[...], nparam_out[...] = norm_new

        def update(lo, grad):
            cols = slice(lo, lo + PART)
            new = adam_update(
                weight_ref[:, cols], grad, first_ref[:, cols], second_ref[:, cols], WEIGHT_RATE, WEIGHT_DECAY
            )
            first_out[:, cols], second_out[:, cols], weight_out[:, cols] = new

        for k in range(groups):
            update(k * GROUPW + PART, final[2 * k])
            update(k * GROUPW + 2 * PART, final[2 * k + 1])
            if k < groups - 1:
                update(k * GROUPW, final[2 * groups + k])
        last.hop4()
        update((groups - 1) * GROUPW, final[3 * groups - 1])
        sends.drain(place)


def backward_call(
    qk, vx, probs, linv, at, dat, xst, wq, dmid, dff, dwo, norm_grads, weights, first, second, nparam, nfirst, nsecond,
    batches, heads,
):
    groups, rows = NHEADS // heads, D // batches
    X = Y = heads // 2
    Z = batches // Y
    tokens = dmid.shape[0]
    whole = lambda shape: pl.BlockSpec(shape, lambda i: (0,) * len(shape), pipeline_mode=pl.Buffered(1))
    spot = lambda i: ((i % heads) * groups + i // heads, 0, 0)
    per_head = lambda *shape: pl.BlockSpec((1,) + shape, spot)
    dff = dff.reshape(2 * groups, 2, X, Z, Y, rows, PART)
    inputs = (linv, at, dat, xst, wq, dmid, dff, dwo, norm_grads, weights, first, second, nparam, nfirst, nsecond)
    shapes = [((tokens, D), F32)] + [(weights.shape, F32)] * 3 + [((4, D), F32)] * 3
    n = 3 * groups
    stages = 1 + sum(len(bits(v)) for v in (X, Y, Z))
    return pl.pallas_call(
        functools.partial(backward_kernel, batches, heads),
        grid=(NHEADS,),
        in_specs=[per_head(tokens, 128), per_head(tokens, 128), per_head(tokens, tokens)]
        + [whole(a.shape) for a in inputs],
        out_specs=[whole(s[0]) for s in shapes],
        out_shape=[jax.ShapeDtypeStruct(*s) for s in shapes],
        scratch_shapes=[
            pltpu.VMEM((NHEADS, tokens, PART), BF),
            pltpu.VMEM((groups, 2, X, Z, Y, rows, PART), BF),
            pltpu.VMEM((n, X, Z, Y, rows, PART), BF),
            pltpu.VMEM((n, X - 1, Z, Y, rows, PART), BF),
            pltpu.VMEM((n, Y - 1, X, Z, rows, PART), BF),
            pltpu.VMEM((n, X - 1, Z, rows, PART), BF),
            pltpu.VMEM((n, Z - 1, rows, PART), BF),
            pltpu.VMEM((n, X, Z, Y, rows, PART), BF),
            pltpu.VMEM((n, Z, Y, rows, PART), BF),
            pltpu.VMEM((n, X, Z, rows, PART), BF),
            pltpu.VMEM((n, Z, rows, PART), BF),
            pltpu.VMEM((n, rows, PART), F32),
            pltpu.VMEM((stages + 1, 4, D), F32),
            pltpu.VMEM((stages, 4, D), F32),
            pltpu.SemaphoreType.DMA((n, 2 * X + Z)),
            pltpu.SemaphoreType.DMA((stages,)),
            pltpu.SemaphoreType.DMA((n * (1 + 2 * (X - 1) + Z - 1) + stages,)),
        ],
        name="attend_backward",
        compiler_params=pltpu.CompilerParams(
            collective_id=2, has_side_effects=True, vmem_limit_bytes=VMEM_BYTES
        ),
    )(qk, vx, probs, *inputs)


def shards(
    post_stream,
    dual_stream,
    post_cotangent,
    dual_cotangent,
    seq_lengths,
    owner_slots,
    weights,
    first_moment,
    second_moment,
    norm_gain,
    norm_bias,
    norm_first,
    norm_second,
):
    batches, heads = lax.axis_size("batch"), lax.axis_size("head")
    length = lax.dynamic_slice(seq_lengths, (lax.axis_index("head"),), (1,))
    qk, vx, probs, linv, at, xst, ga, gb = forward_call(owner_slots, length, post_stream, weights, batches, heads)
    post_out, dual_out, dmid, dat, wq, dff, dwo, norm_grads = middle_call(
        owner_slots, length, at, post_stream, dual_stream, post_cotangent, dual_cotangent, norm_gain, norm_bias,
        ga, gb, batches, heads,
    )
    norm_params = jnp.concatenate([norm_gain, norm_bias], axis=0)
    rest = backward_call(
        qk, vx, probs, linv, at, dat, xst, wq, dmid, dff, dwo, norm_grads,
        weights, first_moment, second_moment, norm_params, norm_first, norm_second, batches, heads,
    )
    return (post_out, dual_out, *rest)


def solution(mesh):
    tokens, table, copied = P(("batch", "head"), None), P("batch", "head"), P()
    in_specs = (tokens,) * 4 + (P("batch"), copied) + (table,) * 3 + (copied,) * 4
    out_specs = (tokens,) * 3 + (table,) * 3 + (copied,) * 3
    return jax.shard_map(shards, mesh=mesh, in_specs=in_specs, out_specs=out_specs, check_vma=False)
```

```python
import functools
import math

import jax
import jax.numpy as jnp
from jax import lax
from jax.experimental import pallas as pl
from jax.experimental.pallas import tpu as pltpu
from jax.sharding import PartitionSpec as P

D = 512
FF = 2048
NHEADS = 8
DH = 64
SEQ_LEN = 1024
STEP = 10
GROUPW = 768
PART = 256

BETA_FIRST = 0.9
BETA_SECOND = 0.999
ADAM_EPSILON = 1e-08
WEIGHT_DECAY = 0.1
WEIGHT_RATE = 0.2
NORM_RATE = 0.2
NORM_EPSILON = 1e-05
MASK_VALUE = -1000000000.0

MESH = pl.DeviceIdType.MESH
F32 = jnp.float32
BF = jnp.bfloat16
VMEM_BYTES = 60 << 20
B_STEPS = (3, 6)


def dot(a, b, ca, cb):
    return lax.dot_general(a, b, (((ca,), (cb,)), ((), ())), preferred_element_type=F32)


class Place:
    def __init__(self, batches, heads):
        self.X = self.Y = heads // 2
        self.Z = batches // self.Y
        self.batches, self.heads = batches, heads
        batch, head = lax.axis_index("batch"), lax.axis_index("head")
        self.j = batch
        self.z, self.y = batch // self.Y, batch % self.Y
        self.x, self.c = head // 2, head % 2
        self.xs = [lax.rem(self.x + d, self.X) for d in range(1, self.X)]
        self.ys = [lax.rem(self.y + d, self.Y) for d in range(1, self.Y)]
        self.zs = [lax.rem(self.z + d, self.Z) for d in range(1, self.Z)]

    def dev(self, z=None, y=None, x=None, c=None):
        z = self.z if z is None else z
        y = self.y if y is None else y
        x = self.x if x is None else x
        c = self.c if c is None else c
        return (z * self.Y + y, x * 2 + c)

    def greet(self, devices):
        barrier = pltpu.get_barrier_semaphore()
        for device in devices:
            pl.semaphore_signal(barrier, inc=1, device_id=device, device_id_type=MESH)
        pl.semaphore_wait(barrier, len(devices))

    def plane(self):
        return [(x, y) for x in [self.x] + self.xs for y in [self.y] + self.ys][1:]


class Sends:
    def __init__(self, sems):
        self.sems, self.count, self.made = sems, 0, []

    def push(self, src, dst, recv, device, like, cond=None):
        copy = pltpu.make_async_remote_copy(
            src_ref=src, dst_ref=dst, send_sem=self.sems.at[self.count], recv_sem=recv,
            device_id=device, device_id_type=MESH,
        )
        if cond is None:
            copy.start()
        else:
            pl.when(cond())(lambda: copy.start())
        self.made.append((self.count, like, cond))
        self.count += 1

    def drain(self, place):
        for k, like, cond in self.made:
            sent = pltpu.make_async_remote_copy(
                src_ref=like(), dst_ref=like(), send_sem=self.sems.at[k], recv_sem=self.sems.at[k],
                device_id=place.dev(), device_id_type=MESH,
            )
            if cond is None:
                sent.wait_send()
            else:
                pl.when(cond())(lambda sent=sent: sent.wait_send())


def arrived(place, ref, recv, send):
    pltpu.make_async_remote_copy(
        src_ref=ref, dst_ref=ref, send_sem=send, recv_sem=recv, device_id=place.dev(), device_id_type=MESH
    ).wait_recv()


def forward_sends(X, Y, Z, groups):
    part_a = groups * (Z - 1 + Y - 1) + (X - 1) * (1 + Z - 1 + Y - 1) + X
    part_b = (X - 1) + (Y - 1) + (Z - 1) + 1 + (Z - 1) * (X + Y - 1)
    part_b += Z * (2 * (X - 1) * (Y - 1) + (X - 1) + (Y - 1) + (X - 1) * (Y - 1))
    return part_a + part_b


def forward_kernel(
    batches, heads, owner_ref, length_ref, post_ref, weight_ref,
    qk_ref, vx_ref, p_ref, linv_ref, at_ref, xst_ref, ga_out, gb_ref,
    xs_ref, own_ref, ga_ref, recv_z, recv_y, recv_x, core_a, recv_b, send_sems, own_sem, out_sem,
):
    place = Place(batches, heads)
    groups, rows = NHEADS // heads, D // batches
    X, Y, Z = place.X, place.Y, place.Z
    step = pl.program_id(0)
    sends = Sends(send_sems)
    c, x, y, z = place.c, place.x, place.y, place.z
    dummy = send_sems.at[0]

    def core_push_a(xx):
        ref = ga_ref.at[c, xx]
        sends.push(ref, ref, core_a.at[xx], place.dev(c=1 - c), lambda: ga_ref.at[0, 0])

    def own_copy():
        return pltpu.make_async_copy(own_ref, gb_ref.at[c, x, z, y], own_sem)

    def got_b(cc, xx, zz, yy):
        arrived(place, gb_ref.at[cc, xx, zz, yy], recv_b.at[cc, xx, zz, yy], dummy)

    def push_b(xx, zz, yy, device, cond=None, src=None):
        ref = gb_ref.at[c, xx, zz, yy]
        sends.push(
            ref if src is None else src, ref, recv_b.at[c, xx, zz, yy], device, lambda: gb_ref.at[0, 0, 0, 0], cond
        )

    def side(offset):
        zo = lax.rem(z + offset, Z)
        low = lambda: lax.rem(place.z + offset, Z) < (3 * Z) // 4
        for xx in place.xs:
            got_b(c, xx, zo, y)
            for yy in place.ys:
                push_b(xx, zo, y, place.dev(y=yy), low)
            push_b(xx, zo, y, place.dev(c=1 - c))
        for yy in place.ys:
            got_b(c, x, zo, yy)
            for xx in place.xs:
                push_b(x, zo, yy, place.dev(x=xx), lambda: jnp.logical_not(low()))
            push_b(x, zo, yy, place.dev(c=1 - c))

    @pl.when(step == 0)
    def _():
        weight = weight_ref[...]
        for g in range(groups):
            ga_ref[c, x, z, y, g] = weight[:, g * GROUPW : g * GROUPW + PART].astype(BF)
        place.greet([place.dev(**{k: v}) for k in "xyz" for v in getattr(place, k + "s")] + [place.dev(c=1 - c)])
        for g in range(groups):
            own = ga_ref.at[c, x, z, y, g]
            for zz in place.zs:
                sends.push(own, own, recv_z.at[g, z], place.dev(z=zz), lambda: ga_ref.at[0, 0, 0, 0, 0])
        own = ga_ref.at[c, x, z, y]
        for xx in place.xs:
            sends.push(own, own, recv_x.at[x, z], place.dev(x=xx), lambda: ga_ref.at[0, 0, 0, 0])
        for g in range(groups):
            for k in range(2):
                low = g * GROUPW + (k + 1) * PART
                own_ref[k, g] = weight[:, low : low + PART].astype(BF)
        for yy in place.ys:
            push_b(x, z, y, place.dev(y=yy), src=own_ref)
        for xx in place.xs:
            push_b(x, z, y, place.dev(x=xx), src=own_ref)
        own_copy().start()
        lane = lax.broadcasted_iota(jnp.int32, (1, D), 1)
        source = lane % rows
        for b in range(batches):
            source = jnp.where(lane // rows == b, source + owner_ref[b] * rows, source)
        pick = (lax.broadcasted_iota(jnp.int32, (D, D), 0) == source).astype(F32).astype(BF)
        ordered = dot(post_ref[...], pick, 1, 0).astype(BF)
        xs_ref[...] = ordered
        xst_ref[...] = ordered.T
        for g in range(groups):
            for zz in place.zs:
                arrived(place, ga_ref.at[c, x, zz, y, g], recv_z.at[g, zz], dummy)
            column = ga_ref.at[c, x, :, y, g]
            for yy in place.ys:
                sends.push(column, column, recv_y.at[g, y], place.dev(y=yy), lambda: ga_ref.at[0, 0, :, 0, 0])
        for zz in place.zs:
            push_b(x, z, y, place.dev(z=zz), src=own_ref)
        for xx in place.xs:
            for zz in place.zs:
                block = ga_ref.at[c, x, zz, y]
                sends.push(block, block, recv_x.at[x, zz], place.dev(x=xx), lambda: ga_ref.at[0, 0, 0, 0])
        push_b(x, z, y, place.dev(c=1 - c), src=own_ref)

    for g in range(groups):

        @pl.when(step == g)
        def _(g=g):
            for yy in place.ys:
                arrived(place, ga_ref.at[c, x, :, yy, g], recv_y.at[g, yy], dummy)
            if g == groups - 1:
                for yy in place.ys:
                    column = ga_ref.at[c, x, :, yy]
                    for xx in place.xs:
                        sends.push(
                            column, column, recv_x.at[x, Z + yy], place.dev(x=xx), lambda: ga_ref.at[0, 0, :, 0]
                        )
                core_push_a(x)

    for k in range(1, heads):

        @pl.when(step == k * groups)
        def _(k=k):
            xx = lax.rem(x + k // 2, X)
            if k % 2 == 0:
                for zz in [z] + place.zs:
                    arrived(place, ga_ref.at[c, xx, zz, y], recv_x.at[xx, zz], dummy)
                for yy in place.ys:
                    arrived(place, ga_ref.at[c, xx, :, yy], recv_x.at[xx, Z + yy], dummy)
                core_push_a(xx)
            else:
                arrived(place, ga_ref.at[1 - c, xx], core_a.at[xx], dummy)

    @pl.when(step == B_STEPS[0])
    def _():
        for zz in place.zs:
            got_b(c, x, zz, y)
            for xx in place.xs:
                push_b(x, zz, y, place.dev(x=xx))
            for yy in place.ys:
                push_b(x, zz, y, place.dev(y=yy))
            push_b(x, zz, y, place.dev(c=1 - c))
        side(0)

    @pl.when(step == B_STEPS[1])
    def _():
        for offset in range(1, Z):
            side(offset)

    @pl.when(step == NHEADS - 1)
    def _():
        pltpu.make_async_copy(ga_ref, ga_out, out_sem).start()

    q, g = step // groups, step % groups
    cc, xx = (c + q) % 2, lax.rem(x + q // 2, X)
    head = (xx * 2 + cc) * groups + g
    w = ga_ref[cc, xx, :, :, g].reshape(D, PART)
    proj = dot(xs_ref[...], w, 1, 0)
    lane = lax.broadcasted_iota(jnp.int32, (SEQ_LEN, 128), 1)
    qk = proj[:, :128].astype(BF)
    qk = jnp.where(lane < DH, qk * BF(DH**-0.5), qk)
    v = proj[:, 128:].astype(BF)
    vx = jnp.where(lane < DH, v, jnp.where(lane < DH + 2, BF(1), BF(0)))
    qk_ref[0] = qk
    vx_ref[0] = vx
    q_only = jnp.where(lane < DH, qk, BF(0))
    kq = jnp.concatenate([qk[:, DH:], qk[:, :DH]], axis=1)
    vxt = vx.T[: DH + 8]
    keep = lax.broadcasted_iota(jnp.int32, (SEQ_LEN, 1), 0) < length_ref[0]
    s = dot(kq, q_only, 1, 1)
    s = jnp.where(keep, s, F32(MASK_VALUE))
    m = jnp.max(s, axis=0, keepdims=True)
    p = jnp.exp(s - m).astype(BF)
    p_ref[0] = p
    o = dot(vxt, p, 1, 0)
    r = 1.0 / o[DH : DH + 1]
    linv_ref[head] = r
    at_ref[head] = (o[:DH] * r).astype(BF)

    @pl.when(step == NHEADS - 1)
    def _():
        pltpu.make_async_copy(ga_ref, ga_out, out_sem).wait()
        own_copy().wait()
        for offset in range(Z):
            zz = lax.rem(z + offset, Z)
            for yy in place.ys:
                for xx in place.xs:
                    got_b(c, xx, zz, yy)
                    push_b(xx, zz, yy, place.dev(c=1 - c))
        for xx in range(X):
            for zz in range(Z):
                for yy in range(Y):
                    got_b(1 - c, xx, zz, yy)
        sends.drain(place)


def forward_call(owner, length, post, weights, batches, heads):
    groups, rows = NHEADS // heads, D // batches
    X, Y = heads // 2, heads // 2
    Z = batches // Y
    tokens = post.shape[0]
    whole = lambda shape: pl.BlockSpec(shape, lambda i: (0,) * len(shape), pipeline_mode=pl.Buffered(1))
    per_head = lambda *shape: pl.BlockSpec((1,) + shape, lambda i: (i, 0, 0))
    shapes = [
        ((NHEADS, tokens, 128), BF),
        ((NHEADS, tokens, 128), BF),
        ((NHEADS, tokens, tokens), BF),
        ((NHEADS, 1, tokens), F32),
        ((NHEADS, DH, tokens), BF),
        ((D, tokens), BF),
        ((2, X, Z, Y, groups, rows, PART), BF),
        ((2, X, Z, Y, 2, groups, rows, PART), BF),
    ]
    return pl.pallas_call(
        functools.partial(forward_kernel, batches, heads),
        grid=(NHEADS,),
        in_specs=[
            pl.BlockSpec(memory_space=pltpu.SMEM),
            pl.BlockSpec(memory_space=pltpu.SMEM),
            whole(post.shape),
            whole(weights.shape),
        ],
        out_specs=[
            per_head(tokens, 128),
            per_head(tokens, 128),
            per_head(tokens, tokens),
            whole(shapes[3][0]),
            whole(shapes[4][0]),
            whole(shapes[5][0]),
            pl.BlockSpec(memory_space=pl.ANY),
            pl.BlockSpec(memory_space=pl.ANY),
        ],
        out_shape=[jax.ShapeDtypeStruct(*s) for s in shapes],
        scratch_shapes=[
            pltpu.VMEM((tokens, D), BF),
            pltpu.VMEM((2, groups, rows, PART), BF),
            pltpu.VMEM(shapes[6][0], BF),
            pltpu.SemaphoreType.DMA((groups, Z)),
            pltpu.SemaphoreType.DMA((groups, Y)),
            pltpu.SemaphoreType.DMA((X, Z + Y)),
            pltpu.SemaphoreType.DMA((X,)),
            pltpu.SemaphoreType.DMA((2, X, Z, Y)),
            pltpu.SemaphoreType.DMA((forward_sends(X, Y, Z, groups),)),
            pltpu.SemaphoreType.DMA,
            pltpu.SemaphoreType.DMA,
        ],
        name="attend_forward",
        compiler_params=pltpu.CompilerParams(
            collective_id=1, has_side_effects=True, vmem_limit_bytes=VMEM_BYTES
        ),
    )(owner, length, post, weights)


def norm_forward(u, gain, bias):
    centred = u - jnp.mean(u, axis=-1, keepdims=True)
    recip = lax.rsqrt(jnp.mean(centred * centred, axis=-1, keepdims=True) + NORM_EPSILON)
    normed = centred * recip
    return normed * gain + bias, normed, recip


def norm_back(grad, normed, recip, gain):
    e = grad * gain
    slope = jnp.mean(e * normed, axis=-1, keepdims=True)
    return recip * (e - jnp.mean(e, axis=-1, keepdims=True) - normed * slope)


def middle_kernel(
    batches, heads, block, owner_ref, length_ref, at_ref, post_ref, dual_ref, pc_ref, dc_ref, gain_ref, bias_ref,
    ga_ref, gb_ref, post_out, dual_out, dmid_ref, dat_ref, wq_ref, dff_ref, dwo_ref, norm_ref,
    wo, w1, w2, a1, a2, ao,
):
    groups, rows, Y = NHEADS // heads, D // batches, heads // 2
    step = pl.program_id(0)

    def seat(h):
        return h % groups, (h // groups) // 2, (h // groups) % 2

    @pl.when(step == 0)
    def _():
        for j in range(batches):
            there = pl.ds(pl.multiple_of(owner_ref[j] * rows, rows), rows)
            for h in range(NHEADS):
                g, x, c = seat(h)
                held = ga_ref[c, x, j // Y, j % Y, g]
                wq_ref[there, h * PART : (h + 1) * PART] = held
                wo[there, h * DH : (h + 1) * DH] = held[:, 3 * DH :]
                w1[there, h * PART : (h + 1) * PART] = gb_ref[c, x, j // Y, j % Y, 0, g]
                w2[there, h * PART : (h + 1) * PART] = gb_ref[c, x, j // Y, j % Y, 1, g]
        a1[...] = jnp.zeros_like(a1)
        a2[...] = jnp.zeros_like(a2)
        ao[...] = jnp.zeros_like(ao)
        norm_ref[...] = jnp.zeros_like(norm_ref)

    at = at_ref[...].reshape(D, block)
    gain, bias = gain_ref[...], bias_ref[...]
    branch = dot(at, wo[...], 0, 1)
    middle, n1, r1 = norm_forward(post_ref[...].astype(F32) + branch, gain[0:1], bias[0:1])
    middle_low = middle.astype(BF)
    pre = dot(middle_low, w1[...], 1, 0)
    cdf = 0.5 + 0.5 * lax.erf(pre * F32(math.sqrt(0.5)))
    density = jnp.exp(pre * pre * F32(-0.5)) * F32(1.0 / math.sqrt(2.0 * math.pi))
    hidden = (pre * cdf).astype(BF)
    slope = cdf + pre * density
    feed = dot(hidden, w2[...], 1, 1)
    out, n2, r2 = norm_forward(middle + feed, gain[1:2], bias[1:2])
    post_out[...] = out.astype(BF)
    dual_out[...] = dual_ref[...] + branch + feed
    keep = step * block + lax.broadcasted_iota(jnp.int32, (block, 1), 0) < length_ref[0]
    d_out = jnp.where(keep, pc_ref[...].astype(F32), 0.0)
    d_dual = jnp.where(keep, dc_ref[...].astype(F32), 0.0)
    d_pre = norm_back(d_out, n2, r2, gain[1:2])
    d_feed = (d_pre + d_dual).astype(BF)
    a2[...] += dot(d_feed, hidden, 0, 0)
    d_hidden = dot(d_feed, w2[...], 1, 0)
    d_hidden_pre = (d_hidden * slope).astype(BF)
    a1[...] += dot(middle_low, d_hidden_pre, 0, 0)
    d_middle = d_pre + dot(d_hidden_pre, w1[...], 1, 1)
    d_mid = norm_back(d_middle, n1, r1, gain[0:1])
    dmid_ref[...] = d_mid
    d_branch = (d_mid + d_dual).astype(BF)
    ao[...] += dot(d_branch, at, 0, 1)
    dat_ref[...] = dot(wo[...], d_branch, 0, 1).astype(BF).reshape(NHEADS, DH, block)
    sums = [jnp.sum(v, axis=0, keepdims=True) for v in (d_middle * n1, d_out * n2, d_middle, d_out)]
    norm_ref[...] += jnp.concatenate(sums, axis=0)

    @pl.when(step == pl.num_programs(0) - 1)
    def _():
        empty = jnp.zeros((rows, DH), BF)
        for j in range(batches):
            there = pl.ds(pl.multiple_of(owner_ref[j] * rows, rows), rows)
            for h in range(NHEADS):
                g, x, c = seat(h)
                dff_ref[g * 2, c, x, j // Y, j % Y] = a1[there, h * PART : (h + 1) * PART].astype(BF)
                dff_ref[g * 2 + 1, c, x, j // Y, j % Y] = a2[there, h * PART : (h + 1) * PART].astype(BF)
                dwo = ao[there, h * DH : (h + 1) * DH].astype(BF)
                dwo_ref[h, j * rows : (j + 1) * rows] = jnp.concatenate([empty, dwo], axis=1)


def middle_call(owner, length, at, post, dual, pc, dc, gain, bias, ga, gb, batches, heads):
    groups, rows, X = NHEADS // heads, D // batches, heads // 2
    tokens, block = post.shape[0], 256
    whole = lambda shape: pl.BlockSpec(shape, lambda i, *_: (0,) * len(shape), pipeline_mode=pl.Buffered(1))
    token = pl.BlockSpec((block, D), lambda i, *_: (i, 0))
    across = pl.BlockSpec((NHEADS, DH, block), lambda i, *_: (0, 0, i))
    shapes = [
        ((tokens, D), BF),
        ((tokens, D), F32),
        ((tokens, D), F32),
        ((NHEADS, DH, tokens), BF),
        ((D, NHEADS * PART), BF),
        ((2 * groups, 2, X, batches // X, X, rows, PART), BF),
        ((NHEADS, D, 128), BF),
        ((4, D), F32),
    ]
    return pl.pallas_call(
        functools.partial(middle_kernel, batches, heads, block),
        grid_spec=pltpu.PrefetchScalarGridSpec(
            num_scalar_prefetch=2,
            grid=(tokens // block,),
            in_specs=[across, token, token, token, token]
            + [whole(a.shape) for a in (gain, bias, ga, gb)],
            out_specs=[token, token, token, across] + [whole(s[0]) for s in shapes[4:]],
            scratch_shapes=[
                pltpu.VMEM((D, D), BF),
                pltpu.VMEM((D, FF), BF),
                pltpu.VMEM((D, FF), BF),
                pltpu.VMEM((D, FF), F32),
                pltpu.VMEM((D, FF), F32),
                pltpu.VMEM((D, D), F32),
            ],
        ),
        out_shape=[jax.ShapeDtypeStruct(*s) for s in shapes],
        name="middle",
        compiler_params=pltpu.CompilerParams(vmem_limit_bytes=VMEM_BYTES),
    )(owner, length, at, post, dual, pc, dc, gain, bias, ga, gb)


def adam_update(param, grad, first, second, rate, decay):
    first_new = BETA_FIRST * first + (1.0 - BETA_FIRST) * grad
    second_new = BETA_SECOND * second + (1.0 - BETA_SECOND) * grad * grad
    first_hat = first_new * (1.0 / (1.0 - BETA_FIRST**STEP))
    second_hat = second_new * (1.0 / (1.0 - BETA_SECOND**STEP))
    param_new = param - rate * (first_hat / (jnp.sqrt(second_hat) + ADAM_EPSILON) + decay * param)
    return first_new, second_new, param_new


class Piece:
    def __init__(self, place, k, source, x_first, bufs, recv, sends):
        self.place, self.source, self.x_first, self.sends = place, source, x_first, sends
        bufs = [b[0 if x_first else 1] if isinstance(b, tuple) else b for b in bufs]
        self.r1, self.s1, self.r2, self.s2, self.r3, self.s3, self.r4, self.final = (b.at[k] for b in bufs)
        self.recv = recv.at[k]

    def axis(self, x):
        p = self.place
        return (p.X, p.x, lambda v: p.dev(x=v)) if x else (p.Y, p.y, lambda v: p.dev(y=v))

    def send(self, axis, cut, buf, base):
        size, me, dev = axis
        for d in range(1, size):
            to = lax.rem(me + d, size)
            self.sends.push(cut(to), buf.at[d - 1], self.recv.at[base + d], dev(to), lambda: buf.at[0])

    def add(self, axis, own, buf, base):
        total = own.astype(F32)
        for d in range(1, axis[0]):
            arrived(self.place, buf.at[d - 1], self.recv.at[base + d], self.sends.sems.at[0])
            total = total + buf[d - 1].astype(F32)
        return total

    def hop0(self):
        p = self.place
        self.sends.push(self.source.at[1 - p.c], self.r1, self.recv.at[0], p.dev(c=1 - p.c), lambda: self.r1)

    def hop1(self):
        p = self.place
        arrived(p, self.r1, self.recv.at[0], self.sends.sems.at[0])
        self.s1[...] = (self.source[p.c].astype(F32) + self.r1[...].astype(F32)).astype(BF)
        cut = lambda to: self.s1.at[to] if self.x_first else self.s1.at[:, :, to]
        self.send(self.axis(self.x_first), cut, self.r2, 0)

    def hop2(self):
        p = self.place
        own = self.s1[p.x] if self.x_first else self.s1[:, :, p.y]
        self.s2[...] = self.add(self.axis(self.x_first), own, self.r2, 0).astype(BF)
        cut = lambda to: self.s2.at[:, to] if self.x_first else self.s2.at[to]
        self.send(self.axis(not self.x_first), cut, self.r3, p.X)

    def hop3(self):
        p = self.place
        own = self.s2[:, p.y] if self.x_first else self.s2[p.x]
        self.s3[...] = self.add(self.axis(not self.x_first), own, self.r3, p.X).astype(BF)
        self.send((p.Z, p.z, lambda v: p.dev(z=v)), lambda to: self.s3.at[to], self.r4, 2 * p.X)

    def hop4(self):
        p = self.place
        self.final[...] = self.add((p.Z, p.z, None), self.s3[p.z], self.r4, 2 * p.X)


class Chunk:
    def __init__(self, place, g, dx, source, bufs, recv, sends):
        self.place, self.dx, self.sends = place, dx, sends
        r1, s1, rx, s2, r2 = bufs
        self.source, self.r1, self.s1, self.rx, self.s2, self.r2 = (
            source.at[g], r1.at[g, dx], s1.at[g, dx], rx.at[g], s2.at[g], r2.at[g]
        )
        self.recv = recv.at[g]

    def hop0(self):
        p = self.place
        x = lax.rem(p.x + self.dx, p.X)
        self.sends.push(self.source.at[1 - p.c, x], self.r1, self.recv.at[self.dx], p.dev(c=1 - p.c), lambda: self.r1)

    def hop1(self):
        p = self.place
        x = lax.rem(p.x + self.dx, p.X)
        arrived(p, self.r1, self.recv.at[self.dx], self.sends.sems.at[0])
        total = self.source[p.c, x].astype(F32) + self.r1[...].astype(F32)
        if self.dx:
            self.s1[...] = total.astype(BF)
            self.sends.push(
                self.s1, self.rx.at[self.dx - 1], self.recv.at[p.X + self.dx], p.dev(x=x), lambda: self.s1
            )
            return
        for d in range(1, p.X):
            arrived(p, self.rx.at[d - 1], self.recv.at[p.X + d], self.sends.sems.at[0])
            total = total + self.rx[d - 1].astype(F32)
        self.s2[...] = total.astype(BF)
        for d in range(1, p.batches):
            j = lax.rem(p.j + d, p.batches)
            self.sends.push(
                self.s2.at[j], self.r2.at[d - 1], self.recv.at[2 * p.X + d], (j, p.x * 2 + p.c), lambda: self.r2.at[0]
            )

    def collect(self):
        p = self.place
        total = self.s2[p.j].astype(F32)
        for d in range(1, p.batches):
            arrived(p, self.r2.at[d - 1], self.recv.at[2 * p.X + d], self.sends.sems.at[0])
            total = total + self.r2[d - 1].astype(F32)
        return total


def bits(n):
    return [1 << k for k in range(n.bit_length() - 1)]


def backward_kernel(
    batches, heads, qk_ref, vx_ref, p_ref, linv_ref, at_ref, dat_ref, xst_ref, wq_ref, dff_ref, dwo_ref, norm_ref,
    partial_ref, grad_ref, norm_out,
    dp_ref, dqkv_ref, r1, s1, xr2, yr2, xs2, ys2, r3, s3, r4, final, qr1, qs1, qrx, qs2, qr2,
    norm_send, norm_recv, recv_f, recv_q, norm_sems, send_sems,
):
    place = Place(batches, heads)
    groups = NHEADS // heads
    X, Y, Z = place.X, place.Y, place.Z
    c, x = place.c, place.x
    step = pl.program_id(0)
    sends = Sends(send_sems)
    bufs = (r1, s1, (xr2, yr2), (xs2, ys2), r3, s3, r4, final)
    pieces = [Piece(place, k, dff_ref.at[k], k == 0, bufs, recv_f, sends) for k in range(2 * groups)]
    chunks = [
        Chunk(place, g, dx, dqkv_ref, (qr1, qs1, qrx, qs2, qr2), recv_q, sends)
        for g in range(groups)
        for dx in reversed(range(X))
    ]
    partners = [place.dev(c=1 - c)]
    flip = lambda v, b: v + b - 2 * b * ((v // b) % 2)
    partners += [place.dev(x=flip(x, b)) for b in bits(X)]
    partners += [place.dev(y=flip(place.y, b)) for b in bits(Y)]
    partners += [place.dev(z=flip(place.z, b)) for b in bits(Z)]

    def norm_push(k):
        sends.push(norm_send.at[k], norm_recv.at[k], norm_sems.at[k], partners[k], lambda: norm_send.at[0])

    def norm_pull(k):
        arrived(place, norm_recv.at[k], norm_sems.at[k], send_sems.at[0])
        norm_send[k + 1] = norm_send[k] + norm_recv[k]

    @pl.when(step == 0)
    def _():
        norm_send[0] = norm_ref[...]
        others = [(dx, dj) for dx in range(X) for dj in range(batches) if dx or dj]
        place.greet(
            [(lax.rem(place.j + dj, batches), lax.rem(x + dx, X) * 2 + c) for dx, dj in others] + [place.dev(c=1 - c)]
        )
        for piece in pieces:
            piece.hop0()
        norm_push(0)

    g, r = step // heads, step % heads
    cc, xx = (c + r) % 2, lax.rem(x + X - 1 - r // 2, X)
    head = (xx * 2 + cc) * groups + g
    lane = lax.broadcasted_iota(jnp.int32, (SEQ_LEN, 128), 1)
    row = lax.broadcasted_iota(jnp.int32, (DH, SEQ_LEN), 0)
    qk, vx = qk_ref[0], vx_ref[0]
    do = dat_ref[head].astype(F32) * linv_ref[head]
    inner = -jnp.sum(do * at_ref[head].astype(F32), axis=0, keepdims=True)
    coarse = inner.astype(BF).astype(F32)
    tail = jnp.where(row == 0, coarse, jnp.where(row == 1, inner - coarse, 0.0))
    et = jnp.concatenate([do, tail], axis=0).astype(BF)
    e = et.T
    kt = qk.T[DH:]
    kq = jnp.concatenate([qk[:, DH:], qk[:, :DH]], axis=1)
    dk = jnp.zeros((SEQ_LEN, 128), F32)
    dv = jnp.zeros((SEQ_LEN, 128), F32)
    dqs = []
    for b in range(2):
        sl = slice(b * (SEQ_LEN // 2), (b + 1) * (SEQ_LEN // 2))
        p = p_ref[0, :, sl]
        ds = (p.astype(F32) * dot(vx, et[:, sl], 1, 0)).astype(BF)
        dv = dv + dot(p, e[sl], 1, 0)
        dk = dk + dot(ds, kq[sl], 1, 0)
        dqs.append(dot(kt, ds, 1, 0))
    dqt = jnp.concatenate(dqs, axis=1) * F32(DH**-0.5)
    dq = jnp.concatenate([dqt, jnp.zeros_like(dqt)], axis=0).T
    d_proj = jnp.concatenate([jnp.where(lane < DH, dq, dk), jnp.where(lane < DH, dv, 0.0)], axis=1).astype(BF)
    dp_ref[head] = d_proj
    dw = dot(xst_ref[...], d_proj, 1, 0)
    dw = jnp.concatenate([dw[:, :128], dw[:, 128:] + dwo_ref[head].astype(F32)], axis=1).astype(BF)
    dqkv_ref[g, cc, xx] = dw.reshape(dqkv_ref.shape[3:])

    early, late = pieces[:2], pieces[2:]
    todo = [[] for _ in range(NHEADS)]
    todo[0] += [p.hop1 for p in early] + [lambda: norm_pull(0), lambda: norm_push(1)]
    todo[1] += [p.hop1 for p in late]
    for n, chunk in enumerate(chunks):
        todo[2 * n + 1].append(chunk.hop0)
        if n + 1 < len(chunks):
            todo[2 * n + 2].append(chunk.hop1)
    todo[2] += [lambda: norm_pull(1), lambda: norm_push(2)]
    todo[3] += [p.hop2 for p in early]
    todo[4] += [p.hop2 for p in late] + [lambda: norm_pull(2), lambda: norm_push(3)]
    todo[5] += [p.hop3 for p in early]
    todo[6] += [p.hop3 for p in late] + [lambda: norm_pull(3), lambda: norm_push(4)]
    todo[7] += [p.hop4 for p in early]

    for t in range(NHEADS - 1):

        @pl.when(step == t)
        def _(t=t):
            for act in todo[t]:
                act()

    @pl.when(step == NHEADS - 1)
    def _():
        for act in todo[NHEADS - 1]:
            act()
        for k in range(4, len(partners)):
            norm_pull(k)
            if k + 1 < len(partners):
                norm_push(k + 1)
        norm_out[...] = norm_send[len(partners)]
        chunks[-1].hop1()
        partial = dot(dp_ref[0], wq_ref[:, :PART], 1, 1)
        for h in range(1, NHEADS):
            partial = partial + dot(dp_ref[h], wq_ref[:, h * PART : (h + 1) * PART], 1, 1)
        partial_ref[...] = partial.astype(BF)
        for p in late:
            p.hop4()
        for k in range(groups):
            for n in range(2):
                low = k * GROUPW + (n + 1) * PART
                grad_ref[:, low : low + PART] = final[2 * k + n]
            grad_ref[:, k * GROUPW : k * GROUPW + PART] = chunks[(k + 1) * X - 1].collect()
        sends.drain(place)


def backward_call(qk, vx, probs, linv, at, dat, xst, wq, dff, dwo, norm_grads, batches, heads):
    groups, rows = NHEADS // heads, D // batches
    X = Y = heads // 2
    Z = batches // Y
    tokens = xst.shape[1]
    whole = lambda shape: pl.BlockSpec(shape, lambda i: (0,) * len(shape), pipeline_mode=pl.Buffered(1))
    spot = lambda i: ((heads - 2 - 2 * ((i % heads) // 2) + i % 2) * groups + i // heads, 0, 0)
    per_head = lambda *shape: pl.BlockSpec((1,) + shape, spot)
    inputs = (linv, at, dat, xst, wq, dff, dwo, norm_grads)
    shapes = [((tokens, D), BF), ((rows, groups * GROUPW), F32), ((4, D), F32)]
    n = 2 * groups
    stages = 1 + sum(len(bits(v)) for v in (X, Y, Z))
    count = n * (1 + X - 1 + Y - 1 + Z - 1) + groups * (X + X - 1 + batches - 1) + stages
    return pl.pallas_call(
        functools.partial(backward_kernel, batches, heads),
        grid=(NHEADS,),
        in_specs=[per_head(tokens, 128), per_head(tokens, 128), per_head(tokens, tokens)]
        + [whole(a.shape) for a in inputs],
        out_specs=[whole(s[0]) for s in shapes],
        out_shape=[jax.ShapeDtypeStruct(*s) for s in shapes],
        scratch_shapes=[
            pltpu.VMEM((NHEADS, tokens, PART), BF),
            pltpu.VMEM((groups, 2, X, batches, rows, PART), BF),
            pltpu.VMEM((n, X, Z, Y, rows, PART), BF),
            pltpu.VMEM((n, X, Z, Y, rows, PART), BF),
            pltpu.VMEM((n, X - 1, Z, Y, rows, PART), BF),
            pltpu.VMEM((n, Y - 1, X, Z, rows, PART), BF),
            pltpu.VMEM((n, Z, Y, rows, PART), BF),
            pltpu.VMEM((n, X, Z, rows, PART), BF),
            pltpu.VMEM((n, X - 1, Z, rows, PART), BF),
            pltpu.VMEM((n, Z, rows, PART), BF),
            pltpu.VMEM((n, Z - 1, rows, PART), BF),
            pltpu.VMEM((n, rows, PART), F32),
            pltpu.VMEM((groups, X, batches, rows, PART), BF),
            pltpu.VMEM((groups, X, batches, rows, PART), BF),
            pltpu.VMEM((groups, X - 1, batches, rows, PART), BF),
            pltpu.VMEM((groups, batches, rows, PART), BF),
            pltpu.VMEM((groups, batches - 1, rows, PART), BF),
            pltpu.VMEM((stages + 1, 4, D), F32),
            pltpu.VMEM((stages, 4, D), F32),
            pltpu.SemaphoreType.DMA((n, 2 * X + Z)),
            pltpu.SemaphoreType.DMA((groups, 2 * X + batches)),
            pltpu.SemaphoreType.DMA((stages,)),
            pltpu.SemaphoreType.DMA((count,)),
        ],
        name="attend_backward",
        compiler_params=pltpu.CompilerParams(
            collective_id=2, has_side_effects=True, vmem_limit_bytes=VMEM_BYTES
        ),
    )(qk, vx, probs, *inputs)


def update_kernel(
    dmid_ref, partial_ref, grad_ref, weight_ref, first_ref, second_ref, ngrad_ref, nparam_ref, nfirst_ref, nsecond_ref,
    post_out, first_out, second_out, weight_out, nfirst_out, nsecond_out, nparam_out,
):
    post_out[...] = dmid_ref[...] + partial_ref[...].astype(F32)
    first_out[...], second_out[...], weight_out[...] = adam_update(
        weight_ref[...], grad_ref[...], first_ref[...], second_ref[...], WEIGHT_RATE, WEIGHT_DECAY
    )
    nfirst_out[...], nsecond_out[...], nparam_out[...] = adam_update(
        nparam_ref[...], ngrad_ref[...], nfirst_ref[...], nsecond_ref[...], NORM_RATE, 0.0
    )


def update_call(dmid, partial, grad, weights, first, second, ngrad, nparam, nfirst, nsecond):
    steps = 2
    cut = lambda a: pl.BlockSpec((a.shape[0] // steps, a.shape[1]), lambda i: (i, 0))
    same = lambda a: pl.BlockSpec(a.shape, lambda i: (0, 0))
    outs = [dmid, weights, weights, weights, nparam, nparam, nparam]
    return pl.pallas_call(
        update_kernel,
        grid=(steps,),
        in_specs=[cut(a) for a in (dmid, partial, grad, weights, first, second)]
        + [same(a) for a in (ngrad, nparam, nfirst, nsecond)],
        out_specs=[cut(a) for a in outs[:4]] + [same(a) for a in outs[4:]],
        out_shape=[jax.ShapeDtypeStruct(a.shape, F32) for a in outs],
        name="update",
        compiler_params=pltpu.CompilerParams(vmem_limit_bytes=VMEM_BYTES),
    )(dmid, partial, grad, weights, first, second, ngrad, nparam, nfirst, nsecond)


def shards(
    post_stream,
    dual_stream,
    post_cotangent,
    dual_cotangent,
    seq_lengths,
    owner_slots,
    weights,
    first_moment,
    second_moment,
    norm_gain,
    norm_bias,
    norm_first,
    norm_second,
):
    batches, heads = lax.axis_size("batch"), lax.axis_size("head")
    length = lax.dynamic_slice(seq_lengths, (lax.axis_index("head"),), (1,))
    qk, vx, probs, linv, at, xst, ga, gb = forward_call(owner_slots, length, post_stream, weights, batches, heads)
    post_out, dual_out, dmid, dat, wq, dff, dwo, norm_grads = middle_call(
        owner_slots, length, at, post_stream, dual_stream, post_cotangent, dual_cotangent, norm_gain, norm_bias,
        ga, gb, batches, heads,
    )
    partial, weight_grad, norm_grad = backward_call(
        qk, vx, probs, linv, at, dat, xst, wq, dff, dwo, norm_grads, batches, heads
    )
    norm_params = jnp.concatenate([norm_gain, norm_bias], axis=0)
    rest = update_call(
        dmid, partial, weight_grad, weights, first_moment, second_moment, norm_grad, norm_params, norm_first, norm_second
    )
    return (post_out, dual_out, *rest)


def solution(mesh):
    tokens, table, copied = P(("batch", "head"), None), P("batch", "head"), P()
    in_specs = (tokens,) * 4 + (P("batch"), copied) + (table,) * 3 + (copied,) * 4
    out_specs = (tokens,) * 3 + (table,) * 3 + (copied,) * 3
    return jax.shard_map(shards, mesh=mesh, in_specs=in_specs, out_specs=out_specs, check_vma=False)
```

```python
import functools
import math

import jax
import jax.numpy as jnp
from jax import lax
from jax.experimental import pallas as pl
from jax.experimental.pallas import tpu as pltpu
from jax.sharding import PartitionSpec as P

D = 512
FF = 2048
NHEADS = 8
DH = 64
SEQ_LEN = 1024
STEP = 10
GROUPW = 768
PART = 256

BETA_FIRST = 0.9
BETA_SECOND = 0.999
ADAM_EPSILON = 1e-08
WEIGHT_DECAY = 0.1
WEIGHT_RATE = 0.2
NORM_RATE = 0.2
NORM_EPSILON = 1e-05
MASK_VALUE = -1000000000.0

MESH = pl.DeviceIdType.MESH
F32 = jnp.float32
BF = jnp.bfloat16
VMEM_BYTES = 63 << 20
B_STEPS = (3, 6)
MID_STEPS = 4


def dot(a, b, ca, cb):
    return lax.dot_general(a, b, (((ca,), (cb,)), ((), ())), preferred_element_type=F32)


class Place:
    def __init__(self, batches, heads):
        self.X = self.Y = heads // 2
        self.Z = batches // self.Y
        self.batches, self.heads = batches, heads
        batch, head = lax.axis_index("batch"), lax.axis_index("head")
        self.j = batch
        self.z, self.y = batch // self.Y, batch % self.Y
        self.x, self.c = head // 2, head % 2
        self.xs = [lax.rem(self.x + d, self.X) for d in range(1, self.X)]
        self.ys = [lax.rem(self.y + d, self.Y) for d in range(1, self.Y)]
        self.zs = [lax.rem(self.z + d, self.Z) for d in range(1, self.Z)]

    def dev(self, z=None, y=None, x=None, c=None):
        z = self.z if z is None else z
        y = self.y if y is None else y
        x = self.x if x is None else x
        c = self.c if c is None else c
        return (z * self.Y + y, x * 2 + c)

    def greet(self, devices):
        barrier = pltpu.get_barrier_semaphore()
        for device in devices:
            pl.semaphore_signal(barrier, inc=1, device_id=device, device_id_type=MESH)
        pl.semaphore_wait(barrier, len(devices))

    def plane(self):
        return [(x, y) for x in [self.x] + self.xs for y in [self.y] + self.ys][1:]


class Sends:
    def __init__(self, sems):
        self.sems, self.count, self.made = sems, 0, []

    def push(self, src, dst, recv, device, like, cond=None):
        copy = pltpu.make_async_remote_copy(
            src_ref=src, dst_ref=dst, send_sem=self.sems.at[self.count], recv_sem=recv,
            device_id=device, device_id_type=MESH,
        )
        if cond is None:
            copy.start()
        else:
            pl.when(cond())(lambda: copy.start())
        self.made.append((self.count, like, cond))
        self.count += 1

    def drain(self, place):
        for k, like, cond in self.made:
            sent = pltpu.make_async_remote_copy(
                src_ref=like(), dst_ref=like(), send_sem=self.sems.at[k], recv_sem=self.sems.at[k],
                device_id=place.dev(), device_id_type=MESH,
            )
            if cond is None:
                sent.wait_send()
            else:
                pl.when(cond())(lambda sent=sent: sent.wait_send())


def arrived(place, ref, recv, send):
    pltpu.make_async_remote_copy(
        src_ref=ref, dst_ref=ref, send_sem=send, recv_sem=recv, device_id=place.dev(), device_id_type=MESH
    ).wait_recv()


def bits(n):
    return [1 << k for k in range(n.bit_length() - 1)]


def norm_forward(u, gain, bias):
    centred = u - jnp.mean(u, axis=-1, keepdims=True)
    recip = lax.rsqrt(jnp.mean(centred * centred, axis=-1, keepdims=True) + NORM_EPSILON)
    normed = centred * recip
    return normed * gain + bias, normed, recip


def norm_back(grad, normed, recip, gain):
    e = grad * gain
    slope = jnp.mean(e * normed, axis=-1, keepdims=True)
    return recip * (e - jnp.mean(e, axis=-1, keepdims=True) - normed * slope)


def adam_update(param, grad, first, second, rate, decay):
    first_new = BETA_FIRST * first + (1.0 - BETA_FIRST) * grad
    second_new = BETA_SECOND * second + (1.0 - BETA_SECOND) * grad * grad
    first_hat = first_new * (1.0 / (1.0 - BETA_FIRST**STEP))
    second_hat = second_new * (1.0 / (1.0 - BETA_SECOND**STEP))
    param_new = param - rate * (first_hat / (jnp.sqrt(second_hat) + ADAM_EPSILON) + decay * param)
    return first_new, second_new, param_new


class Piece:
    def __init__(self, place, source, x_first, bufs, recv, sends):
        self.place, self.source, self.x_first, self.sends = place, source, x_first, sends
        self.s1 = source.at[place.c]
        self.r1, self.r2, self.s2, self.r3, self.s3, self.r4, self.final = bufs
        self.recv = recv

    def axis(self, x):
        p = self.place
        return (p.X, p.x, lambda v: p.dev(x=v)) if x else (p.Y, p.y, lambda v: p.dev(y=v))

    def send(self, axis, cut, buf, base):
        size, me, dev = axis
        for d in range(1, size):
            to = lax.rem(me + d, size)
            self.sends.push(cut(to), buf.at[d - 1], self.recv.at[base + d], dev(to), lambda: buf.at[0])

    def add(self, axis, own, buf, base):
        total = own.astype(F32)
        for d in range(1, axis[0]):
            arrived(self.place, buf.at[d - 1], self.recv.at[base + d], self.sends.sems.at[0])
            total = total + buf[d - 1].astype(F32)
        return total

    def hop0(self):
        p = self.place
        self.sends.push(self.source.at[1 - p.c], self.r1, self.recv.at[0], p.dev(c=1 - p.c), lambda: self.r1)

    def hop1(self):
        p = self.place
        arrived(p, self.r1, self.recv.at[0], self.sends.sems.at[0])
        self.s1[...] = (self.s1[...].astype(F32) + self.r1[...].astype(F32)).astype(BF)
        cut = lambda to: self.s1.at[to] if self.x_first else self.s1.at[:, :, to]
        self.send(self.axis(self.x_first), cut, self.r2, 0)

    def hop2(self):
        p = self.place
        own = self.s1[p.x] if self.x_first else self.s1[:, :, p.y]
        self.s2[...] = self.add(self.axis(self.x_first), own, self.r2, 0).astype(BF)
        cut = lambda to: self.s2.at[:, to] if self.x_first else self.s2.at[to]
        self.send(self.axis(not self.x_first), cut, self.r3, p.X)

    def hop3(self):
        p = self.place
        own = self.s2[:, p.y] if self.x_first else self.s2[p.x]
        self.s3[...] = self.add(self.axis(not self.x_first), own, self.r3, p.X).astype(BF)
        self.send((p.Z, p.z, lambda v: p.dev(z=v)), lambda to: self.s3.at[to], self.r4, 2 * p.X)

    def hop4(self):
        p = self.place
        self.final[...] = self.add((p.Z, p.z, None), self.s3[p.z], self.r4, 2 * p.X)


class Chunk:
    def __init__(self, place, g, dx, source, bufs, recv, sends):
        self.place, self.dx, self.sends = place, dx, sends
        r1, rx, r2 = bufs
        self.source, self.r1, self.rx, self.r2 = source.at[g], r1.at[g, dx], rx.at[g], r2.at[g]
        self.recv = recv.at[g]

    def hop0(self):
        p = self.place
        x = lax.rem(p.x + self.dx, p.X)
        self.sends.push(self.source.at[1 - p.c, x], self.r1, self.recv.at[self.dx], p.dev(c=1 - p.c), lambda: self.r1)

    def hop1(self):
        p = self.place
        x = lax.rem(p.x + self.dx, p.X)
        arrived(p, self.r1, self.recv.at[self.dx], self.sends.sems.at[0])
        total = self.source[p.c, x].astype(F32) + self.r1[...].astype(F32)
        if self.dx:
            self.source[p.c, x] = total.astype(BF)
            self.sends.push(
                self.source.at[p.c, x], self.rx.at[self.dx - 1], self.recv.at[p.X + self.dx], p.dev(x=x), lambda: self.r1
            )
            return
        for d in range(1, p.X):
            arrived(p, self.rx.at[d - 1], self.recv.at[p.X + d], self.sends.sems.at[0])
            total = total + self.rx[d - 1].astype(F32)
        self.source[p.c, x] = total.astype(BF)
        for d in range(1, p.batches):
            j = lax.rem(p.j + d, p.batches)
            self.sends.push(
                self.source.at[p.c, x, j], self.r2.at[d - 1], self.recv.at[2 * p.X + d], (j, p.x * 2 + p.c), lambda: self.r2.at[0]
            )

    def collect(self):
        p = self.place
        total = self.source[p.c, p.x, p.j].astype(F32)
        for d in range(1, p.batches):
            arrived(p, self.r2.at[d - 1], self.recv.at[2 * p.X + d], self.sends.sems.at[0])
            total = total + self.r2[d - 1].astype(F32)
        return total


def forward_sends(X, Y, Z, groups):
    part_a = groups * (Z - 1 + Y - 1) + (X - 1) * (1 + Z - 1 + Y - 1) + X
    part_b = (X - 1) + (Y - 1) + (Z - 1) + 1 + (Z - 1) * (X + Y - 1)
    part_b += Z * (2 * (X - 1) * (Y - 1) + (X - 1) + (Y - 1) + (X - 1) * (Y - 1))
    return part_a + part_b


def backward_sends(X, Y, Z, groups):
    stages = 1 + sum(len(bits(v)) for v in (X, Y, Z))
    return 2 * groups * (X + Y + Z - 2) + groups * (X + X - 1 + Y * Z - 1) + stages


def layer_kernel(
    batches, heads, owner_ref, length_ref, post_ref, weight_ref, gain_ref, bias_ref, dual_ref, pc_ref, dc_ref,
    post_out, dual_out, dmid_ref, partial_ref, grad_ref, norm_out, p_hbm,
    pick_ref, xs_ref, xst_ref, ga_ref, gb_ref, qk_ref, vx_ref, wide_ref, linv_ref, at_ref, dat_ref,
    w12_ref, wo_ref, mbt_ref, dft_ref, dbt_ref, dwo_ref, dqkv_ref,
    r1, xr2, yr2, xs2, ys2, r3, s3, r4, final, qr1, qrx, qr2, norm_send, norm_recv,
    recv_z, recv_y, recv_x, core_a, recv_b, send_f, recv_f, recv_q, norm_sems, send_r, p_sems,
):
    place = Place(batches, heads)
    groups, rows = NHEADS // heads, D // batches
    parts = 2 * groups
    X, Y, Z = place.X, place.Y, place.Z
    c, x, y, z = place.c, place.x, place.y, place.z
    step = pl.program_id(0)
    mid_at, dw_at, back_at = NHEADS, NHEADS + MID_STEPS, NHEADS + MID_STEPS + parts
    last_at = back_at + NHEADS - 1
    sends = Sends(send_f)
    dummy = send_f.at[0]

    def at_step(k):
        return pl.when(step == k)

    def core_push_a(xx):
        ref = ga_ref.at[c, xx]
        sends.push(ref, ref, core_a.at[xx], place.dev(c=1 - c), lambda: ga_ref.at[0, 0])

    def got_b(cc, xx, zz, yy):
        arrived(place, gb_ref.at[:, cc, xx, zz, yy], recv_b.at[cc, xx, zz, yy], dummy)

    def push_b(xx, zz, yy, device, cond=None):
        ref = gb_ref.at[:, c, xx, zz, yy]
        sends.push(ref, ref, recv_b.at[c, xx, zz, yy], device, lambda: gb_ref.at[:, 0, 0, 0, 0], cond)

    def side(offset):
        zo = lax.rem(z + offset, Z)
        low = lambda: lax.rem(place.z + offset, Z) < (3 * Z) // 4
        for xx in place.xs:
            got_b(c, xx, zo, y)
            for yy in place.ys:
                push_b(xx, zo, y, place.dev(y=yy), low)
            push_b(xx, zo, y, place.dev(c=1 - c))
        for yy in place.ys:
            got_b(c, x, zo, yy)
            for xx in place.xs:
                push_b(x, zo, yy, place.dev(x=xx), lambda: jnp.logical_not(low()))
            push_b(x, zo, yy, place.dev(c=1 - c))

    @at_step(0)
    def _():
        weight = weight_ref[...]
        for g in range(groups):
            ga_ref[c, x, z, y, g] = weight[:, g * GROUPW : g * GROUPW + PART].astype(BF)
        peers = [place.dev(z=zz, y=yy) for zz in [z] + place.zs for yy in [y] + place.ys][1:]
        place.greet(peers + [place.dev(x=xx) for xx in place.xs] + [place.dev(c=1 - c)])
        for g in range(groups):
            own = ga_ref.at[c, x, z, y, g]
            for zz in place.zs:
                sends.push(own, own, recv_z.at[g, z], place.dev(z=zz), lambda: ga_ref.at[0, 0, 0, 0, 0])
        own = ga_ref.at[c, x, z, y]
        for xx in place.xs:
            sends.push(own, own, recv_x.at[x, z], place.dev(x=xx), lambda: ga_ref.at[0, 0, 0, 0])
        for k in range(parts):
            low = (k % groups) * GROUPW + (2 - k // groups) * PART
            gb_ref[k, c, x, z, y] = weight[:, low : low + PART].astype(BF)
        for yy in place.ys:
            push_b(x, z, y, place.dev(y=yy))
        for xx in place.xs:
            push_b(x, z, y, place.dev(x=xx))
        lane = lax.broadcasted_iota(jnp.int32, (1, D), 1)
        source = lane % rows
        for b in range(batches):
            source = jnp.where(lane // rows == b, source + owner_ref[b] * rows, source)
        pick = (lax.broadcasted_iota(jnp.int32, (D, D), 0) == source).astype(F32).astype(BF)
        pick_ref[...] = pick
        ordered = dot(post_ref[...], pick, 1, 0).astype(BF)
        xs_ref[...] = ordered
        xst_ref[...] = ordered.T
        for g in range(groups):
            for zz in place.zs:
                arrived(place, ga_ref.at[c, x, zz, y, g], recv_z.at[g, zz], dummy)
            column = ga_ref.at[c, x, :, y, g]
            for yy in place.ys:
                sends.push(column, column, recv_y.at[g, y], place.dev(y=yy), lambda: ga_ref.at[0, 0, :, 0, 0])
        for zz in place.zs:
            push_b(x, z, y, place.dev(z=zz))
        for xx in place.xs:
            for zz in place.zs:
                block = ga_ref.at[c, x, zz, y]
                sends.push(block, block, recv_x.at[x, zz], place.dev(x=xx), lambda: ga_ref.at[0, 0, 0, 0])
        push_b(x, z, y, place.dev(c=1 - c))

    for g in range(groups):

        @at_step(g)
        def _(g=g):
            for yy in place.ys:
                arrived(place, ga_ref.at[c, x, :, yy, g], recv_y.at[g, yy], dummy)
            if g == groups - 1:
                for yy in place.ys:
                    column = ga_ref.at[c, x, :, yy]
                    for xx in place.xs:
                        sends.push(
                            column, column, recv_x.at[x, Z + yy], place.dev(x=xx), lambda: ga_ref.at[0, 0, :, 0]
                        )
                core_push_a(x)

    for k in range(1, heads):

        @at_step(k * groups)
        def _(k=k):
            xx = lax.rem(x + k // 2, X)
            if k % 2 == 0:
                for zz in [z] + place.zs:
                    arrived(place, ga_ref.at[c, xx, zz, y], recv_x.at[xx, zz], dummy)
                for yy in place.ys:
                    arrived(place, ga_ref.at[c, xx, :, yy], recv_x.at[xx, Z + yy], dummy)
                core_push_a(xx)
            else:
                arrived(place, ga_ref.at[1 - c, xx], core_a.at[xx], dummy)

    @at_step(B_STEPS[0])
    def _():
        for zz in place.zs:
            got_b(c, x, zz, y)
            for xx in place.xs:
                push_b(x, zz, y, place.dev(x=xx))
            for yy in place.ys:
                push_b(x, zz, y, place.dev(y=yy))
            push_b(x, zz, y, place.dev(c=1 - c))
        side(0)

    @at_step(B_STEPS[1])
    def _():
        for offset in range(1, Z):
            side(offset)

    def p_store(i):
        slot = lax.rem(i, 4)
        return pltpu.make_async_copy(wide_ref.at[pl.ds(2 * slot, 2)], p_hbm.at[i], p_sems.at[slot])

    def p_fetch(i):
        g, r = i // heads, i % heads
        spot = (heads - 2 - 2 * (r // 2) + r % 2) * groups + g
        slot = lax.rem(i, 2)
        return pltpu.make_async_copy(p_hbm.at[spot], wide_ref.at[pl.ds(2 * slot, 2)], p_sems.at[slot])

    @pl.when(step < mid_at)
    def _():
        @pl.when(step >= 4)
        def _():
            p_store(step - 4).wait()

        q, g = step // groups, step % groups
        cc, xx = (c + q) % 2, lax.rem(x + q // 2, X)
        head = (xx * 2 + cc) * groups + g
        w = ga_ref[cc, xx, :, :, g].reshape(D, PART)
        proj = dot(xs_ref[...], w, 1, 0)
        lane = lax.broadcasted_iota(jnp.int32, (SEQ_LEN, 128), 1)
        qk = proj[:, :128].astype(BF)
        qk = jnp.where(lane < DH, qk * BF(DH**-0.5), qk)
        v = proj[:, 128:].astype(BF)
        vx = jnp.where(lane < DH, v, jnp.where(lane < DH + 2, BF(1), BF(0)))
        qk_ref[head] = qk
        vx_ref[head] = vx
        q_only = jnp.where(lane < DH, qk, BF(0))
        kq = jnp.concatenate([qk[:, DH:], qk[:, :DH]], axis=1)
        vxt = vx.T[: DH + 8]
        keep = lax.broadcasted_iota(jnp.int32, (SEQ_LEN, 1), 0) < length_ref[0]
        s = dot(kq, q_only, 1, 1)
        s = jnp.where(keep, s, F32(MASK_VALUE))
        m = jnp.max(s, axis=0, keepdims=True)
        p = jnp.exp(s - m).astype(BF)
        slot = lax.rem(step, 4)
        wide_ref[2 * slot] = p[:, : SEQ_LEN // 2]
        wide_ref[2 * slot + 1] = p[:, SEQ_LEN // 2 :]
        o = dot(vxt, p, 1, 0)
        r = 1.0 / o[DH : DH + 1]
        linv_ref[head] = r
        at_ref[head] = (o[:DH] * r).astype(BF)
        p_store(step).start()

    @at_step(mid_at)
    def _():
        for i in range(NHEADS - 4, NHEADS):
            p_store(i).wait()
        for offset in range(Z):
            zz = lax.rem(z + offset, Z)
            for yy in place.ys:
                for xx in place.xs:
                    got_b(c, xx, zz, yy)
                    push_b(xx, zz, yy, place.dev(c=1 - c))
        for xx in range(X):
            for zz in range(Z):
                for yy in range(Y):
                    got_b(1 - c, xx, zz, yy)
        held = []
        for b in range(batches):
            found = 0
            for j in range(1, batches):
                found = jnp.where(owner_ref[j] == b, j, found)
            held.append(found)
        for b in range(batches):
            there = slice(b * rows, (b + 1) * rows)
            for h in range(NHEADS):
                g, xx, cc = h % groups, (h // groups) // 2, (h // groups) % 2
                wo_ref[there, h * DH : (h + 1) * DH] = ga_ref[cc, xx, held[b] // Y, held[b] % Y, g][:, 3 * DH :]
                for k in range(2):
                    w12_ref[1 - k, there, h * PART : (h + 1) * PART] = gb_ref[
                        k * groups + g, cc, xx, held[b] // Y, held[b] % Y
                    ]
        norm_send[0] = jnp.zeros((4, D), F32)

    @pl.when(jnp.logical_and(step >= mid_at, step < dw_at))
    def _():
        t = step - mid_at
        block = SEQ_LEN // MID_STEPS
        here = pl.ds(pl.multiple_of(t * block, block), block)
        at = at_ref[:, :, here].reshape(D, block)
        gain, bias = gain_ref[...], bias_ref[...]
        w1, w2, wo, pick = w12_ref[0], w12_ref[1], wo_ref[...], pick_ref[...]
        branch = dot(at, wo, 0, 1)
        middle, n1, r1_ = norm_forward(post_ref[here, :].astype(F32) + branch, gain[0:1], bias[0:1])
        middle_low = middle.astype(BF)
        pre = dot(middle_low, w1, 1, 0)
        cdf = 0.5 + 0.5 * lax.erf(pre * F32(math.sqrt(0.5)))
        density = jnp.exp(pre * pre * F32(-0.5)) * F32(1.0 / math.sqrt(2.0 * math.pi))
        hidden = (pre * cdf).astype(BF)
        slope = cdf + pre * density
        feed = dot(hidden, w2, 1, 1)
        out, n2, r2_ = norm_forward(middle + feed, gain[1:2], bias[1:2])
        post_out[...] = out.astype(BF)
        dual_out[...] = dual_ref[...] + branch + feed
        keep = t * block + lax.broadcasted_iota(jnp.int32, (block, 1), 0) < length_ref[0]
        d_out = jnp.where(keep, pc_ref[...].astype(F32), 0.0)
        d_dual = jnp.where(keep, dc_ref[...].astype(F32), 0.0)
        d_pre = norm_back(d_out, n2, r2_, gain[1:2])
        d_feed = (d_pre + d_dual).astype(BF)
        d_hidden = dot(d_feed, w2, 1, 0)
        d_hidden_pre = (d_hidden * slope).astype(BF)
        for k in range(4):
            wide_ref[k, here, :] = hidden[:, k * 512 : (k + 1) * 512]
            wide_ref[4 + k, here, :] = d_hidden_pre[:, k * 512 : (k + 1) * 512]
        d_middle = d_pre + dot(d_hidden_pre, w1, 1, 1)
        d_mid = norm_back(d_middle, n1, r1_, gain[0:1])
        dmid_ref[...] = d_mid
        d_branch = (d_mid + d_dual).astype(BF)
        mbt_ref[:, here] = dot(pick, middle_low, 0, 1).astype(BF)
        dft_ref[:, here] = dot(pick, d_feed, 0, 1).astype(BF)
        dbt_ref[:, here] = dot(pick, d_branch, 0, 1).astype(BF)
        dat_ref[:, :, here] = dot(wo, d_branch, 0, 1).astype(BF).reshape(NHEADS, DH, block)
        sums = [jnp.sum(v, axis=0, keepdims=True) for v in (d_middle * n1, d_out * n2, d_middle, d_out)]
        norm_send[0] = norm_send[0] + jnp.concatenate(sums, axis=0)

    reduce_sends = Sends(send_r)
    pieces = []
    for k in range(parts):
        x_first = k == 0
        bufs = (r1.at[k], xr2.at[0], xs2.at[0]) if x_first else (r1.at[k], yr2.at[k - 1], ys2.at[k - 1])
        bufs += tuple(b.at[k] for b in (r3, s3, r4, final))
        pieces.append(Piece(place, gb_ref.at[k], x_first, bufs, recv_f.at[k], reduce_sends))
    chunks = [
        Chunk(place, g, dx, dqkv_ref, (qr1, qrx, qr2), recv_q, reduce_sends)
        for g in range(groups)
        for dx in reversed(range(X))
    ]
    partners = [place.dev(c=1 - c)]
    flip = lambda v, b: v + b - 2 * b * ((v // b) % 2)
    partners += [place.dev(x=flip(x, b)) for b in bits(X)]
    partners += [place.dev(y=flip(y, b)) for b in bits(Y)]
    partners += [place.dev(z=flip(z, b)) for b in bits(Z)]

    def norm_push(k):
        reduce_sends.push(norm_send.at[k], norm_recv.at[k], norm_sems.at[k], partners[k], lambda: norm_send.at[0])

    def norm_pull(k):
        arrived(place, norm_recv.at[k], norm_sems.at[k], send_r.at[0])
        norm_send[k + 1] = norm_send[k] + norm_recv[k]

    for k in range(parts):

        @at_step(dw_at + k)
        def _(k=k):
            if k == 0:
                sends.drain(place)
                norm_push(0)
                dwo = dot(dbt_ref[...], at_ref[...].reshape(D, SEQ_LEN), 1, 1).astype(BF)
                empty = jnp.zeros((D, DH), BF)
                for h in range(NHEADS):
                    dwo_ref[h] = jnp.concatenate([empty, dwo[:, h * DH : (h + 1) * DH]], axis=1)
            if k == groups:
                p_fetch(0).start()
                p_fetch(1).start()
            left = (dft_ref if k < groups else mbt_ref)[...]
            for device in range(heads):
                h = device * groups + k % groups
                held = wide_ref[4 * (k // groups) + h // 2, :, (h % 2) * PART : (h % 2 + 1) * PART]
                grad = dot(left, held, 1, 0).astype(BF)
                gb_ref[k, device % 2, device // 2] = grad.reshape(Z, Y, rows, PART)
            pieces[k].hop0()
            if k:
                pieces[k - 1].hop1()

    @pl.when(step >= back_at)
    def _():
        i = step - back_at
        p_fetch(i).wait()
        g, r = i // heads, i % heads
        cc, xx = (c + r) % 2, lax.rem(x + X - 1 - r // 2, X)
        head = (xx * 2 + cc) * groups + g
        lane = lax.broadcasted_iota(jnp.int32, (SEQ_LEN, 128), 1)
        row = lax.broadcasted_iota(jnp.int32, (DH, SEQ_LEN), 0)
        qk, vx = qk_ref[head], vx_ref[head]
        do = dat_ref[head].astype(F32) * linv_ref[head]
        inner = -jnp.sum(do * at_ref[head].astype(F32), axis=0, keepdims=True)
        coarse = inner.astype(BF).astype(F32)
        tail = jnp.where(row == 0, coarse, jnp.where(row == 1, inner - coarse, 0.0))
        et = jnp.concatenate([do, tail], axis=0).astype(BF)
        e = et.T
        kt = qk.T[DH:]
        kq = jnp.concatenate([qk[:, DH:], qk[:, :DH]], axis=1)
        dk = jnp.zeros((SEQ_LEN, 128), F32)
        dv = jnp.zeros((SEQ_LEN, 128), F32)
        dqs = []
        slot = lax.rem(i, 2)
        for b in range(2):
            sl = slice(b * (SEQ_LEN // 2), (b + 1) * (SEQ_LEN // 2))
            p = wide_ref[2 * slot + b]
            ds = (p.astype(F32) * dot(vx, et[:, sl], 1, 0)).astype(BF)
            dv = dv + dot(p, e[sl], 1, 0)
            dk = dk + dot(ds, kq[sl], 1, 0)
            dqs.append(dot(kt, ds, 1, 0))
        dqt = jnp.concatenate(dqs, axis=1) * F32(DH**-0.5)
        dq = jnp.concatenate([dqt, jnp.zeros_like(dqt)], axis=0).T
        d_proj = jnp.concatenate([jnp.where(lane < DH, dq, dk), jnp.where(lane < DH, dv, 0.0)], axis=1).astype(BF)
        cols = pl.ds(pl.multiple_of(head * PART, PART), PART)
        w12_ref[0, :, cols] = d_proj[: SEQ_LEN // 2]
        w12_ref[1, :, cols] = d_proj[SEQ_LEN // 2 :]
        dw = dot(xst_ref[...], d_proj, 1, 0)
        dw = jnp.concatenate([dw[:, :128], dw[:, 128:] + dwo_ref[head].astype(F32)], axis=1).astype(BF)
        dqkv_ref[g, cc, xx] = dw.reshape(dqkv_ref.shape[3:])

        @pl.when(i + 2 < NHEADS)
        def _():
            p_fetch(i + 2).start()

    todo = [[] for _ in range(NHEADS)]
    todo[0] += [pieces[-1].hop1, lambda: norm_pull(0), lambda: norm_push(1)]
    for n, chunk in enumerate(chunks):
        todo[2 * n + 1].append(chunk.hop0)
        if n + 1 < len(chunks):
            todo[2 * n + 2].append(chunk.hop1)
    half = parts // 2
    todo[1] += [p.hop2 for p in pieces[:half]]
    todo[2] += [lambda: norm_pull(1), lambda: norm_push(2)]
    todo[3] += [p.hop2 for p in pieces[half:]] + [p.hop3 for p in pieces[:half]]
    todo[4] += [lambda: norm_pull(2), lambda: norm_push(3)]
    todo[5] += [p.hop3 for p in pieces[half:]] + [p.hop4 for p in pieces[:half]]
    todo[6] += [lambda: norm_pull(3), lambda: norm_push(4)]
    todo[7] += [p.hop4 for p in pieces[half:]]

    for t in range(NHEADS):

        @at_step(back_at + t)
        def _(t=t):
            for act in todo[t]:
                act()

    @at_step(last_at)
    def _():
        for k in range(4, len(partners)):
            norm_pull(k)
            if k + 1 < len(partners):
                norm_push(k + 1)
        norm_out[...] = norm_send[len(partners)]
        chunks[-1].hop1()
        table = []
        for h in range(NHEADS):
            g, xx, cc = h % groups, (h // groups) // 2, (h // groups) % 2
            table.append(ga_ref[cc, xx, :, :, g].reshape(D, PART))
        table = jnp.concatenate(table, axis=1)
        for k in range(2):
            ordered = dot(w12_ref[k], table, 1, 1).astype(BF)
            partial_ref[k * (SEQ_LEN // 2) : (k + 1) * (SEQ_LEN // 2)] = dot(ordered, pick_ref[...], 1, 1).astype(BF)
        for g in range(groups):
            low = g * GROUPW
            grad_ref[:, low + PART : low + 2 * PART] = final[groups + g]
            grad_ref[:, low + 2 * PART : low + 3 * PART] = final[g]
            grad_ref[:, low : low + PART] = chunks[(g + 1) * X - 1].collect()
        reduce_sends.drain(place)


def layer_call(owner, length, post, weights, gain, bias, dual, pc, dc, batches, heads):
    groups, rows = NHEADS // heads, D // batches
    parts = 2 * groups
    X = Y = heads // 2
    Z = batches // Y
    tokens = post.shape[0]
    assert tokens == SEQ_LEN
    block = tokens // MID_STEPS
    stages = 1 + sum(len(bits(v)) for v in (X, Y, Z))
    scalar = pl.BlockSpec(memory_space=pltpu.SMEM)
    whole = lambda a: pl.BlockSpec(a.shape, lambda i: (0,) * len(a.shape), pipeline_mode=pl.Buffered(1))
    token = pl.BlockSpec((block, D), lambda i: (jnp.clip(i - NHEADS, 0, MID_STEPS - 1), 0))
    outs = [
        jax.ShapeDtypeStruct((tokens, D), BF),
        jax.ShapeDtypeStruct((tokens, D), F32),
        jax.ShapeDtypeStruct((tokens, D), F32),
        jax.ShapeDtypeStruct((tokens, D), BF),
        jax.ShapeDtypeStruct((rows, groups * GROUPW), F32),
        jax.ShapeDtypeStruct((4, D), F32),
        jax.ShapeDtypeStruct((NHEADS, 2, tokens, tokens // 2), BF),
    ]
    dma = pltpu.SemaphoreType.DMA
    return pl.pallas_call(
        functools.partial(layer_kernel, batches, heads),
        grid=(NHEADS + MID_STEPS + parts + NHEADS,),
        in_specs=[scalar, scalar, whole(post), whole(weights), whole(gain), whole(bias), token, token, token],
        out_specs=[token, token, token] + [whole(a) for a in outs[3:6]] + [pl.BlockSpec(memory_space=pl.ANY)],
        out_shape=outs,
        scratch_shapes=[
            pltpu.VMEM((D, D), BF),
            pltpu.VMEM((tokens, D), BF),
            pltpu.VMEM((D, tokens), BF),
            pltpu.VMEM((2, X, Z, Y, groups, rows, PART), BF),
            pltpu.VMEM((parts, 2, X, Z, Y, rows, PART), BF),
            pltpu.VMEM((NHEADS, tokens, 128), BF),
            pltpu.VMEM((NHEADS, tokens, 128), BF),
            pltpu.VMEM((8, tokens, tokens // 2), BF),
            pltpu.VMEM((NHEADS, 1, tokens), F32),
            pltpu.VMEM((NHEADS, DH, tokens), BF),
            pltpu.VMEM((NHEADS, DH, tokens), BF),
            pltpu.VMEM((2, D, FF), BF),
            pltpu.VMEM((D, D), BF),
            pltpu.VMEM((D, tokens), BF),
            pltpu.VMEM((D, tokens), BF),
            pltpu.VMEM((D, tokens), BF),
            pltpu.VMEM((NHEADS, D, 128), BF),
            pltpu.VMEM((groups, 2, X, batches, rows, PART), BF),
            pltpu.VMEM((parts, X, Z, Y, rows, PART), BF),
            pltpu.VMEM((1, X - 1, Z, Y, rows, PART), BF),
            pltpu.VMEM((parts - 1, Y - 1, X, Z, rows, PART), BF),
            pltpu.VMEM((1, Z, Y, rows, PART), BF),
            pltpu.VMEM((parts - 1, X, Z, rows, PART), BF),
            pltpu.VMEM((parts, X - 1, Z, rows, PART), BF),
            pltpu.VMEM((parts, Z, rows, PART), BF),
            pltpu.VMEM((parts, Z - 1, rows, PART), BF),
            pltpu.VMEM((parts, rows, PART), F32),
            pltpu.VMEM((groups, X, batches, rows, PART), BF),
            pltpu.VMEM((groups, X - 1, batches, rows, PART), BF),
            pltpu.VMEM((groups, batches - 1, rows, PART), BF),
            pltpu.VMEM((stages + 1, 4, D), F32),
            pltpu.VMEM((stages, 4, D), F32),
            dma((groups, Z)),
            dma((groups, Y)),
            dma((X, Z + Y)),
            dma((X,)),
            dma((2, X, Z, Y)),
            dma((forward_sends(X, Y, Z, groups),)),
            dma((parts, 2 * X + Z)),
            dma((groups, 2 * X + batches)),
            dma((stages,)),
            dma((backward_sends(X, Y, Z, groups),)),
            dma((4,)),
        ],
        name="layer",
        compiler_params=pltpu.CompilerParams(
            collective_id=1, has_side_effects=True, vmem_limit_bytes=VMEM_BYTES
        ),
    )(owner, length, post, weights, gain, bias, dual, pc, dc)


def update_kernel(
    post_in, dual_in, dmid_ref, partial_ref, grad_ref, weight_ref, first_ref, second_ref,
    ngrad_ref, nparam_ref, nfirst_ref, nsecond_ref,
    post_out, dual_out, grad_out, first_out, second_out, weight_out, nfirst_out, nsecond_out, nparam_out,
):
    post_out[...] = post_in[...]
    dual_out[...] = dual_in[...]
    grad_out[...] = dmid_ref[...] + partial_ref[...].astype(F32)
    first_out[...], second_out[...], weight_out[...] = adam_update(
        weight_ref[...], grad_ref[...], first_ref[...], second_ref[...], WEIGHT_RATE, WEIGHT_DECAY
    )
    nfirst_out[...], nsecond_out[...], nparam_out[...] = adam_update(
        nparam_ref[...], ngrad_ref[...], nfirst_ref[...], nsecond_ref[...], NORM_RATE, 0.0
    )


def update_call(post, dual, dmid, partial, grad, weights, first, second, ngrad, nparam, nfirst, nsecond):
    steps = 2
    cut = lambda a: pl.BlockSpec((a.shape[0] // steps, a.shape[1]), lambda i: (i, 0))
    same = lambda a: pl.BlockSpec(a.shape, lambda i: (0, 0))
    outs = [post, dual, dmid, weights, weights, weights, nparam, nparam, nparam]
    return pl.pallas_call(
        update_kernel,
        grid=(steps,),
        in_specs=[cut(a) for a in (post, dual, dmid, partial, grad, weights, first, second)]
        + [same(a) for a in (ngrad, nparam, nfirst, nsecond)],
        out_specs=[cut(a) for a in outs[:6]] + [same(a) for a in outs[6:]],
        out_shape=[jax.ShapeDtypeStruct(a.shape, a.dtype) for a in outs],
        name="update",
        compiler_params=pltpu.CompilerParams(vmem_limit_bytes=VMEM_BYTES),
    )(post, dual, dmid, partial, grad, weights, first, second, ngrad, nparam, nfirst, nsecond)


def shards(
    post_stream,
    dual_stream,
    post_cotangent,
    dual_cotangent,
    seq_lengths,
    owner_slots,
    weights,
    first_moment,
    second_moment,
    norm_gain,
    norm_bias,
    norm_first,
    norm_second,
):
    batches, heads = lax.axis_size("batch"), lax.axis_size("head")
    length = lax.dynamic_slice(seq_lengths, (lax.axis_index("head"),), (1,))
    post, dual, dmid, partial, grad, norm_grad, _ = layer_call(
        owner_slots, length, post_stream, weights, norm_gain, norm_bias, dual_stream, post_cotangent, dual_cotangent,
        batches, heads,
    )
    norm_params = jnp.concatenate([norm_gain, norm_bias], axis=0)
    return update_call(
        post, dual, dmid, partial, grad, weights, first_moment, second_moment,
        norm_grad, norm_params, norm_first, norm_second,
    )


def solution(mesh):
    tokens, table, copied = P(("batch", "head"), None), P("batch", "head"), P()
    in_specs = (tokens,) * 4 + (P("batch"), copied) + (table,) * 3 + (copied,) * 4
    out_specs = (tokens,) * 3 + (table,) * 3 + (copied,) * 3
    return jax.shard_map(shards, mesh=mesh, in_specs=in_specs, out_specs=out_specs, check_vma=False)
```

```python
import functools
import math

import jax
import jax.numpy as jnp
from jax import lax
from jax.experimental import pallas as pl
from jax.experimental.pallas import tpu as pltpu
from jax.sharding import PartitionSpec as P

D = 512
FF = 2048
NHEADS = 8
DH = 64
SEQ_LEN = 1024
STEP = 10
GROUPW = 768
PART = 256

BETA_FIRST = 0.9
BETA_SECOND = 0.999
ADAM_EPSILON = 1e-08
WEIGHT_DECAY = 0.1
WEIGHT_RATE = 0.2
NORM_RATE = 0.2
NORM_EPSILON = 1e-05
MASK_VALUE = -1000000000.0

MESH = pl.DeviceIdType.MESH
F32 = jnp.float32
BF = jnp.bfloat16
VMEM_BYTES = 63 << 20
B_PLAN = {'first': [], 'after': [('send', 1), ('send', 2), ('send', 3)], 0: [], 1: [], 2: [('side', 0)], 3: [('pass', 1), ('pass', 2), ('pass', 3)], 4: [], 5: [('side', 1)], 6: [('side', 2)], 7: [('side', 3)]}
MID_STEPS = 2
UNROLL = 2
X_FIRST = (0, 2)


def dot(a, b, ca, cb):
    return lax.dot_general(a, b, (((ca,), (cb,)), ((), ())), preferred_element_type=F32)


class Place:
    def __init__(self, batches, heads):
        self.X = self.Y = heads // 2
        self.Z = batches // self.Y
        self.batches, self.heads = batches, heads
        batch, head = lax.axis_index("batch"), lax.axis_index("head")
        self.j = batch
        self.z, self.y = batch // self.Y, batch % self.Y
        self.x, self.c = head // 2, head % 2
        self.xs = [lax.rem(self.x + d, self.X) for d in range(1, self.X)]
        self.ys = [lax.rem(self.y + d, self.Y) for d in range(1, self.Y)]
        self.zs = [lax.rem(self.z + d, self.Z) for d in range(1, self.Z)]

    def dev(self, z=None, y=None, x=None, c=None):
        z = self.z if z is None else z
        y = self.y if y is None else y
        x = self.x if x is None else x
        c = self.c if c is None else c
        return (z * self.Y + y, x * 2 + c)

    def greet(self, devices):
        barrier = pltpu.get_barrier_semaphore()
        for device in devices:
            pl.semaphore_signal(barrier, inc=1, device_id=device, device_id_type=MESH)
        pl.semaphore_wait(barrier, len(devices))

    def plane(self):
        return [(x, y) for x in [self.x] + self.xs for y in [self.y] + self.ys][1:]


class Sends:
    def __init__(self, sems):
        self.sems, self.count, self.made = sems, 0, []

    def push(self, src, dst, recv, device, like, cond=None, given=None):
        copy = pltpu.make_async_remote_copy(
            src_ref=src, dst_ref=dst, send_sem=self.sems.at[self.count], recv_sem=recv,
            device_id=device, device_id_type=MESH,
        )
        if cond is None:
            copy.start()
        else:
            pl.when(cond())(lambda: copy.start())
        self.made.append((self.count, like, cond or given))
        self.count += 1

    def drain(self, place):
        for k, like, cond in self.made:
            sent = pltpu.make_async_remote_copy(
                src_ref=like(), dst_ref=like(), send_sem=self.sems.at[k], recv_sem=self.sems.at[k],
                device_id=place.dev(), device_id_type=MESH,
            )
            if cond is None:
                sent.wait_send()
            else:
                pl.when(cond())(lambda sent=sent: sent.wait_send())


def arrived(place, ref, recv, send):
    pltpu.make_async_remote_copy(
        src_ref=ref, dst_ref=ref, send_sem=send, recv_sem=recv, device_id=place.dev(), device_id_type=MESH
    ).wait_recv()


def bits(n):
    return [1 << k for k in range(n.bit_length() - 1)]


def norm_forward(u, gain, bias):
    centred = u - jnp.mean(u, axis=-1, keepdims=True)
    recip = lax.rsqrt(jnp.mean(centred * centred, axis=-1, keepdims=True) + NORM_EPSILON)
    normed = centred * recip
    return normed * gain + bias, normed, recip


def norm_back(grad, normed, recip, gain):
    e = grad * gain
    slope = jnp.mean(e * normed, axis=-1, keepdims=True)
    return recip * (e - jnp.mean(e, axis=-1, keepdims=True) - normed * slope)


def adam_update(param, grad, first, second, rate, decay):
    first_new = BETA_FIRST * first + (1.0 - BETA_FIRST) * grad
    second_new = BETA_SECOND * second + (1.0 - BETA_SECOND) * grad * grad
    first_hat = first_new * (1.0 / (1.0 - BETA_FIRST**STEP))
    second_hat = second_new * (1.0 / (1.0 - BETA_SECOND**STEP))
    param_new = param - rate * (first_hat / (jnp.sqrt(second_hat) + ADAM_EPSILON) + decay * param)
    return first_new, second_new, param_new


class Piece:
    def __init__(self, place, source, x_first, bufs, recv, sends):
        self.place, self.source, self.x_first, self.sends = place, source, x_first, sends
        self.s1 = source.at[place.c]
        self.r1, self.r2, self.s2, self.r3, self.s3, self.r4, self.final = bufs
        self.recv = recv

    def axis(self, x):
        p = self.place
        return (p.X, p.x, lambda v: p.dev(x=v)) if x else (p.Y, p.y, lambda v: p.dev(y=v))

    def send(self, axis, cut, buf, base):
        size, me, dev = axis
        for d in range(1, size):
            to = lax.rem(me + d, size)
            self.sends.push(cut(to), buf.at[d - 1], self.recv.at[base + d], dev(to), lambda: buf.at[0])

    def add(self, axis, own, buf, base):
        total = own.astype(F32)
        for d in range(1, axis[0]):
            arrived(self.place, buf.at[d - 1], self.recv.at[base + d], self.sends.sems.at[0])
            total = total + buf[d - 1].astype(F32)
        return total

    def hop0(self):
        p = self.place
        self.sends.push(self.source.at[1 - p.c], self.r1, self.recv.at[0], p.dev(c=1 - p.c), lambda: self.r1)

    def hop1(self):
        p = self.place
        arrived(p, self.r1, self.recv.at[0], self.sends.sems.at[0])
        self.s1[...] = (self.s1[...].astype(F32) + self.r1[...].astype(F32)).astype(BF)
        cut = lambda to: self.s1.at[to] if self.x_first else self.s1.at[:, :, to]
        self.send(self.axis(self.x_first), cut, self.r2, 0)

    def hop2(self):
        p = self.place
        own = self.s1[p.x] if self.x_first else self.s1[:, :, p.y]
        self.s2[...] = self.add(self.axis(self.x_first), own, self.r2, 0).astype(BF)
        cut = lambda to: self.s2.at[:, to] if self.x_first else self.s2.at[to]
        self.send(self.axis(not self.x_first), cut, self.r3, p.X)

    def hop3(self):
        p = self.place
        own = self.s2[:, p.y] if self.x_first else self.s2[p.x]
        self.s3[...] = self.add(self.axis(not self.x_first), own, self.r3, p.X).astype(BF)
        self.send((p.Z, p.z, lambda v: p.dev(z=v)), lambda to: self.s3.at[to], self.r4, 2 * p.X)

    def hop4(self):
        p = self.place
        self.final[...] = self.add((p.Z, p.z, None), self.s3[p.z], self.r4, 2 * p.X)


class Chunk:
    def __init__(self, place, g, dx, cc, source, bufs, recv, sends):
        self.place, self.dx, self.cc, self.sends = place, dx, cc, sends
        r1, rx, r2 = bufs
        self.source, self.r1, self.rx, self.r2 = source.at[g], r1.at[g, dx], rx.at[g], r2.at[g]
        self.recv = recv.at[g]

    def mine(self):
        return self.place.c == self.cc

    def hop0(self):
        p = self.place
        x = lax.rem(p.x + self.dx, p.X)
        self.sends.push(
            self.source.at[self.cc, x], self.r1, self.recv.at[self.dx], p.dev(c=self.cc), lambda: self.r1,
            lambda: self.place.c != self.cc,
        )

    def hop1(self):
        pl.when(self.mine())(self.pass_on)

    def pass_on(self):
        p = self.place
        x = lax.rem(p.x + self.dx, p.X)
        arrived(p, self.r1, self.recv.at[self.dx], self.sends.sems.at[0])
        total = self.source[self.cc, x].astype(F32) + self.r1[...].astype(F32)
        if self.dx:
            self.source[self.cc, x] = total.astype(BF)
            self.sends.push(
                self.source.at[self.cc, x], self.rx.at[self.dx - 1], self.recv.at[p.X + self.dx], p.dev(x=x),
                lambda: self.r1, given=self.mine,
            )
            return
        for d in range(1, p.X):
            arrived(p, self.rx.at[d - 1], self.recv.at[p.X + d], self.sends.sems.at[0])
            total = total + self.rx[d - 1].astype(F32)
        self.source[self.cc, x] = total.astype(BF)
        for d in range(1, p.batches):
            j = lax.rem(p.j + d, p.batches)
            self.sends.push(
                self.source.at[self.cc, x, j], self.r2.at[d - 1], self.recv.at[2 * p.X + d], (j, p.x * 2 + p.c),
                lambda: self.r2.at[0], given=self.mine,
            )


def collect(place, source, r2, recv, dummy):
    total = source[place.c, place.x, place.j].astype(F32)
    for d in range(1, place.batches):
        arrived(place, r2.at[d - 1], recv.at[2 * place.X + d], dummy)
        total = total + r2[d - 1].astype(F32)
    return total


def forward_sends(X, Y, Z, groups):
    part_a = groups * (Z - 1 + Z * (Y - 1)) + (X - 1) * (1 + Z - 1 + Y - 1) + X
    part_b = (X - 1) + (Y - 1) + (Z - 1) + 1 + (Z - 1) * (X + Y - 1)
    part_b += Z * (2 * (X - 1) * (Y - 1) + (X - 1) + (Y - 1) + (X - 1) * (Y - 1))
    return part_a + part_b


def backward_sends(X, Y, Z, groups):
    stages = 1 + sum(len(bits(v)) for v in (X, Y, Z))
    return 2 * groups * (X + Y + Z - 2) + groups * 2 * (X + X - 1 + Y * Z - 1) + stages


def layer_kernel(
    batches, heads, owner_ref, lengths_ref, gain_ref, bias_ref, post_in, weight_in, dual_in, pc_in, dc_in,
    post_out, dual_out, dpost_out, grad_ref, norm_out, p_hbm,
    post_ref, weight_ref, dual_ref, pc_ref, dc_ref, dmid_ref, dpre_ref, recip_ref, pick_ref, xs_ref, xst_ref, ga_ref, gb_ref, qk_ref, vx_ref, wide_ref, linv_ref, at_ref, dat_ref,
    w12_ref, wo_ref, mbt_ref, dft_ref, dbt_ref, dwo_ref, dqkv_ref,
    r1, xr2, yr2, xs2, ys2, r3, s3, r4, final, qr1, qrx, qr2, norm_send, norm_recv,
    recv_z, recv_y, recv_x, core_a, recv_b, send_f, recv_f, recv_q, norm_sems, send_r, p_sems, in_sems, out_sems,
):
    place = Place(batches, heads)
    groups, rows = NHEADS // heads, D // batches
    parts = 2 * groups
    X, Y, Z = place.X, place.Y, place.Z
    c, x, y, z = place.c, place.x, place.y, place.z
    sends = Sends(send_f)
    dummy = send_f.at[0]
    length = lengths_ref[lax.axis_index("head")]
    ins = ((weight_in, weight_ref), (post_in, post_ref), (pc_in, pc_ref), (dc_in, dc_ref), (dual_in, dual_ref))

    def load(k):
        return pltpu.make_async_copy(*ins[k], in_sems.at[k])

    def core_push_a(xx):
        ref = ga_ref.at[c, xx]
        sends.push(ref, ref, core_a.at[xx], place.dev(c=1 - c), lambda: ga_ref.at[0, 0])

    def got_b(cc, xx, zz, yy):
        arrived(place, gb_ref.at[:, cc, xx, zz, yy], recv_b.at[cc, xx, zz, yy], dummy)

    def push_b(xx, zz, yy, device, cond=None):
        ref = gb_ref.at[:, c, xx, zz, yy]
        sends.push(ref, ref, recv_b.at[c, xx, zz, yy], device, lambda: gb_ref.at[:, 0, 0, 0, 0], cond)

    def side(offset):
        zo = lax.rem(z + offset, Z)
        low = lambda: lax.rem(place.z + offset, Z) < (3 * Z) // 4
        for xx in place.xs:
            got_b(c, xx, zo, y)
            for yy in place.ys:
                push_b(xx, zo, y, place.dev(y=yy), low)
            push_b(xx, zo, y, place.dev(c=1 - c))
        for yy in place.ys:
            got_b(c, x, zo, yy)
            for xx in place.xs:
                push_b(x, zo, yy, place.dev(x=xx), lambda: jnp.logical_not(low()))
            push_b(x, zo, yy, place.dev(c=1 - c))

    def spread(act, offset):
        for d in [d for d in range(Z) if d == offset or (offset == Z - 1 and d >= offset) or (offset == 1 and 0)]:
            zz = lax.rem(z + d, Z)
            if act == "send":
                push_b(x, z, y, place.dev(z=zz))
            elif act == "side":
                side(d)
            else:
                got_b(c, x, zz, y)
                for xx in place.xs:
                    push_b(x, zz, y, place.dev(x=xx))
                for yy in place.ys:
                    push_b(x, zz, y, place.dev(y=yy))
                push_b(x, zz, y, place.dev(c=1 - c))

    for n in range(len(ins)):
        load(n).start()
    load(0).wait()
    weight = weight_ref[...]
    for g in range(groups):
        ga_ref[c, x, z, y, g] = weight[:, g * GROUPW : g * GROUPW + PART].astype(BF)
    peers = [place.dev(z=zz, y=yy) for zz in [z] + place.zs for yy in [y] + place.ys][1:]
    place.greet(peers + [place.dev(x=xx) for xx in place.xs] + [place.dev(c=1 - c)])
    for g in range(groups):
        own = ga_ref.at[c, x, z, y, g]
        for zz in place.zs:
            sends.push(own, own, recv_z.at[g, z], place.dev(z=zz), lambda: ga_ref.at[0, 0, 0, 0, 0])
        for yy in place.ys:
            sends.push(own, own, recv_y.at[g, z, y], place.dev(y=yy), lambda: ga_ref.at[0, 0, 0, 0, 0])
    own = ga_ref.at[c, x, z, y]
    for xx in place.xs:
        sends.push(own, own, recv_x.at[x, z], place.dev(x=xx), lambda: ga_ref.at[0, 0, 0, 0])
    for k in range(parts):
        low = (k % groups) * GROUPW + (2 - k // groups) * PART
        gb_ref[k, c, x, z, y] = weight[:, low : low + PART].astype(BF)
    for act, offset in B_PLAN["first"]:
        spread(act, offset)
    for yy in place.ys:
        push_b(x, z, y, place.dev(y=yy))
    for xx in place.xs:
        push_b(x, z, y, place.dev(x=xx))
    load(1).wait()
    lane = lax.broadcasted_iota(jnp.int32, (1, D), 1)
    source = lane % rows
    for b in range(batches):
        source = jnp.where(lane // rows == b, source + owner_ref[b] * rows, source)
    pick = (lax.broadcasted_iota(jnp.int32, (D, D), 0) == source).astype(F32).astype(BF)
    pick_ref[...] = pick
    ordered = dot(post_ref[...], pick, 1, 0).astype(BF)
    xs_ref[...] = ordered
    xst_ref[...] = ordered.T
    for g in range(groups):
        for zz in place.zs:
            block = ga_ref.at[c, x, zz, y, g]
            arrived(place, block, recv_z.at[g, zz], dummy)
            for yy in place.ys:
                sends.push(block, block, recv_y.at[g, zz, y], place.dev(y=yy), lambda: ga_ref.at[0, 0, 0, 0, 0])
    for act, offset in B_PLAN["after"]:
        spread(act, offset)
    for xx in place.xs:
        for zz in place.zs:
            block = ga_ref.at[c, x, zz, y]
            sends.push(block, block, recv_x.at[x, zz], place.dev(x=xx), lambda: ga_ref.at[0, 0, 0, 0])
    push_b(x, z, y, place.dev(c=1 - c))


    def forward_transfers(t):
        if t < groups:
            for zz in range(Z):
                for yy in place.ys:
                    arrived(place, ga_ref.at[c, x, zz, yy, t], recv_y.at[t, zz, yy], dummy)
        if t == groups - 1:
            for yy in place.ys:
                column = ga_ref.at[c, x, :, yy]
                for xx in place.xs:
                    sends.push(column, column, recv_x.at[x, Z + yy], place.dev(x=xx), lambda: ga_ref.at[0, 0, :, 0])
            core_push_a(x)
        if t and t % groups == 0:
            k = t // groups
            xx = lax.rem(x + k // 2, X)
            if k % 2 == 0:
                for zz in [z] + place.zs:
                    arrived(place, ga_ref.at[c, xx, zz, y], recv_x.at[xx, zz], dummy)
                for yy in place.ys:
                    arrived(place, ga_ref.at[c, xx, :, yy], recv_x.at[xx, Z + yy], dummy)
                core_push_a(xx)
            else:
                arrived(place, ga_ref.at[1 - c, xx], core_a.at[xx], dummy)
        for act, offset in B_PLAN[t]:
            spread(act, offset)

    def p_store(i):
        slot = lax.rem(i, 4)
        return pltpu.make_async_copy(wide_ref.at[pl.ds(2 * slot, 2)], p_hbm.at[i], p_sems.at[slot])

    def p_fetch(i):
        g, r = i // heads, i % heads
        dx, cc = X - 1 - r // 2, r % 2
        spot = (2 * dx + (cc + c) % 2) * groups + g
        slot = lax.rem(i, 2)
        return pltpu.make_async_copy(p_hbm.at[spot], wide_ref.at[pl.ds(2 * slot, 2)], p_sems.at[slot])

    @pl.loop(0, NHEADS)
    def _(step):
        for t in range(NHEADS):
            pl.when(step == t)(functools.partial(forward_transfers, t))

        @pl.when(step >= 4)
        def _():
            p_store(step - 4).wait()

        q, g = step // groups, step % groups
        cc, xx = (c + q) % 2, lax.rem(x + q // 2, X)
        head = (xx * 2 + cc) * groups + g
        w = ga_ref[cc, xx, :, :, g].reshape(D, PART)
        proj = dot(xs_ref[...], w, 1, 0)
        lane = lax.broadcasted_iota(jnp.int32, (SEQ_LEN, 128), 1)
        qk = proj[:, :128].astype(BF)
        qk = jnp.where(lane < DH, qk * BF(DH**-0.5), qk)
        v = proj[:, 128:].astype(BF)
        vx = jnp.where(lane < DH, v, jnp.where(lane < DH + 2, BF(1), BF(0)))
        qk_ref[head] = qk
        vx_ref[head] = vx
        q_only = jnp.where(lane < DH, qk, BF(0))
        kq = jnp.concatenate([qk[:, DH:], qk[:, :DH]], axis=1)
        vxt = vx.T[: DH + 8]
        keep = lax.broadcasted_iota(jnp.int32, (SEQ_LEN, 1), 0) < length
        s = dot(kq, q_only, 1, 1)
        s = jnp.where(keep, s, F32(MASK_VALUE))
        m = jnp.max(s, axis=0, keepdims=True)
        p = jnp.exp(s - m).astype(BF)
        slot = lax.rem(step, 4)
        wide_ref[2 * slot] = p[:, : SEQ_LEN // 2]
        wide_ref[2 * slot + 1] = p[:, SEQ_LEN // 2 :]
        o = dot(vxt, p, 1, 0)
        r = 1.0 / o[DH : DH + 1]
        linv_ref[head] = r
        at_ref[head] = (o[:DH] * r).astype(BF)
        p_store(step).start()

    reduce_sends = Sends(send_r)
    pieces = []
    for k in range(parts):
        x_first = k in X_FIRST
        bufs = (r1.at[k], xr2.at[k], xs2.at[k]) if x_first else (r1.at[k], yr2.at[k], ys2.at[k])
        bufs += tuple(b.at[k] for b in (r3, s3, r4, final))
        pieces.append(Piece(place, gb_ref.at[k], x_first, bufs, recv_f.at[k], reduce_sends))
    chunks = [
        Chunk(place, g, dx, cc, dqkv_ref, (qr1, qrx, qr2), recv_q, reduce_sends)
        for g in range(groups)
        for dx in reversed(range(X))
        for cc in range(2)
    ]
    partners = [place.dev(c=1 - c)]
    flip = lambda v, b: v + b - 2 * b * ((v // b) % 2)
    partners += [place.dev(x=flip(x, b)) for b in bits(X)]
    partners += [place.dev(y=flip(y, b)) for b in bits(Y)]
    partners += [place.dev(z=flip(z, b)) for b in bits(Z)]

    def norm_push(k):
        reduce_sends.push(norm_send.at[k], norm_recv.at[k], norm_sems.at[k], partners[k], lambda: norm_send.at[0])

    def norm_pull(k):
        arrived(place, norm_recv.at[k], norm_sems.at[k], send_r.at[0])
        norm_send[k + 1] = norm_send[k] + norm_recv[k]

    for i in range(NHEADS - 4, NHEADS):
        p_store(i).wait()
    for n in range(2, len(ins)):
        load(n).wait()
    held = []
    for b in range(batches):
        found = 0
        for j in range(1, batches):
            found = jnp.where(owner_ref[j] == b, j, found)
        held.append(found)
    for b in range(batches):
        there = slice(b * rows, (b + 1) * rows)
        for h in range(NHEADS):
            g, xx, cc = h % groups, (h // groups) // 2, (h // groups) % 2
            wo_ref[there, h * DH : (h + 1) * DH] = ga_ref[cc, xx, held[b] // Y, held[b] % Y, g][:, 3 * DH :]
    norm_send[0] = jnp.zeros((4, D), F32)

    block = SEQ_LEN // MID_STEPS
    outs = ((pc_ref, post_out), (dual_ref, dual_out))

    def store(n, t):
        here = pl.ds(pl.multiple_of(t * block, block), block)
        return pltpu.make_async_copy(outs[n][0].at[here], outs[n][1].at[here], out_sems.at[n, t])

    def block_of(t):
        return pl.ds(pl.multiple_of(t * block, block), block)

    def kept(t):
        return t * block + lax.broadcasted_iota(jnp.int32, (block, 1), 0) < length

    gain, bias = gain_ref[...], bias_ref[...]
    zero = jnp.zeros((1, D), F32)

    def over_tokens(value):
        return jnp.sum(value, axis=0, keepdims=True)

    @pl.loop(0, MID_STEPS, unroll=UNROLL)
    def _(t):
        here = block_of(t)
        branch = dot(at_ref[:, :, here].reshape(D, block), wo_ref[...], 0, 1)
        middle, n1, recip = norm_forward(post_ref[here, :].astype(F32) + branch, gain[0:1], bias[0:1])
        dual_ref[here, :] = dual_ref[here, :] + branch
        dmid_ref[here, :] = n1
        recip_ref[here, :] = recip
        middle_low = middle.astype(BF)
        post_ref[here, :] = middle_low
        mbt_ref[:, here] = dot(pick_ref[...], middle_low, 0, 1).astype(BF)

    for offset in range(Z):
        zz = lax.rem(z + offset, Z)
        for yy in place.ys:
            for xx in place.xs:
                got_b(c, xx, zz, yy)
                push_b(xx, zz, yy, place.dev(c=1 - c))
    for xx in range(X):
        for zz in range(Z):
            for yy in range(Y):
                got_b(1 - c, xx, zz, yy)
    for b in range(batches):
        there = slice(b * rows, (b + 1) * rows)
        for h in range(NHEADS):
            g, xx, cc = h % groups, (h // groups) // 2, (h // groups) % 2
            for k in range(2):
                w12_ref[1 - k, there, h * PART : (h + 1) * PART] = gb_ref[
                    k * groups + g, cc, xx, held[b] // Y, held[b] % Y
                ]

    @pl.loop(0, MID_STEPS, unroll=UNROLL)
    def _(t):
        here = block_of(t)
        pre = dot(post_ref[here, :], w12_ref[0], 1, 0)
        cdf = 0.5 + 0.5 * lax.erf(pre * F32(math.sqrt(0.5)))
        density = jnp.exp(pre * pre * F32(-0.5)) * F32(1.0 / math.sqrt(2.0 * math.pi))
        hidden = (pre * cdf).astype(BF)
        slope = (cdf + pre * density).astype(BF)
        for k in range(4):
            wide_ref[k, here, :] = hidden[:, k * 512 : (k + 1) * 512]
            wide_ref[4 + k, here, :] = slope[:, k * 512 : (k + 1) * 512]

    @pl.loop(0, MID_STEPS, unroll=UNROLL)
    def _(t):
        here = block_of(t)
        hidden = jnp.concatenate([wide_ref[k, here, :] for k in range(4)], axis=1)
        feed = dot(hidden, w12_ref[1], 1, 1)
        out, n2, recip = norm_forward(dmid_ref[here, :] * gain[0:1] + bias[0:1] + feed, gain[1:2], bias[1:2])
        dual_ref[here, :] = dual_ref[here, :] + feed
        d_out = jnp.where(kept(t), pc_ref[here, :].astype(F32), 0.0)
        d_dual = jnp.where(kept(t), dc_ref[here, :].astype(F32), 0.0)
        pc_ref[here, :] = out.astype(BF)
        store(0, t).start()
        store(1, t).start()
        d_pre = norm_back(d_out, n2, recip, gain[1:2])
        dpre_ref[here, :] = d_pre
        d_feed = (d_pre + d_dual).astype(BF)
        post_ref[here, :] = d_feed
        dft_ref[:, here] = dot(pick_ref[...], d_feed, 0, 1).astype(BF)
        norm_send[0] = norm_send[0] + jnp.concatenate([zero, over_tokens(d_out * n2), zero, over_tokens(d_out)], axis=0)

    def weight_piece(k):
        left = (dft_ref if k < groups else mbt_ref)[...]
        for device in range(heads):
            h = device * groups + k % groups
            held = wide_ref[4 * (k // groups) + h // 2, :, (h % 2) * PART : (h % 2 + 1) * PART]
            grad = dot(left, held, 1, 0).astype(BF)
            gb_ref[k, device % 2, device // 2] = grad.reshape(Z, Y, rows, PART)
        pieces[k].hop0()

    sends.drain(place)
    for k in range(groups):
        weight_piece(k)
    p_fetch(0).start()
    p_fetch(1).start()

    @pl.loop(0, MID_STEPS, unroll=UNROLL)
    def _(t):
        here = block_of(t)
        d_hidden = dot(post_ref[here, :], w12_ref[1], 1, 0)
        slope = jnp.concatenate([wide_ref[4 + k, here, :] for k in range(4)], axis=1)
        d_hidden_pre = (d_hidden * slope.astype(F32)).astype(BF)
        for k in range(4):
            wide_ref[4 + k, here, :] = d_hidden_pre[:, k * 512 : (k + 1) * 512]
        d_middle = dpre_ref[here, :] + dot(d_hidden_pre, w12_ref[0], 1, 1)
        n1 = dmid_ref[here, :]
        d_mid = norm_back(d_middle, n1, recip_ref[here, :], gain[0:1])
        dmid_ref[here, :] = d_mid
        d_branch = (d_mid + jnp.where(kept(t), dc_ref[here, :].astype(F32), 0.0)).astype(BF)
        dbt_ref[:, here] = dot(pick_ref[...], d_branch, 0, 1).astype(BF)
        dat_ref[:, :, here] = dot(wo_ref[...], d_branch, 0, 1).astype(BF).reshape(NHEADS, DH, block)
        norm_send[0] = norm_send[0] + jnp.concatenate(
            [over_tokens(d_middle * n1), zero, over_tokens(d_middle), zero], axis=0
        )
        for k in range(groups):
            pl.when(t == k)(pieces[k].hop1)

    norm_push(0)
    for k in range(groups, parts):
        weight_piece(k)
    dwo = dot(dbt_ref[...], at_ref[...].reshape(D, SEQ_LEN), 1, 1).astype(BF)
    empty = jnp.zeros((D, DH), BF)
    for h in range(NHEADS):
        dwo_ref[h] = jnp.concatenate([empty, dwo[:, h * DH : (h + 1) * DH]], axis=1)

    half = parts // 2
    todo = [[] for _ in range(NHEADS)]
    for n, chunk in enumerate(chunks):
        todo[n].append(chunk.hop0)
        if n + 1 < len(chunks):
            todo[n + 1].append(chunk.hop1)
    early, late = pieces[:half], pieces[half:]
    todo[0] += [p.hop1 for p in late] + [lambda: norm_pull(0), lambda: norm_push(1)]
    todo[0] += [p.hop2 for p in early]
    todo[2] += [lambda: norm_pull(1), lambda: norm_push(2)]
    todo[2] += [p.hop3 for p in early]
    todo[3] += [p.hop2 for p in late]
    todo[4] += [p.hop4 for p in early] + [lambda: norm_pull(2), lambda: norm_push(3)]
    todo[5] += [p.hop3 for p in late]
    todo[6] += [lambda: norm_pull(3), lambda: norm_push(4)]

    def backward_transfers(t):
        for act in todo[t]:
            act()

    @pl.loop(0, NHEADS)
    def _(i):
        p_fetch(i).wait()
        g, r = i // heads, i % heads
        cc, xx = r % 2, lax.rem(x + X - 1 - r // 2, X)
        head = (xx * 2 + cc) * groups + g
        lane = lax.broadcasted_iota(jnp.int32, (SEQ_LEN, 128), 1)
        row = lax.broadcasted_iota(jnp.int32, (DH, SEQ_LEN), 0)
        qk, vx = qk_ref[head], vx_ref[head]
        do = dat_ref[head].astype(F32) * linv_ref[head]
        inner = -jnp.sum(do * at_ref[head].astype(F32), axis=0, keepdims=True)
        coarse = inner.astype(BF).astype(F32)
        tail = jnp.where(row == 0, coarse, jnp.where(row == 1, inner - coarse, 0.0))
        et = jnp.concatenate([do, tail], axis=0).astype(BF)
        e = et.T
        kt = qk.T[DH:]
        kq = jnp.concatenate([qk[:, DH:], qk[:, :DH]], axis=1)
        dk = jnp.zeros((SEQ_LEN, 128), F32)
        dv = jnp.zeros((SEQ_LEN, 128), F32)
        dqs = []
        slot = lax.rem(i, 2)
        for b in range(2):
            sl = slice(b * (SEQ_LEN // 2), (b + 1) * (SEQ_LEN // 2))
            p = wide_ref[2 * slot + b]
            ds = (p.astype(F32) * dot(vx, et[:, sl], 1, 0)).astype(BF)
            dv = dv + dot(p, e[sl], 1, 0)
            dk = dk + dot(ds, kq[sl], 1, 0)
            dqs.append(dot(kt, ds, 1, 0))
        dqt = jnp.concatenate(dqs, axis=1) * F32(DH**-0.5)
        dq = jnp.concatenate([dqt, jnp.zeros_like(dqt)], axis=0).T
        d_proj = jnp.concatenate([jnp.where(lane < DH, dq, dk), jnp.where(lane < DH, dv, 0.0)], axis=1).astype(BF)
        cols = pl.ds(pl.multiple_of(head * PART, PART), PART)
        w12_ref[0, :, cols] = d_proj[: SEQ_LEN // 2]
        w12_ref[1, :, cols] = d_proj[SEQ_LEN // 2 :]
        dw = dot(xst_ref[...], d_proj, 1, 0)
        dw = jnp.concatenate([dw[:, :128], dw[:, 128:] + dwo_ref[head].astype(F32)], axis=1).astype(BF)
        dqkv_ref[g, cc, xx] = dw.reshape(dqkv_ref.shape[3:])

        @pl.when(i + 2 < NHEADS)
        def _():
            p_fetch(i + 2).start()

        for t in range(NHEADS):
            pl.when(i == t)(functools.partial(backward_transfers, t))

    for k in range(4, len(partners)):
        norm_pull(k)
        if k + 1 < len(partners):
            norm_push(k + 1)
    norm_out[...] = norm_send[len(partners)]
    chunks[-1].hop1()
    table = []
    for h in range(NHEADS):
        g, xx, cc = h % groups, (h // groups) // 2, (h // groups) % 2
        table.append(ga_ref[cc, xx, :, :, g].reshape(D, PART))
    table = jnp.concatenate(table, axis=1)
    dpost = []
    for k in range(2):
        here = slice(k * (SEQ_LEN // 2), (k + 1) * (SEQ_LEN // 2))
        ordered = dot(w12_ref[k], table, 1, 1).astype(BF)
        dmid_ref[here, :] = dmid_ref[here, :] + dot(ordered, pick_ref[...], 1, 1)
        dpost.append(pltpu.make_async_copy(dmid_ref.at[here], dpost_out.at[here], in_sems.at[k]))
        dpost[k].start()
    for piece in pieces[len(pieces) // 2 :]:
        piece.hop4()
    for g in range(groups):
        low = g * GROUPW
        grad_ref[:, low + PART : low + 2 * PART] = final[groups + g]
        grad_ref[:, low + 2 * PART : low + 3 * PART] = final[g]
        grad_ref[:, low : low + PART] = collect(place, dqkv_ref.at[g], qr2.at[g], recv_q.at[g], send_r.at[0])
    for copy in dpost:
        copy.wait()
    for n in range(len(outs)):
        for t in range(MID_STEPS):
            store(n, t).wait()
    reduce_sends.drain(place)


def layer_call(owner, lengths, gain, bias, post, weights, dual, pc, dc, batches, heads):
    groups, rows = NHEADS // heads, D // batches
    parts = 2 * groups
    X = Y = heads // 2
    Z = batches // Y
    tokens = post.shape[0]
    assert tokens == SEQ_LEN
    stages = 1 + sum(len(bits(v)) for v in (X, Y, Z))
    smem, vmem = pl.BlockSpec(memory_space=pltpu.SMEM), pl.BlockSpec(memory_space=pltpu.VMEM)
    far = pl.BlockSpec(memory_space=pl.ANY)
    outs = [
        jax.ShapeDtypeStruct((tokens, D), BF),
        jax.ShapeDtypeStruct((tokens, D), F32),
        jax.ShapeDtypeStruct((tokens, D), F32),
        jax.ShapeDtypeStruct((rows, groups * GROUPW), F32),
        jax.ShapeDtypeStruct((4, D), F32),
        jax.ShapeDtypeStruct((NHEADS, 2, tokens, tokens // 2), BF),
    ]
    dma = pltpu.SemaphoreType.DMA
    return pl.pallas_call(
        functools.partial(layer_kernel, batches, heads),
        in_specs=[smem, smem, vmem, vmem] + [far] * 5,
        out_specs=[far, far, far, vmem, vmem, far],
        out_shape=outs,
        scratch_shapes=[
            pltpu.VMEM((tokens, D), BF),
            pltpu.VMEM(weights.shape, F32),
            pltpu.VMEM((tokens, D), F32),
            pltpu.VMEM((tokens, D), BF),
            pltpu.VMEM((tokens, D), BF),
            pltpu.VMEM((tokens, D), F32),
            pltpu.VMEM((tokens, D), F32),
            pltpu.VMEM((tokens, 1), F32),
            pltpu.VMEM((D, D), BF),
            pltpu.VMEM((tokens, D), BF),
            pltpu.VMEM((D, tokens), BF),
            pltpu.VMEM((2, X, Z, Y, groups, rows, PART), BF),
            pltpu.VMEM((parts, 2, X, Z, Y, rows, PART), BF),
            pltpu.VMEM((NHEADS, tokens, 128), BF),
            pltpu.VMEM((NHEADS, tokens, 128), BF),
            pltpu.VMEM((8, tokens, tokens // 2), BF),
            pltpu.VMEM((NHEADS, 1, tokens), F32),
            pltpu.VMEM((NHEADS, DH, tokens), BF),
            pltpu.VMEM((NHEADS, DH, tokens), BF),
            pltpu.VMEM((2, D, FF), BF),
            pltpu.VMEM((D, D), BF),
            pltpu.VMEM((D, tokens), BF),
            pltpu.VMEM((D, tokens), BF),
            pltpu.VMEM((D, tokens), BF),
            pltpu.VMEM((NHEADS, D, 128), BF),
            pltpu.VMEM((groups, 2, X, batches, rows, PART), BF),
            pltpu.VMEM((parts, X, Z, Y, rows, PART), BF),
            pltpu.VMEM((parts, X - 1, Z, Y, rows, PART), BF),
            pltpu.VMEM((parts, Y - 1, X, Z, rows, PART), BF),
            pltpu.VMEM((parts, Z, Y, rows, PART), BF),
            pltpu.VMEM((parts, X, Z, rows, PART), BF),
            pltpu.VMEM((parts, X - 1, Z, rows, PART), BF),
            pltpu.VMEM((parts, Z, rows, PART), BF),
            pltpu.VMEM((parts, Z - 1, rows, PART), BF),
            pltpu.VMEM((parts, rows, PART), F32),
            pltpu.VMEM((groups, X, batches, rows, PART), BF),
            pltpu.VMEM((groups, X - 1, batches, rows, PART), BF),
            pltpu.VMEM((groups, batches - 1, rows, PART), BF),
            pltpu.VMEM((stages + 1, 4, D), F32),
            pltpu.VMEM((stages, 4, D), F32),
            dma((groups, Z)),
            dma((groups, Z, Y)),
            dma((X, Z + Y)),
            dma((X,)),
            dma((2, X, Z, Y)),
            dma((forward_sends(X, Y, Z, groups),)),
            dma((parts, 2 * X + Z)),
            dma((groups, 2 * X + batches)),
            dma((stages,)),
            dma((backward_sends(X, Y, Z, groups),)),
            dma((4,)),
            dma((5,)),
            dma((2, MID_STEPS)),
        ],
        name="layer",
        compiler_params=pltpu.CompilerParams(
            collective_id=1, has_side_effects=True, vmem_limit_bytes=VMEM_BYTES
        ),
    )(owner, lengths, gain, bias, post, weights, dual, pc, dc)


def update_kernel(
    post_in, dual_in, dpost_in, grad_ref, weight_ref, first_ref, second_ref,
    ngrad_ref, gain_ref, bias_ref, nfirst_ref, nsecond_ref,
    post_out, dual_out, dpost_out, first_out, second_out, weight_out, nfirst_out, nsecond_out, nparam_out,
):
    post_out[...] = post_in[...]
    dual_out[...] = dual_in[...]
    dpost_out[...] = dpost_in[...]
    first_out[...], second_out[...], weight_out[...] = adam_update(
        weight_ref[...], grad_ref[...], first_ref[...], second_ref[...], WEIGHT_RATE, WEIGHT_DECAY
    )
    nparam = jnp.concatenate([gain_ref[...], bias_ref[...]], axis=0)
    nfirst_out[...], nsecond_out[...], nparam_out[...] = adam_update(
        nparam, ngrad_ref[...], nfirst_ref[...], nsecond_ref[...], NORM_RATE, 0.0
    )


def update_call(post, dual, dpost, grad, weights, first, second, ngrad, gain, bias, nfirst, nsecond):
    steps = 2
    cut = lambda a: pl.BlockSpec((a.shape[0] // steps, a.shape[1]), lambda i: (i, 0))
    same = lambda a: pl.BlockSpec(a.shape, lambda i: (0, 0))
    outs = [post, dual, dpost, weights, weights, weights, nfirst, nfirst, nfirst]
    return pl.pallas_call(
        update_kernel,
        grid=(steps,),
        in_specs=[cut(a) for a in (post, dual, dpost, grad, weights, first, second)]
        + [same(a) for a in (ngrad, gain, bias, nfirst, nsecond)],
        out_specs=[cut(a) for a in outs[:6]] + [same(a) for a in outs[6:]],
        out_shape=[jax.ShapeDtypeStruct(a.shape, a.dtype) for a in outs],
        name="update",
        compiler_params=pltpu.CompilerParams(vmem_limit_bytes=VMEM_BYTES),
    )(post, dual, dpost, grad, weights, first, second, ngrad, gain, bias, nfirst, nsecond)


def shards(
    post_stream,
    dual_stream,
    post_cotangent,
    dual_cotangent,
    seq_lengths,
    owner_slots,
    weights,
    first_moment,
    second_moment,
    norm_gain,
    norm_bias,
    norm_first,
    norm_second,
):
    batches, heads = lax.axis_size("batch"), lax.axis_size("head")
    post, dual, dpost, grad, norm_grad, _ = layer_call(
        owner_slots, seq_lengths, norm_gain, norm_bias, post_stream, weights, dual_stream, post_cotangent,
        dual_cotangent, batches, heads,
    )
    return update_call(
        post, dual, dpost, grad, weights, first_moment, second_moment,
        norm_grad, norm_gain, norm_bias, norm_first, norm_second,
    )


def solution(mesh):
    tokens, table, copied = P(("batch", "head"), None), P("batch", "head"), P()
    in_specs = (tokens,) * 4 + (P("batch"), copied) + (table,) * 3 + (copied,) * 4
    out_specs = (tokens,) * 3 + (table,) * 3 + (copied,) * 3
    return jax.shard_map(shards, mesh=mesh, in_specs=in_specs, out_specs=out_specs, check_vma=False)
```

```python
import functools
import math

import jax
import jax.numpy as jnp
from jax import lax
from jax.experimental import pallas as pl
from jax.experimental.pallas import tpu as pltpu
from jax.sharding import PartitionSpec as P

D = 512
FF = 2048
NHEADS = 8
DH = 64
SEQ_LEN = 1024
STEP = 10
GROUPW = 768
PART = 256

BETA_FIRST = 0.9
BETA_SECOND = 0.999
ADAM_EPSILON = 1e-08
WEIGHT_DECAY = 0.1
WEIGHT_RATE = 0.2
NORM_RATE = 0.2
NORM_EPSILON = 1e-05
MASK_VALUE = -1000000000.0

MESH = pl.DeviceIdType.MESH
F32 = jnp.float32
BF = jnp.bfloat16
VMEM_BYTES = 63 << 20
B_PLAN = {'first': [], 'after': [('send', 1), ('send', 2), ('send', 3)], 0: [], 1: [], 2: [('side', 0)], 3: [('pass', 1), ('pass', 2), ('pass', 3)], 4: [], 5: [('side', 1)], 6: [('side', 2)], 7: [('side', 3)]}
MID_STEPS = 2
UNROLL = 2
REDUCE_PLAN = ((0, 'hop1', 1), (0, 'hop2', 0), (2, 'hop3', 0), (3, 'hop2', 1), (4, 'hop4', 0), (5, 'hop3', 1))
X_FIRST = (0, 2)


def dot(a, b, ca, cb):
    return lax.dot_general(a, b, (((ca,), (cb,)), ((), ())), preferred_element_type=F32)


class Place:
    def __init__(self, batches, heads):
        self.X = self.Y = heads // 2
        self.Z = batches // self.Y
        self.batches, self.heads = batches, heads
        batch, head = lax.axis_index("batch"), lax.axis_index("head")
        self.j = batch
        self.z, self.y = batch // self.Y, batch % self.Y
        self.x, self.c = head // 2, head % 2
        self.xs = [lax.rem(self.x + d, self.X) for d in range(1, self.X)]
        self.ys = [lax.rem(self.y + d, self.Y) for d in range(1, self.Y)]
        self.zs = [lax.rem(self.z + d, self.Z) for d in range(1, self.Z)]

    def dev(self, z=None, y=None, x=None, c=None):
        z = self.z if z is None else z
        y = self.y if y is None else y
        x = self.x if x is None else x
        c = self.c if c is None else c
        return (z * self.Y + y, x * 2 + c)

    def greet(self, devices):
        barrier = pltpu.get_barrier_semaphore()
        for device in devices:
            pl.semaphore_signal(barrier, inc=1, device_id=device, device_id_type=MESH)

    def greeted(self, devices):
        pl.semaphore_wait(pltpu.get_barrier_semaphore(), len(devices))

    def plane(self):
        return [(x, y) for x in [self.x] + self.xs for y in [self.y] + self.ys][1:]


class Sends:
    def __init__(self, sems):
        self.sems, self.count, self.made = sems, 0, []

    def push(self, src, dst, recv, device, like, cond=None, given=None):
        copy = pltpu.make_async_remote_copy(
            src_ref=src, dst_ref=dst, send_sem=self.sems.at[self.count], recv_sem=recv,
            device_id=device, device_id_type=MESH,
        )
        if cond is None:
            copy.start()
        else:
            pl.when(cond())(lambda: copy.start())
        self.made.append((self.count, like, cond or given))
        self.count += 1

    def drain(self, place):
        for k, like, cond in self.made:
            sent = pltpu.make_async_remote_copy(
                src_ref=like(), dst_ref=like(), send_sem=self.sems.at[k], recv_sem=self.sems.at[k],
                device_id=place.dev(), device_id_type=MESH,
            )
            if cond is None:
                sent.wait_send()
            else:
                pl.when(cond())(lambda sent=sent: sent.wait_send())


def arrived(place, ref, recv, send):
    pltpu.make_async_remote_copy(
        src_ref=ref, dst_ref=ref, send_sem=send, recv_sem=recv, device_id=place.dev(), device_id_type=MESH
    ).wait_recv()


def bits(n):
    return [1 << k for k in range(n.bit_length() - 1)]


def norm_forward(u, gain, bias):
    centred = u - jnp.mean(u, axis=-1, keepdims=True)
    recip = lax.rsqrt(jnp.mean(centred * centred, axis=-1, keepdims=True) + NORM_EPSILON)
    normed = centred * recip
    return normed * gain + bias, normed, recip


def norm_back(grad, normed, recip, gain):
    e = grad * gain
    slope = jnp.mean(e * normed, axis=-1, keepdims=True)
    return recip * (e - jnp.mean(e, axis=-1, keepdims=True) - normed * slope)


def adam_update(param, grad, first, second, rate, decay):
    first_new = BETA_FIRST * first + (1.0 - BETA_FIRST) * grad
    second_new = BETA_SECOND * second + (1.0 - BETA_SECOND) * grad * grad
    first_hat = first_new * (1.0 / (1.0 - BETA_FIRST**STEP))
    second_hat = second_new * (1.0 / (1.0 - BETA_SECOND**STEP))
    param_new = param - rate * (first_hat / (jnp.sqrt(second_hat) + ADAM_EPSILON) + decay * param)
    return first_new, second_new, param_new


class Piece:
    def __init__(self, place, source, x_first, bufs, recv, sends):
        self.place, self.source, self.x_first, self.sends = place, source, x_first, sends
        self.s1 = source.at[place.c]
        self.r1, self.r2, self.s2, self.r3, self.s3, self.r4, self.final = bufs
        self.recv = recv

    def axis(self, x):
        p = self.place
        return (p.X, p.x, lambda v: p.dev(x=v)) if x else (p.Y, p.y, lambda v: p.dev(y=v))

    def send(self, axis, cut, buf, base):
        size, me, dev = axis
        for d in range(1, size):
            to = lax.rem(me + d, size)
            self.sends.push(cut(to), buf.at[d - 1], self.recv.at[base + d], dev(to), lambda: buf.at[0])

    def add(self, axis, own, buf, base):
        total = own.astype(F32)
        for d in range(1, axis[0]):
            arrived(self.place, buf.at[d - 1], self.recv.at[base + d], self.sends.sems.at[0])
            total = total + buf[d - 1].astype(F32)
        return total

    def hop0(self):
        p = self.place
        self.sends.push(self.source.at[1 - p.c], self.r1, self.recv.at[0], p.dev(c=1 - p.c), lambda: self.r1)

    def hop1(self):
        p = self.place
        arrived(p, self.r1, self.recv.at[0], self.sends.sems.at[0])
        self.s1[...] = (self.s1[...].astype(F32) + self.r1[...].astype(F32)).astype(BF)
        cut = lambda to: self.s1.at[to] if self.x_first else self.s1.at[:, :, to]
        self.send(self.axis(self.x_first), cut, self.r2, 0)

    def hop2(self):
        p = self.place
        own = self.s1[p.x] if self.x_first else self.s1[:, :, p.y]
        self.s2[...] = self.add(self.axis(self.x_first), own, self.r2, 0).astype(BF)
        cut = lambda to: self.s2.at[:, to] if self.x_first else self.s2.at[to]
        self.send(self.axis(not self.x_first), cut, self.r3, p.X)

    def hop3(self):
        p = self.place
        own = self.s2[:, p.y] if self.x_first else self.s2[p.x]
        self.s3[...] = self.add(self.axis(not self.x_first), own, self.r3, p.X).astype(BF)
        self.send((p.Z, p.z, lambda v: p.dev(z=v)), lambda to: self.s3.at[to], self.r4, 2 * p.X)

    def hop4(self):
        p = self.place
        self.final[...] = self.add((p.Z, p.z, None), self.s3[p.z], self.r4, 2 * p.X)


class Chunk:
    def __init__(self, place, g, dx, cc, source, bufs, recv, sends):
        self.place, self.dx, self.cc, self.sends = place, dx, cc, sends
        r1, rx, r2 = bufs
        self.source, self.r1, self.rx, self.r2 = source.at[g], r1.at[g, dx], rx.at[g], r2.at[g]
        self.recv = recv.at[g]

    def mine(self):
        return self.place.c == self.cc

    def hop0(self):
        p = self.place
        x = lax.rem(p.x + self.dx, p.X)
        self.sends.push(
            self.source.at[self.cc, x], self.r1, self.recv.at[self.dx], p.dev(c=self.cc), lambda: self.r1,
            lambda: self.place.c != self.cc,
        )

    def hop1(self):
        pl.when(self.mine())(self.pass_on)

    def pass_on(self):
        p = self.place
        x = lax.rem(p.x + self.dx, p.X)
        arrived(p, self.r1, self.recv.at[self.dx], self.sends.sems.at[0])
        total = self.source[self.cc, x].astype(F32) + self.r1[...].astype(F32)
        if self.dx:
            self.source[self.cc, x] = total.astype(BF)
            self.sends.push(
                self.source.at[self.cc, x], self.rx.at[self.dx - 1], self.recv.at[p.X + self.dx], p.dev(x=x),
                lambda: self.r1, given=self.mine,
            )
            return
        for d in range(1, p.X):
            arrived(p, self.rx.at[d - 1], self.recv.at[p.X + d], self.sends.sems.at[0])
            total = total + self.rx[d - 1].astype(F32)
        self.source[self.cc, x] = total.astype(BF)
        for d in range(1, p.batches):
            j = lax.rem(p.j + d, p.batches)
            self.sends.push(
                self.source.at[self.cc, x, j], self.r2.at[d - 1], self.recv.at[2 * p.X + d], (j, p.x * 2 + p.c),
                lambda: self.r2.at[0], given=self.mine,
            )


def collect(place, source, r2, recv, dummy):
    total = source[place.c, place.x, place.j].astype(F32)
    for d in range(1, place.batches):
        arrived(place, r2.at[d - 1], recv.at[2 * place.X + d], dummy)
        total = total + r2[d - 1].astype(F32)
    return total


def forward_sends(X, Y, Z, groups):
    part_a = groups * (Z - 1 + Z * (Y - 1)) + (X - 1) * (1 + Z - 1 + Y - 1) + X
    part_b = (X - 1) + (Y - 1) + (Z - 1) + 1 + (Z - 1) * (X + Y - 1)
    part_b += Z * (2 * (X - 1) * (Y - 1) + (X - 1) + (Y - 1) + (X - 1) * (Y - 1))
    return part_a + part_b


def backward_sends(X, Y, Z, groups):
    stages = 1 + sum(len(bits(v)) for v in (X, Y, Z))
    return 2 * groups * (X + Y + Z - 2) + groups * 2 * (X + X - 1 + Y * Z - 1) + stages


def layer_kernel(
    batches, heads, owner_ref, lengths_ref, gain_ref, bias_ref, post_in, weight_in, dual_in, pc_in, dc_in,
    post_out, dual_out, dpost_out, grad_ref, norm_out, p_hbm,
    post_ref, weight_ref, dual_ref, dc_ref, dmid_ref, dpre_ref, recip_ref, pick_ref, xs_ref, xst_ref, ga_ref, gb_ref, qk_ref, vx_ref, wide_ref, linv_ref, at_ref, dat_ref,
    w12_ref, wo_ref, mbt_ref, dft_ref, dbt_ref, dwo_ref, dqkv_ref,
    r1, xr2, yr2, xs2, ys2, r3, s3, r4, final, qr1, qrx, qr2, norm_send, norm_recv,
    recv_z, recv_y, recv_x, core_a, recv_b, send_f, recv_f, recv_q, norm_sems, send_r, p_sems, in_sems, out_sems,
):
    place = Place(batches, heads)
    groups, rows = NHEADS // heads, D // batches
    parts = 2 * groups
    X, Y, Z = place.X, place.Y, place.Z
    c, x, y, z = place.c, place.x, place.y, place.z
    sends = Sends(send_f)
    dummy = send_f.at[0]
    length = lengths_ref[lax.axis_index("head")]
    pc_ref = xs_ref
    ins = ((weight_in, weight_ref), (post_in, post_ref), (dc_in, dc_ref), (dual_in, dual_ref), (pc_in, pc_ref))

    def load(k):
        return pltpu.make_async_copy(*ins[k], in_sems.at[k])

    def core_push_a(xx):
        ref = ga_ref.at[c, xx]
        sends.push(ref, ref, core_a.at[xx], place.dev(c=1 - c), lambda: ga_ref.at[0, 0])

    def got_b(cc, xx, zz, yy):
        arrived(place, gb_ref.at[:, cc, xx, zz, yy], recv_b.at[cc, xx, zz, yy], dummy)

    def push_b(xx, zz, yy, device, cond=None):
        ref = gb_ref.at[:, c, xx, zz, yy]
        sends.push(ref, ref, recv_b.at[c, xx, zz, yy], device, lambda: gb_ref.at[:, 0, 0, 0, 0], cond)

    def side(offset):
        zo = lax.rem(z + offset, Z)
        low = lambda: lax.rem(place.z + offset, Z) < (3 * Z) // 4
        for xx in place.xs:
            got_b(c, xx, zo, y)
            for yy in place.ys:
                push_b(xx, zo, y, place.dev(y=yy), low)
            push_b(xx, zo, y, place.dev(c=1 - c))
        for yy in place.ys:
            got_b(c, x, zo, yy)
            for xx in place.xs:
                push_b(x, zo, yy, place.dev(x=xx), lambda: jnp.logical_not(low()))
            push_b(x, zo, yy, place.dev(c=1 - c))

    def spread(act, offset):
        for d in [d for d in range(Z) if d == offset or (offset == Z - 1 and d >= offset) or (offset == 1 and 0)]:
            zz = lax.rem(z + d, Z)
            if act == "send":
                push_b(x, z, y, place.dev(z=zz))
            elif act == "side":
                side(d)
            else:
                got_b(c, x, zz, y)
                for xx in place.xs:
                    push_b(x, zz, y, place.dev(x=xx))
                for yy in place.ys:
                    push_b(x, zz, y, place.dev(y=yy))
                push_b(x, zz, y, place.dev(c=1 - c))

    peers = [place.dev(z=zz, y=yy) for zz in [z] + place.zs for yy in [y] + place.ys][1:]
    peers += [place.dev(x=xx) for xx in place.xs] + [place.dev(c=1 - c)]
    place.greet(peers)
    for n in range(len(ins) - 1):
        load(n).start()
    load(0).wait()
    weight = weight_ref[...]
    for g in range(groups):
        ga_ref[c, x, z, y, g] = weight[:, g * GROUPW : g * GROUPW + PART].astype(BF)
    for k in range(parts):
        low = (k % groups) * GROUPW + (2 - k // groups) * PART
        gb_ref[k, c, x, z, y] = weight[:, low : low + PART].astype(BF)
    place.greeted(peers)

    def first_sends(g):
        own = ga_ref.at[c, x, z, y, g]
        for zz in place.zs:
            sends.push(own, own, recv_z.at[g, z], place.dev(z=zz), lambda: ga_ref.at[0, 0, 0, 0, 0])
        for yy in place.ys:
            sends.push(own, own, recv_y.at[g, z, y], place.dev(y=yy), lambda: ga_ref.at[0, 0, 0, 0, 0])

    for g in range(groups):
        first_sends(g)
    load(1).wait()
    lane = lax.broadcasted_iota(jnp.int32, (1, D), 1)
    source = lane % rows
    for b in range(batches):
        source = jnp.where(lane // rows == b, source + owner_ref[b] * rows, source)
    pick = (lax.broadcasted_iota(jnp.int32, (D, D), 0) == source).astype(F32).astype(BF)
    pick_ref[...] = pick
    ordered = dot(post_ref[...], pick, 1, 0).astype(BF)
    xs_ref[...] = ordered
    xst_ref[...] = ordered.T
    own = ga_ref.at[c, x, z, y]
    for xx in place.xs:
        sends.push(own, own, recv_x.at[x, z], place.dev(x=xx), lambda: ga_ref.at[0, 0, 0, 0])
    for act, offset in B_PLAN["first"]:
        spread(act, offset)
    for yy in place.ys:
        push_b(x, z, y, place.dev(y=yy))
    for xx in place.xs:
        push_b(x, z, y, place.dev(x=xx))
    for g in range(groups):
        for zz in place.zs:
            block = ga_ref.at[c, x, zz, y, g]
            arrived(place, block, recv_z.at[g, zz], dummy)
            for yy in place.ys:
                sends.push(block, block, recv_y.at[g, zz, y], place.dev(y=yy), lambda: ga_ref.at[0, 0, 0, 0, 0])
    for act, offset in B_PLAN["after"]:
        spread(act, offset)
    for xx in place.xs:
        for zz in place.zs:
            block = ga_ref.at[c, x, zz, y]
            sends.push(block, block, recv_x.at[x, zz], place.dev(x=xx), lambda: ga_ref.at[0, 0, 0, 0])
    push_b(x, z, y, place.dev(c=1 - c))


    def forward_transfers(t):
        if t < groups:
            for zz in range(Z):
                for yy in place.ys:
                    arrived(place, ga_ref.at[c, x, zz, yy, t], recv_y.at[t, zz, yy], dummy)
        if t == groups - 1:
            for yy in place.ys:
                column = ga_ref.at[c, x, :, yy]
                for xx in place.xs:
                    sends.push(column, column, recv_x.at[x, Z + yy], place.dev(x=xx), lambda: ga_ref.at[0, 0, :, 0])
            core_push_a(x)
        if t and t % groups == 0:
            k = t // groups
            xx = lax.rem(x + k // 2, X)
            if k % 2 == 0:
                for zz in [z] + place.zs:
                    arrived(place, ga_ref.at[c, xx, zz, y], recv_x.at[xx, zz], dummy)
                for yy in place.ys:
                    arrived(place, ga_ref.at[c, xx, :, yy], recv_x.at[xx, Z + yy], dummy)
                core_push_a(xx)
            else:
                arrived(place, ga_ref.at[1 - c, xx], core_a.at[xx], dummy)
        for act, offset in B_PLAN[t]:
            spread(act, offset)

    def p_store(i):
        slot = lax.rem(i, 4)
        return pltpu.make_async_copy(wide_ref.at[pl.ds(2 * slot, 2)], p_hbm.at[i], p_sems.at[slot])

    def p_fetch(i):
        g, r = i // heads, i % heads
        dx, cc = X - 1 - r // 2, r % 2
        spot = (2 * dx + (cc + c) % 2) * groups + g
        slot = lax.rem(i, 2)
        return pltpu.make_async_copy(p_hbm.at[spot], wide_ref.at[pl.ds(2 * slot, 2)], p_sems.at[slot])

    @pl.loop(0, NHEADS)
    def _(step):
        for t in range(NHEADS):
            pl.when(step == t)(functools.partial(forward_transfers, t))

        @pl.when(step >= 4)
        def _():
            p_store(step - 4).wait()

        q, g = step // groups, step % groups
        cc, xx = (c + q) % 2, lax.rem(x + q // 2, X)
        head = (xx * 2 + cc) * groups + g
        w = ga_ref[cc, xx, :, :, g].reshape(D, PART)
        proj = dot(xs_ref[...], w, 1, 0)
        lane = lax.broadcasted_iota(jnp.int32, (SEQ_LEN, 128), 1)
        qk = proj[:, :128].astype(BF)
        qk = jnp.where(lane < DH, qk * BF(DH**-0.5), qk)
        v = proj[:, 128:].astype(BF)
        vx = jnp.where(lane < DH, v, jnp.where(lane < DH + 2, BF(1), BF(0)))
        qk_ref[head] = qk
        vx_ref[head] = vx
        q_only = jnp.where(lane < DH, qk, BF(0))
        kq = jnp.concatenate([qk[:, DH:], qk[:, :DH]], axis=1)
        vxt = vx.T[: DH + 8]
        keep = lax.broadcasted_iota(jnp.int32, (SEQ_LEN, 1), 0) < length
        s = dot(kq, q_only, 1, 1)
        s = jnp.where(keep, s, F32(MASK_VALUE))
        m = jnp.max(s, axis=0, keepdims=True)
        p = jnp.exp(s - m).astype(BF)
        slot = lax.rem(step, 4)
        wide_ref[2 * slot] = p[:, : SEQ_LEN // 2]
        wide_ref[2 * slot + 1] = p[:, SEQ_LEN // 2 :]
        o = dot(vxt, p, 1, 0)
        r = 1.0 / o[DH : DH + 1]
        linv_ref[head] = r
        at_ref[head] = (o[:DH] * r).astype(BF)
        p_store(step).start()

    reduce_sends = Sends(send_r)
    pieces = []
    for k in range(parts):
        x_first = k in X_FIRST
        order = sum((j in X_FIRST) == x_first for j in range(k))
        bufs = (r1.at[k], xr2.at[order], xs2.at[order]) if x_first else (r1.at[k], yr2.at[order], ys2.at[order])
        bufs += tuple(b.at[k] for b in (r3, s3, r4, final))
        pieces.append(Piece(place, gb_ref.at[k], x_first, bufs, recv_f.at[k], reduce_sends))
    chunks = [
        Chunk(place, g, dx, cc, dqkv_ref, (qr1, qrx, qr2), recv_q, reduce_sends)
        for g in range(groups)
        for dx in reversed(range(X))
        for cc in range(2)
    ]
    partners = [place.dev(c=1 - c)]
    flip = lambda v, b: v + b - 2 * b * ((v // b) % 2)
    partners += [place.dev(x=flip(x, b)) for b in bits(X)]
    partners += [place.dev(y=flip(y, b)) for b in bits(Y)]
    partners += [place.dev(z=flip(z, b)) for b in bits(Z)]

    def norm_push(k):
        reduce_sends.push(norm_send.at[k], norm_recv.at[k], norm_sems.at[k], partners[k], lambda: norm_send.at[0])

    def norm_pull(k):
        arrived(place, norm_recv.at[k], norm_sems.at[k], send_r.at[0])
        norm_send[k + 1] = norm_send[k] + norm_recv[k]

    for i in range(NHEADS - 4, NHEADS):
        p_store(i).wait()
    load(4).start()
    load(2).wait()
    load(3).wait()
    held = []
    for b in range(batches):
        found = 0
        for j in range(1, batches):
            found = jnp.where(owner_ref[j] == b, j, found)
        held.append(found)
    for b in range(batches):
        there = slice(b * rows, (b + 1) * rows)
        for h in range(NHEADS):
            g, xx, cc = h % groups, (h // groups) // 2, (h // groups) % 2
            wo_ref[there, h * DH : (h + 1) * DH] = ga_ref[cc, xx, held[b] // Y, held[b] % Y, g][:, 3 * DH :]
    norm_send[0] = jnp.zeros((4, D), F32)

    block = SEQ_LEN // MID_STEPS
    outs = ((pc_ref, post_out), (dual_ref, dual_out))

    def store(n, t):
        here = pl.ds(pl.multiple_of(t * block, block), block)
        return pltpu.make_async_copy(outs[n][0].at[here], outs[n][1].at[here], out_sems.at[n, t])

    def block_of(t):
        return pl.ds(pl.multiple_of(t * block, block), block)

    def kept(t):
        return t * block + lax.broadcasted_iota(jnp.int32, (block, 1), 0) < length

    gain, bias = gain_ref[...], bias_ref[...]
    zero = jnp.zeros((1, D), F32)

    def over_tokens(value):
        return jnp.sum(value, axis=0, keepdims=True)

    @pl.loop(0, MID_STEPS, unroll=UNROLL)
    def _(t):
        here = block_of(t)
        branch = dot(at_ref[:, :, here].reshape(D, block), wo_ref[...], 0, 1)
        middle, n1, recip = norm_forward(post_ref[here, :].astype(F32) + branch, gain[0:1], bias[0:1])
        dual_ref[here, :] = dual_ref[here, :] + branch
        dmid_ref[here, :] = n1
        recip_ref[here, :] = recip
        middle_low = middle.astype(BF)
        post_ref[here, :] = middle_low
        mbt_ref[:, :, here] = middle_low.T.reshape(batches, rows, block)

    for offset in range(Z):
        zz = lax.rem(z + offset, Z)
        for yy in place.ys:
            for xx in place.xs:
                got_b(c, xx, zz, yy)
                push_b(xx, zz, yy, place.dev(c=1 - c))
    for xx in range(X):
        for zz in range(Z):
            for yy in range(Y):
                got_b(1 - c, xx, zz, yy)
    for b in range(batches):
        there = slice(b * rows, (b + 1) * rows)
        for h in range(NHEADS):
            g, xx, cc = h % groups, (h // groups) // 2, (h // groups) % 2
            for k in range(2):
                w12_ref[1 - k, there, h * PART : (h + 1) * PART] = gb_ref[
                    k * groups + g, cc, xx, held[b] // Y, held[b] % Y
                ]

    @pl.loop(0, MID_STEPS, unroll=UNROLL)
    def _(t):
        here = block_of(t)
        pre = dot(post_ref[here, :], w12_ref[0], 1, 0)
        cdf = 0.5 + 0.5 * lax.erf(pre * F32(math.sqrt(0.5)))
        density = jnp.exp(pre * pre * F32(-0.5)) * F32(1.0 / math.sqrt(2.0 * math.pi))
        hidden = (pre * cdf).astype(BF)
        slope = (cdf + pre * density).astype(BF)
        for k in range(4):
            wide_ref[k, here, :] = hidden[:, k * 512 : (k + 1) * 512]
            wide_ref[4 + k, here, :] = slope[:, k * 512 : (k + 1) * 512]

    load(4).wait()

    @pl.loop(0, MID_STEPS, unroll=UNROLL)
    def _(t):
        here = block_of(t)
        hidden = jnp.concatenate([wide_ref[k, here, :] for k in range(4)], axis=1)
        feed = dot(hidden, w12_ref[1], 1, 1)
        out, n2, recip = norm_forward(dmid_ref[here, :] * gain[0:1] + bias[0:1] + feed, gain[1:2], bias[1:2])
        dual_ref[here, :] = dual_ref[here, :] + feed
        d_out = jnp.where(kept(t), pc_ref[here, :].astype(F32), 0.0)
        d_dual = jnp.where(kept(t), dc_ref[here, :].astype(F32), 0.0)
        pc_ref[here, :] = out.astype(BF)
        store(0, t).start()
        store(1, t).start()
        d_pre = norm_back(d_out, n2, recip, gain[1:2])
        dpre_ref[here, :] = d_pre
        d_feed = (d_pre + d_dual).astype(BF)
        post_ref[here, :] = d_feed
        dft_ref[:, :, here] = d_feed.T.reshape(batches, rows, block)
        norm_send[0] = norm_send[0] + jnp.concatenate([zero, over_tokens(d_out * n2), zero, over_tokens(d_out)], axis=0)

    def in_slots(ref):
        return jnp.concatenate([ref[owner_ref[j]] for j in range(batches)], axis=0)

    def weight_piece(k):
        left = in_slots(dft_ref if k < groups else mbt_ref)
        for device in range(heads):
            h = device * groups + k % groups
            held = wide_ref[4 * (k // groups) + h // 2, :, (h % 2) * PART : (h % 2 + 1) * PART]
            grad = dot(left, held, 1, 0).astype(BF)
            gb_ref[k, device % 2, device // 2] = grad.reshape(Z, Y, rows, PART)
        pieces[k].hop0()

    sends.drain(place)
    for k in range(groups):
        weight_piece(k)
    p_fetch(0).start()
    p_fetch(1).start()

    @pl.loop(0, MID_STEPS, unroll=UNROLL)
    def _(t):
        here = block_of(t)
        d_hidden = dot(post_ref[here, :], w12_ref[1], 1, 0)
        slope = jnp.concatenate([wide_ref[4 + k, here, :] for k in range(4)], axis=1)
        d_hidden_pre = (d_hidden * slope.astype(F32)).astype(BF)
        for k in range(4):
            wide_ref[4 + k, here, :] = d_hidden_pre[:, k * 512 : (k + 1) * 512]
        d_middle = dpre_ref[here, :] + dot(d_hidden_pre, w12_ref[0], 1, 1)
        n1 = dmid_ref[here, :]
        d_mid = norm_back(d_middle, n1, recip_ref[here, :], gain[0:1])
        dmid_ref[here, :] = d_mid
        d_branch = (d_mid + jnp.where(kept(t), dc_ref[here, :].astype(F32), 0.0)).astype(BF)
        dbt_ref[:, :, here] = d_branch.T.reshape(batches, rows, block)
        dat_ref[:, :, here] = dot(wo_ref[...], d_branch, 0, 1).astype(BF).reshape(NHEADS, DH, block)
        norm_send[0] = norm_send[0] + jnp.concatenate(
            [over_tokens(d_middle * n1), zero, over_tokens(d_middle), zero], axis=0
        )
        for k in range(groups):
            pl.when(t == k)(pieces[k].hop1)

    norm_push(0)
    for k in range(groups, parts):
        weight_piece(k)
    dwo = dot(in_slots(dbt_ref), at_ref[...].reshape(D, SEQ_LEN), 1, 1).astype(BF)
    empty = jnp.zeros((D, DH), BF)
    for h in range(NHEADS):
        dwo_ref[h] = jnp.concatenate([empty, dwo[:, h * DH : (h + 1) * DH]], axis=1)

    half = parts // 2
    todo = [[] for _ in range(NHEADS + 1)]
    early, late = pieces[:half], pieces[half:]
    for n, chunk in enumerate(chunks):
        todo[n].append(chunk.hop0)
        if n + 1 < len(chunks):
            todo[n + 1].append(chunk.hop1)
    for k in range(4):
        todo[2 * k] += [functools.partial(norm_pull, k), functools.partial(norm_push, k + 1)]
    for t, hop, some in REDUCE_PLAN:
        todo[t] += [getattr(p, hop) for p in (early, late)[some]]

    def backward_transfers(t):
        for act in todo[t]:
            act()

    backward_transfers(-1)

    @pl.loop(0, NHEADS)
    def _(i):
        p_fetch(i).wait()
        g, r = i // heads, i % heads
        cc, xx = r % 2, lax.rem(x + X - 1 - r // 2, X)
        head = (xx * 2 + cc) * groups + g
        lane = lax.broadcasted_iota(jnp.int32, (SEQ_LEN, 128), 1)
        row = lax.broadcasted_iota(jnp.int32, (DH, SEQ_LEN), 0)
        qk, vx = qk_ref[head], vx_ref[head]
        do = dat_ref[head].astype(F32) * linv_ref[head]
        inner = -jnp.sum(do * at_ref[head].astype(F32), axis=0, keepdims=True)
        coarse = inner.astype(BF).astype(F32)
        tail = jnp.where(row == 0, coarse, jnp.where(row == 1, inner - coarse, 0.0))
        et = jnp.concatenate([do, tail], axis=0).astype(BF)
        e = et.T
        kt = qk.T[DH:]
        kq = jnp.concatenate([qk[:, DH:], qk[:, :DH]], axis=1)
        dk = jnp.zeros((SEQ_LEN, 128), F32)
        dv = jnp.zeros((SEQ_LEN, 128), F32)
        dqs = []
        slot = lax.rem(i, 2)
        for b in range(2):
            sl = slice(b * (SEQ_LEN // 2), (b + 1) * (SEQ_LEN // 2))
            p = wide_ref[2 * slot + b]
            ds = (p.astype(F32) * dot(vx, et[:, sl], 1, 0)).astype(BF)
            dv = dv + dot(p, e[sl], 1, 0)
            dk = dk + dot(ds, kq[sl], 1, 0)
            dqs.append(dot(kt, ds, 1, 0))
        dqt = jnp.concatenate(dqs, axis=1) * F32(DH**-0.5)
        dq = jnp.concatenate([dqt, jnp.zeros_like(dqt)], axis=0).T
        d_proj = jnp.concatenate([jnp.where(lane < DH, dq, dk), jnp.where(lane < DH, dv, 0.0)], axis=1).astype(BF)
        cols = pl.ds(pl.multiple_of(head * PART, PART), PART)
        w12_ref[0, :, cols] = d_proj[: SEQ_LEN // 2]
        w12_ref[1, :, cols] = d_proj[SEQ_LEN // 2 :]
        dw = dot(xst_ref[...], d_proj, 1, 0)
        dw = jnp.concatenate([dw[:, :128], dw[:, 128:] + dwo_ref[head].astype(F32)], axis=1).astype(BF)
        dqkv_ref[g, cc, xx] = dw.reshape(dqkv_ref.shape[3:])

        @pl.when(i + 2 < NHEADS)
        def _():
            p_fetch(i + 2).start()

        for t in range(NHEADS):
            pl.when(i == t)(functools.partial(backward_transfers, t))

    for k in range(4, len(partners)):
        norm_pull(k)
        if k + 1 < len(partners):
            norm_push(k + 1)
    norm_out[...] = norm_send[len(partners)]
    chunks[-1].hop1()
    table = []
    for h in range(NHEADS):
        g, xx, cc = h % groups, (h // groups) // 2, (h // groups) % 2
        table.append(ga_ref[cc, xx, :, :, g].reshape(D, PART))
    table = jnp.concatenate(table, axis=1)
    dpost = []
    for k in range(2):
        here = slice(k * (SEQ_LEN // 2), (k + 1) * (SEQ_LEN // 2))
        ordered = dot(w12_ref[k], table, 1, 1).astype(BF)
        dmid_ref[here, :] = dmid_ref[here, :] + dot(ordered, pick_ref[...], 1, 1)
        dpost.append(pltpu.make_async_copy(dmid_ref.at[here], dpost_out.at[here], in_sems.at[k]))
        dpost[k].start()
    for piece in pieces[len(pieces) // 2 :]:
        piece.hop4()
    for g in range(groups):
        low = g * GROUPW
        grad_ref[:, low + PART : low + 2 * PART] = final[groups + g]
        grad_ref[:, low + 2 * PART : low + 3 * PART] = final[g]
        grad_ref[:, low : low + PART] = collect(place, dqkv_ref.at[g], qr2.at[g], recv_q.at[g], send_r.at[0])
    for copy in dpost:
        copy.wait()
    for n in range(len(outs)):
        for t in range(MID_STEPS):
            store(n, t).wait()
    reduce_sends.drain(place)


def layer_call(owner, lengths, gain, bias, post, weights, dual, pc, dc, batches, heads):
    groups, rows = NHEADS // heads, D // batches
    parts = 2 * groups
    X = Y = heads // 2
    Z = batches // Y
    tokens = post.shape[0]
    assert tokens == SEQ_LEN
    stages = 1 + sum(len(bits(v)) for v in (X, Y, Z))
    smem, vmem = pl.BlockSpec(memory_space=pltpu.SMEM), pl.BlockSpec(memory_space=pltpu.VMEM)
    far = pl.BlockSpec(memory_space=pl.ANY)
    outs = [
        jax.ShapeDtypeStruct((tokens, D), BF),
        jax.ShapeDtypeStruct((tokens, D), F32),
        jax.ShapeDtypeStruct((tokens, D), F32),
        jax.ShapeDtypeStruct((rows, groups * GROUPW), F32),
        jax.ShapeDtypeStruct((4, D), F32),
        jax.ShapeDtypeStruct((NHEADS, 2, tokens, tokens // 2), BF),
    ]
    dma = pltpu.SemaphoreType.DMA
    x_parts = sum(k < parts for k in X_FIRST)
    return pl.pallas_call(
        functools.partial(layer_kernel, batches, heads),
        in_specs=[smem, smem, vmem, vmem] + [far] * 5,
        out_specs=[far, far, far, vmem, vmem, far],
        out_shape=outs,
        scratch_shapes=[
            pltpu.VMEM((tokens, D), BF),
            pltpu.VMEM(weights.shape, F32),
            pltpu.VMEM((tokens, D), F32),
            pltpu.VMEM((tokens, D), BF),
            pltpu.VMEM((tokens, D), F32),
            pltpu.VMEM((tokens, D), F32),
            pltpu.VMEM((tokens, 1), F32),
            pltpu.VMEM((D, D), BF),
            pltpu.VMEM((tokens, D), BF),
            pltpu.VMEM((D, tokens), BF),
            pltpu.VMEM((2, X, Z, Y, groups, rows, PART), BF),
            pltpu.VMEM((parts, 2, X, Z, Y, rows, PART), BF),
            pltpu.VMEM((NHEADS, tokens, 128), BF),
            pltpu.VMEM((NHEADS, tokens, 128), BF),
            pltpu.VMEM((8, tokens, tokens // 2), BF),
            pltpu.VMEM((NHEADS, 1, tokens), F32),
            pltpu.VMEM((NHEADS, DH, tokens), BF),
            pltpu.VMEM((NHEADS, DH, tokens), BF),
            pltpu.VMEM((2, D, FF), BF),
            pltpu.VMEM((D, D), BF),
            pltpu.VMEM((batches, rows, tokens), BF),
            pltpu.VMEM((batches, rows, tokens), BF),
            pltpu.VMEM((batches, rows, tokens), BF),
            pltpu.VMEM((NHEADS, D, 128), BF),
            pltpu.VMEM((groups, 2, X, batches, rows, PART), BF),
            pltpu.VMEM((parts, X, Z, Y, rows, PART), BF),
            pltpu.VMEM((x_parts, X - 1, Z, Y, rows, PART), BF),
            pltpu.VMEM((parts - x_parts, Y - 1, X, Z, rows, PART), BF),
            pltpu.VMEM((x_parts, Z, Y, rows, PART), BF),
            pltpu.VMEM((parts - x_parts, X, Z, rows, PART), BF),
            pltpu.VMEM((parts, X - 1, Z, rows, PART), BF),
            pltpu.VMEM((parts, Z, rows, PART), BF),
            pltpu.VMEM((parts, Z - 1, rows, PART), BF),
            pltpu.VMEM((parts, rows, PART), F32),
            pltpu.VMEM((groups, X, batches, rows, PART), BF),
            pltpu.VMEM((groups, X - 1, batches, rows, PART), BF),
            pltpu.VMEM((groups, batches - 1, rows, PART), BF),
            pltpu.VMEM((stages + 1, 4, D), F32),
            pltpu.VMEM((stages, 4, D), F32),
            dma((groups, Z)),
            dma((groups, Z, Y)),
            dma((X, Z + Y)),
            dma((X,)),
            dma((2, X, Z, Y)),
            dma((forward_sends(X, Y, Z, groups),)),
            dma((parts, 2 * X + Z)),
            dma((groups, 2 * X + batches)),
            dma((stages,)),
            dma((backward_sends(X, Y, Z, groups),)),
            dma((4,)),
            dma((5,)),
            dma((2, MID_STEPS)),
        ],
        name="layer",
        compiler_params=pltpu.CompilerParams(
            collective_id=1, has_side_effects=True, vmem_limit_bytes=VMEM_BYTES
        ),
    )(owner, lengths, gain, bias, post, weights, dual, pc, dc)


def update_kernel(
    post_in, dual_in, dpost_in, grad_ref, weight_ref, first_ref, second_ref,
    ngrad_ref, gain_ref, bias_ref, nfirst_ref, nsecond_ref,
    post_out, dual_out, dpost_out, first_out, second_out, weight_out, nfirst_out, nsecond_out, nparam_out,
):
    post_out[...] = post_in[...]
    dual_out[...] = dual_in[...]
    dpost_out[...] = dpost_in[...]
    first_out[...], second_out[...], weight_out[...] = adam_update(
        weight_ref[...], grad_ref[...], first_ref[...], second_ref[...], WEIGHT_RATE, WEIGHT_DECAY
    )
    nparam = jnp.concatenate([gain_ref[...], bias_ref[...]], axis=0)
    nfirst_out[...], nsecond_out[...], nparam_out[...] = adam_update(
        nparam, ngrad_ref[...], nfirst_ref[...], nsecond_ref[...], NORM_RATE, 0.0
    )


def update_call(post, dual, dpost, grad, weights, first, second, ngrad, gain, bias, nfirst, nsecond):
    steps = 2
    cut = lambda a: pl.BlockSpec((a.shape[0] // steps, a.shape[1]), lambda i: (i, 0))
    same = lambda a: pl.BlockSpec(a.shape, lambda i: (0, 0))
    outs = [post, dual, dpost, weights, weights, weights, nfirst, nfirst, nfirst]
    return pl.pallas_call(
        update_kernel,
        grid=(steps,),
        in_specs=[cut(a) for a in (post, dual, dpost, grad, weights, first, second)]
        + [same(a) for a in (ngrad, gain, bias, nfirst, nsecond)],
        out_specs=[cut(a) for a in outs[:6]] + [same(a) for a in outs[6:]],
        out_shape=[jax.ShapeDtypeStruct(a.shape, a.dtype) for a in outs],
        name="update",
        compiler_params=pltpu.CompilerParams(vmem_limit_bytes=VMEM_BYTES),
    )(post, dual, dpost, grad, weights, first, second, ngrad, gain, bias, nfirst, nsecond)


def shards(
    post_stream,
    dual_stream,
    post_cotangent,
    dual_cotangent,
    seq_lengths,
    owner_slots,
    weights,
    first_moment,
    second_moment,
    norm_gain,
    norm_bias,
    norm_first,
    norm_second,
):
    batches, heads = lax.axis_size("batch"), lax.axis_size("head")
    post, dual, dpost, grad, norm_grad, _ = layer_call(
        owner_slots, seq_lengths, norm_gain, norm_bias, post_stream, weights, dual_stream, post_cotangent,
        dual_cotangent, batches, heads,
    )
    return update_call(
        post, dual, dpost, grad, weights, first_moment, second_moment,
        norm_grad, norm_gain, norm_bias, norm_first, norm_second,
    )


def solution(mesh):
    tokens, table, copied = P(("batch", "head"), None), P("batch", "head"), P()
    in_specs = (tokens,) * 4 + (P("batch"), copied) + (table,) * 3 + (copied,) * 4
    out_specs = (tokens,) * 3 + (table,) * 3 + (copied,) * 3
    return jax.shard_map(shards, mesh=mesh, in_specs=in_specs, out_specs=out_specs, check_vma=False)
```

```python
import functools
import math

import jax
import jax.numpy as jnp
from jax import lax
from jax.experimental import pallas as pl
from jax.experimental.pallas import tpu as pltpu
from jax.sharding import PartitionSpec as P

D = 512
FF = 2048
NHEADS = 8
DH = 64
SEQ_LEN = 1024
STEP = 10
GROUPW = 768
PART = 256

BETA_FIRST = 0.9
BETA_SECOND = 0.999
ADAM_EPSILON = 1e-08
WEIGHT_DECAY = 0.1
WEIGHT_RATE = 0.2
NORM_RATE = 0.2
NORM_EPSILON = 1e-05
MASK_VALUE = -1000000000.0

MESH = pl.DeviceIdType.MESH
F32 = jnp.float32
BF = jnp.bfloat16
VMEM_BYTES = 63 << 20
B_PLAN = {'first': [], 'after': [('send', 1), ('send', 2), ('send', 3)], 0: [], 1: [], 2: [('side', 0)], 3: [('pass', 1), ('pass', 2), ('pass', 3)], 4: [], 5: [('side', 1)], 6: [('side', 2)], 7: [('side', 3)]}
MID_STEPS = 2
UNROLL = 2
REDUCE_PLAN = ((0, 'hop1', 1), (0, 'hop2', 0), (2, 'hop3', 0), (3, 'hop2', 1), (4, 'hop4', 0), (5, 'hop3', 1))
X_FIRST = (0, 2)


def dot(a, b, ca, cb):
    return lax.dot_general(a, b, (((ca,), (cb,)), ((), ())), preferred_element_type=F32)


class Place:
    def __init__(self, batches, heads):
        self.X = self.Y = heads // 2
        self.Z = batches // self.Y
        self.batches, self.heads = batches, heads
        batch, head = lax.axis_index("batch"), lax.axis_index("head")
        self.j = batch
        self.z, self.y = batch // self.Y, batch % self.Y
        self.x, self.c = head // 2, head % 2
        self.xs = [lax.rem(self.x + d, self.X) for d in range(1, self.X)]
        self.ys = [lax.rem(self.y + d, self.Y) for d in range(1, self.Y)]
        self.zs = [lax.rem(self.z + d, self.Z) for d in range(1, self.Z)]

    def dev(self, z=None, y=None, x=None, c=None):
        z = self.z if z is None else z
        y = self.y if y is None else y
        x = self.x if x is None else x
        c = self.c if c is None else c
        return (z * self.Y + y, x * 2 + c)

    def greet(self, devices):
        barrier = pltpu.get_barrier_semaphore()
        for device in devices:
            pl.semaphore_signal(barrier, inc=1, device_id=device, device_id_type=MESH)

    def greeted(self, devices):
        pl.semaphore_wait(pltpu.get_barrier_semaphore(), len(devices))

    def plane(self):
        return [(x, y) for x in [self.x] + self.xs for y in [self.y] + self.ys][1:]


class Sends:
    def __init__(self, sems):
        self.sems, self.count, self.made = sems, 0, []

    def push(self, src, dst, recv, device, like, cond=None, given=None):
        copy = pltpu.make_async_remote_copy(
            src_ref=src, dst_ref=dst, send_sem=self.sems.at[self.count], recv_sem=recv,
            device_id=device, device_id_type=MESH,
        )
        if cond is None:
            copy.start()
        else:
            pl.when(cond())(lambda: copy.start())
        self.made.append((self.count, like, cond or given))
        self.count += 1

    def drain(self, place):
        for k, like, cond in self.made:
            sent = pltpu.make_async_remote_copy(
                src_ref=like(), dst_ref=like(), send_sem=self.sems.at[k], recv_sem=self.sems.at[k],
                device_id=place.dev(), device_id_type=MESH,
            )
            if cond is None:
                sent.wait_send()
            else:
                pl.when(cond())(lambda sent=sent: sent.wait_send())


def arrived(place, ref, recv, send):
    pltpu.make_async_remote_copy(
        src_ref=ref, dst_ref=ref, send_sem=send, recv_sem=recv, device_id=place.dev(), device_id_type=MESH
    ).wait_recv()


def bits(n):
    return [1 << k for k in range(n.bit_length() - 1)]


def norm_forward(u, gain, bias):
    centred = u - jnp.mean(u, axis=-1, keepdims=True)
    recip = lax.rsqrt(jnp.mean(centred * centred, axis=-1, keepdims=True) + NORM_EPSILON)
    normed = centred * recip
    return normed * gain + bias, normed, recip


def norm_back(grad, normed, recip, gain):
    e = grad * gain
    slope = jnp.mean(e * normed, axis=-1, keepdims=True)
    return recip * (e - jnp.mean(e, axis=-1, keepdims=True) - normed * slope)


def adam_update(param, grad, first, second, rate, decay):
    first_new = BETA_FIRST * first + (1.0 - BETA_FIRST) * grad
    second_new = BETA_SECOND * second + (1.0 - BETA_SECOND) * grad * grad
    first_hat = first_new * (1.0 / (1.0 - BETA_FIRST**STEP))
    second_hat = second_new * (1.0 / (1.0 - BETA_SECOND**STEP))
    param_new = param - rate * (first_hat / (jnp.sqrt(second_hat) + ADAM_EPSILON) + decay * param)
    return first_new, second_new, param_new


class Piece:
    def __init__(self, place, source, x_first, bufs, recv, sends):
        self.place, self.source, self.x_first, self.sends = place, source, x_first, sends
        self.s1 = source.at[place.c]
        self.r1, self.r2, self.s2, self.r3, self.s3, self.r4, self.final = bufs
        self.recv = recv

    def axis(self, x):
        p = self.place
        return (p.X, p.x, lambda v: p.dev(x=v)) if x else (p.Y, p.y, lambda v: p.dev(y=v))

    def send(self, axis, cut, buf, base):
        size, me, dev = axis
        for d in range(1, size):
            to = lax.rem(me + d, size)
            self.sends.push(cut(to), buf.at[d - 1], self.recv.at[base + d], dev(to), lambda: buf.at[0])

    def add(self, axis, own, buf, base):
        total = own.astype(F32)
        for d in range(1, axis[0]):
            arrived(self.place, buf.at[d - 1], self.recv.at[base + d], self.sends.sems.at[0])
            total = total + buf[d - 1].astype(F32)
        return total

    def hop0(self):
        p = self.place
        self.sends.push(self.source.at[1 - p.c], self.r1, self.recv.at[0], p.dev(c=1 - p.c), lambda: self.r1)

    def hop1(self):
        p = self.place
        arrived(p, self.r1, self.recv.at[0], self.sends.sems.at[0])
        self.s1[...] = (self.s1[...].astype(F32) + self.r1[...].astype(F32)).astype(BF)
        cut = lambda to: self.s1.at[to] if self.x_first else self.s1.at[:, :, to]
        self.send(self.axis(self.x_first), cut, self.r2, 0)

    def hop2(self):
        p = self.place
        own = self.s1[p.x] if self.x_first else self.s1[:, :, p.y]
        self.s2[...] = self.add(self.axis(self.x_first), own, self.r2, 0).astype(BF)
        cut = lambda to: self.s2.at[:, to] if self.x_first else self.s2.at[to]
        self.send(self.axis(not self.x_first), cut, self.r3, p.X)

    def hop3(self):
        p = self.place
        own = self.s2[:, p.y] if self.x_first else self.s2[p.x]
        self.s3[...] = self.add(self.axis(not self.x_first), own, self.r3, p.X).astype(BF)
        self.send((p.Z, p.z, lambda v: p.dev(z=v)), lambda to: self.s3.at[to], self.r4, 2 * p.X)

    def hop4(self):
        p = self.place
        self.final[...] = self.add((p.Z, p.z, None), self.s3[p.z], self.r4, 2 * p.X)


class Chunk:
    def __init__(self, place, g, dx, cc, source, bufs, recv, sends):
        self.place, self.dx, self.cc, self.sends = place, dx, cc, sends
        r1, rx, r2 = bufs
        self.source, self.r1, self.rx, self.r2 = source.at[g], r1.at[g, dx], rx.at[g], r2.at[g]
        self.recv = recv.at[g]

    def mine(self):
        return self.place.c == self.cc

    def hop0(self):
        p = self.place
        x = lax.rem(p.x + self.dx, p.X)
        self.sends.push(
            self.source.at[self.cc, x], self.r1, self.recv.at[self.dx], p.dev(c=self.cc), lambda: self.r1,
            lambda: self.place.c != self.cc,
        )

    def hop1(self):
        pl.when(self.mine())(self.pass_on)

    def pass_on(self):
        p = self.place
        x = lax.rem(p.x + self.dx, p.X)
        arrived(p, self.r1, self.recv.at[self.dx], self.sends.sems.at[0])
        total = self.source[self.cc, x].astype(F32) + self.r1[...].astype(F32)
        if self.dx:
            self.source[self.cc, x] = total.astype(BF)
            self.sends.push(
                self.source.at[self.cc, x], self.rx.at[self.dx - 1], self.recv.at[p.X + self.dx], p.dev(x=x),
                lambda: self.r1, given=self.mine,
            )
            return
        for d in range(1, p.X):
            arrived(p, self.rx.at[d - 1], self.recv.at[p.X + d], self.sends.sems.at[0])
            total = total + self.rx[d - 1].astype(F32)
        self.source[self.cc, x] = total.astype(BF)
        for d in range(1, p.batches):
            j = lax.rem(p.j + d, p.batches)
            self.sends.push(
                self.source.at[self.cc, x, j], self.r2.at[d - 1], self.recv.at[2 * p.X + d], (j, p.x * 2 + p.c),
                lambda: self.r2.at[0], given=self.mine,
            )


def collect(place, source, r2, recv, dummy):
    total = source[place.c, place.x, place.j].astype(F32)
    for d in range(1, place.batches):
        arrived(place, r2.at[d - 1], recv.at[2 * place.X + d], dummy)
        total = total + r2[d - 1].astype(F32)
    return total


def forward_sends(X, Y, Z, groups):
    part_a = groups * (Z - 1 + Z * (Y - 1)) + (X - 1) * (1 + Z - 1 + Y - 1) + X
    part_b = (X - 1) + (Y - 1) + (Z - 1) + 1 + (Z - 1) * (X + Y - 1)
    part_b += Z * (2 * (X - 1) * (Y - 1) + (X - 1) + (Y - 1) + (X - 1) * (Y - 1))
    return part_a + part_b


def backward_sends(X, Y, Z, groups):
    stages = 1 + sum(len(bits(v)) for v in (X, Y, Z))
    return 2 * groups * (X + Y + Z - 2) + groups * 2 * (X + X - 1 + Y * Z - 1) + stages


def layer_kernel(
    batches, heads, owner_ref, lengths_ref, gain_ref, bias_ref, post_in, weight_in, dual_in, pc_in, dc_in,
    post_out, dual_out, dpost_out, grad_ref, norm_out, p_hbm,
    post_ref, weight_ref, dual_ref, dc_ref, dmid_ref, dpre_ref, recip_ref, pick_ref, xs_ref, xst_ref, ga_ref, gb_ref, qk_ref, vx_ref, wide_ref, linv_ref, at_ref, dat_ref,
    w12_ref, wo_ref, mbt_ref, dft_ref, dbt_ref, dwo_ref, dqkv_ref,
    r1, xr2, yr2, xs2, ys2, r3, s3, r4, final, qr1, qrx, qr2, norm_send, norm_recv,
    recv_z, recv_y, recv_x, core_a, recv_b, send_f, recv_f, recv_q, norm_sems, send_r, p_sems, in_sems, out_sems,
):
    place = Place(batches, heads)
    groups, rows = NHEADS // heads, D // batches
    parts = 2 * groups
    X, Y, Z = place.X, place.Y, place.Z
    c, x, y, z = place.c, place.x, place.y, place.z
    sends = Sends(send_f)
    dummy = send_f.at[0]
    length = lengths_ref[lax.axis_index("head")]
    pc_ref = xs_ref
    ins = ((weight_in, weight_ref), (post_in, post_ref), (dc_in, dc_ref), (dual_in, dual_ref), (pc_in, pc_ref))

    def load(k):
        return pltpu.make_async_copy(*ins[k], in_sems.at[k])

    def core_push_a(xx):
        ref = ga_ref.at[c, xx]
        sends.push(ref, ref, core_a.at[xx], place.dev(c=1 - c), lambda: ga_ref.at[0, 0])

    def got_b(cc, xx, zz, yy):
        arrived(place, gb_ref.at[:, cc, xx, zz, yy], recv_b.at[cc, xx, zz, yy], dummy)

    def push_b(xx, zz, yy, device, cond=None):
        ref = gb_ref.at[:, c, xx, zz, yy]
        sends.push(ref, ref, recv_b.at[c, xx, zz, yy], device, lambda: gb_ref.at[:, 0, 0, 0, 0], cond)

    def side(offset):
        zo = lax.rem(z + offset, Z)
        low = lambda: lax.rem(place.z + offset, Z) < (3 * Z) // 4
        for xx in place.xs:
            got_b(c, xx, zo, y)
            for yy in place.ys:
                push_b(xx, zo, y, place.dev(y=yy), low)
            push_b(xx, zo, y, place.dev(c=1 - c))
        for yy in place.ys:
            got_b(c, x, zo, yy)
            for xx in place.xs:
                push_b(x, zo, yy, place.dev(x=xx), lambda: jnp.logical_not(low()))
            push_b(x, zo, yy, place.dev(c=1 - c))

    def spread(act, offset):
        for d in [d for d in range(Z) if d == offset or (offset == Z - 1 and d >= offset) or (offset == 1 and 0)]:
            zz = lax.rem(z + d, Z)
            if act == "send":
                push_b(x, z, y, place.dev(z=zz))
            elif act == "side":
                side(d)
            else:
                got_b(c, x, zz, y)
                for xx in place.xs:
                    push_b(x, zz, y, place.dev(x=xx))
                for yy in place.ys:
                    push_b(x, zz, y, place.dev(y=yy))
                push_b(x, zz, y, place.dev(c=1 - c))

    peers = [place.dev(z=zz, y=yy) for zz in [z] + place.zs for yy in [y] + place.ys][1:]
    peers += [place.dev(x=xx) for xx in place.xs] + [place.dev(c=1 - c)]
    place.greet(peers)
    for n in range(len(ins) - 1):
        load(n).start()
    load(0).wait()
    weight = weight_ref[...]
    for g in range(groups):
        ga_ref[c, x, z, y, g] = weight[:, g * GROUPW : g * GROUPW + PART].astype(BF)
    for k in range(parts):
        low = (k % groups) * GROUPW + (2 - k // groups) * PART
        gb_ref[k, c, x, z, y] = weight[:, low : low + PART].astype(BF)
    place.greeted(peers)

    def first_sends(g):
        own = ga_ref.at[c, x, z, y, g]
        for zz in place.zs:
            sends.push(own, own, recv_z.at[g, z], place.dev(z=zz), lambda: ga_ref.at[0, 0, 0, 0, 0])
        for yy in place.ys:
            sends.push(own, own, recv_y.at[g, z, y], place.dev(y=yy), lambda: ga_ref.at[0, 0, 0, 0, 0])

    for g in range(groups):
        first_sends(g)
    load(1).wait()
    lane = lax.broadcasted_iota(jnp.int32, (1, D), 1)
    source = lane % rows
    for b in range(batches):
        source = jnp.where(lane // rows == b, source + owner_ref[b] * rows, source)
    pick = (lax.broadcasted_iota(jnp.int32, (D, D), 0) == source).astype(F32).astype(BF)
    pick_ref[...] = pick
    ordered = dot(post_ref[...], pick, 1, 0).astype(BF)
    xs_ref[...] = ordered
    xst_ref[...] = ordered.T
    own = ga_ref.at[c, x, z, y]
    for xx in place.xs:
        sends.push(own, own, recv_x.at[x, z], place.dev(x=xx), lambda: ga_ref.at[0, 0, 0, 0])
    for act, offset in B_PLAN["first"]:
        spread(act, offset)
    for yy in place.ys:
        push_b(x, z, y, place.dev(y=yy))
    for xx in place.xs:
        push_b(x, z, y, place.dev(x=xx))
    for g in range(groups):
        for zz in place.zs:
            block = ga_ref.at[c, x, zz, y, g]
            arrived(place, block, recv_z.at[g, zz], dummy)
            for yy in place.ys:
                sends.push(block, block, recv_y.at[g, zz, y], place.dev(y=yy), lambda: ga_ref.at[0, 0, 0, 0, 0])
    for act, offset in B_PLAN["after"]:
        spread(act, offset)
    for xx in place.xs:
        for zz in place.zs:
            block = ga_ref.at[c, x, zz, y]
            sends.push(block, block, recv_x.at[x, zz], place.dev(x=xx), lambda: ga_ref.at[0, 0, 0, 0])
    push_b(x, z, y, place.dev(c=1 - c))


    def forward_transfers(t):
        if t < groups:
            for zz in range(Z):
                for yy in place.ys:
                    arrived(place, ga_ref.at[c, x, zz, yy, t], recv_y.at[t, zz, yy], dummy)
        if t == groups - 1:
            for yy in place.ys:
                column = ga_ref.at[c, x, :, yy]
                for xx in place.xs:
                    sends.push(column, column, recv_x.at[x, Z + yy], place.dev(x=xx), lambda: ga_ref.at[0, 0, :, 0])
            core_push_a(x)
        if t and t % groups == 0:
            k = t // groups
            xx = lax.rem(x + k // 2, X)
            if k % 2 == 0:
                for zz in [z] + place.zs:
                    arrived(place, ga_ref.at[c, xx, zz, y], recv_x.at[xx, zz], dummy)
                for yy in place.ys:
                    arrived(place, ga_ref.at[c, xx, :, yy], recv_x.at[xx, Z + yy], dummy)
                core_push_a(xx)
            else:
                arrived(place, ga_ref.at[1 - c, xx], core_a.at[xx], dummy)
        for act, offset in B_PLAN[t]:
            spread(act, offset)

    def p_store(i):
        slot = lax.rem(i, 4)
        return pltpu.make_async_copy(wide_ref.at[pl.ds(2 * slot, 2)], p_hbm.at[i], p_sems.at[slot])

    def p_fetch(i):
        g, r = i // heads, i % heads
        dx, cc = X - 1 - r // 2, r % 2
        spot = (2 * dx + (cc + c) % 2) * groups + g
        slot = lax.rem(i, 2)
        return pltpu.make_async_copy(p_hbm.at[spot], wide_ref.at[pl.ds(2 * slot, 2)], p_sems.at[slot])

    @pl.loop(0, NHEADS)
    def _(step):
        for t in range(NHEADS):
            pl.when(step == t)(functools.partial(forward_transfers, t))

        @pl.when(step >= 4)
        def _():
            p_store(step - 4).wait()

        q, g = step // groups, step % groups
        cc, xx = (c + q) % 2, lax.rem(x + q // 2, X)
        head = (xx * 2 + cc) * groups + g
        w = ga_ref[cc, xx, :, :, g].reshape(D, PART)
        proj = dot(xs_ref[...], w, 1, 0)
        lane = lax.broadcasted_iota(jnp.int32, (SEQ_LEN, 128), 1)
        qk = proj[:, :128].astype(BF)
        qk = jnp.where(lane < DH, qk * BF(DH**-0.5), qk)
        v = proj[:, 128:].astype(BF)
        vx = jnp.where(lane < DH, v, jnp.where(lane < DH + 2, BF(1), BF(0)))
        qk_ref[head] = qk
        vx_ref[head] = vx
        q_only = jnp.where(lane < DH, qk, BF(0))
        kq = jnp.concatenate([qk[:, DH:], qk[:, :DH]], axis=1)
        vxt = vx.T[: DH + 8]
        keep = lax.broadcasted_iota(jnp.int32, (SEQ_LEN, 1), 0) < length
        s = dot(kq, q_only, 1, 1)
        s = jnp.where(keep, s, F32(MASK_VALUE))
        m = jnp.max(s, axis=0, keepdims=True)
        p = jnp.exp(s - m).astype(BF)
        slot = lax.rem(step, 4)
        wide_ref[2 * slot] = p[:, : SEQ_LEN // 2]
        wide_ref[2 * slot + 1] = p[:, SEQ_LEN // 2 :]
        o = dot(vxt, p, 1, 0)
        r = 1.0 / o[DH : DH + 1]
        linv_ref[head] = r
        at_ref[head] = (o[:DH] * r).astype(BF)
        p_store(step).start()

    reduce_sends = Sends(send_r)
    pieces = []
    for k in range(parts):
        x_first = k in X_FIRST
        order = sum((j in X_FIRST) == x_first for j in range(k))
        bufs = (r1.at[k], xr2.at[order], xs2.at[order]) if x_first else (r1.at[k], yr2.at[order], ys2.at[order])
        bufs += tuple(b.at[k] for b in (r3, s3, r4, final))
        pieces.append(Piece(place, gb_ref.at[k], x_first, bufs, recv_f.at[k], reduce_sends))
    chunks = [
        Chunk(place, g, dx, cc, dqkv_ref, (qr1, qrx, qr2), recv_q, reduce_sends)
        for g in range(groups)
        for dx in reversed(range(X))
        for cc in range(2)
    ]
    partners = [place.dev(c=1 - c)]
    flip = lambda v, b: v + b - 2 * b * ((v // b) % 2)
    partners += [place.dev(x=flip(x, b)) for b in bits(X)]
    partners += [place.dev(y=flip(y, b)) for b in bits(Y)]
    partners += [place.dev(z=flip(z, b)) for b in bits(Z)]

    def norm_push(k):
        reduce_sends.push(norm_send.at[k], norm_recv.at[k], norm_sems.at[k], partners[k], lambda: norm_send.at[0])

    def norm_pull(k):
        arrived(place, norm_recv.at[k], norm_sems.at[k], send_r.at[0])
        norm_send[k + 1] = norm_send[k] + norm_recv[k]

    for i in range(NHEADS - 4, NHEADS):
        p_store(i).wait()
    load(4).start()
    load(2).wait()
    load(3).wait()
    held = []
    for b in range(batches):
        found = 0
        for j in range(1, batches):
            found = jnp.where(owner_ref[j] == b, j, found)
        held.append(found)
    for b in range(batches):
        there = slice(b * rows, (b + 1) * rows)
        for h in range(NHEADS):
            g, xx, cc = h % groups, (h // groups) // 2, (h // groups) % 2
            wo_ref[there, h * DH : (h + 1) * DH] = ga_ref[cc, xx, held[b] // Y, held[b] % Y, g][:, 3 * DH :]
    norm_send[0] = jnp.zeros((4, D), F32)

    block = SEQ_LEN // MID_STEPS
    outs = ((pc_ref, post_out), (dual_ref, dual_out))

    def store(n, t):
        here = pl.ds(pl.multiple_of(t * block, block), block)
        return pltpu.make_async_copy(outs[n][0].at[here], outs[n][1].at[here], out_sems.at[n, t])

    def block_of(t):
        return pl.ds(pl.multiple_of(t * block, block), block)

    def kept(t):
        return t * block + lax.broadcasted_iota(jnp.int32, (block, 1), 0) < length

    gain, bias = gain_ref[...], bias_ref[...]
    zero = jnp.zeros((1, D), F32)

    def over_tokens(value):
        return jnp.sum(value, axis=0, keepdims=True)

    @pl.loop(0, MID_STEPS, unroll=UNROLL)
    def _(t):
        here = block_of(t)
        branch = dot(at_ref[:, :, here].reshape(D, block), wo_ref[...], 0, 1)
        middle, n1, recip = norm_forward(post_ref[here, :].astype(F32) + branch, gain[0:1], bias[0:1])
        dual_ref[here, :] = dual_ref[here, :] + branch
        dmid_ref[here, :] = n1
        recip_ref[here, :] = recip
        middle_low = middle.astype(BF)
        post_ref[here, :] = middle_low
        mbt_ref[:, :, here] = middle_low.T.reshape(batches, rows, block)

    for offset in range(Z):
        zz = lax.rem(z + offset, Z)
        for yy in place.ys:
            for xx in place.xs:
                got_b(c, xx, zz, yy)
                push_b(xx, zz, yy, place.dev(c=1 - c))
    for xx in range(X):
        for zz in range(Z):
            for yy in range(Y):
                got_b(1 - c, xx, zz, yy)
    for b in range(batches):
        there = slice(b * rows, (b + 1) * rows)
        for h in range(NHEADS):
            g, xx, cc = h % groups, (h // groups) // 2, (h // groups) % 2
            for k in range(2):
                w12_ref[1 - k, there, h * PART : (h + 1) * PART] = gb_ref[
                    k * groups + g, cc, xx, held[b] // Y, held[b] % Y
                ]

    load(4).wait()

    @pl.loop(0, MID_STEPS)
    def _(t):
        here = block_of(t)
        pre = dot(post_ref[here, :], w12_ref[0], 1, 0)
        cdf = 0.5 + 0.5 * lax.erf(pre * F32(math.sqrt(0.5)))
        density = jnp.exp(pre * pre * F32(-0.5)) * F32(1.0 / math.sqrt(2.0 * math.pi))
        hidden = (pre * cdf).astype(BF)
        slope = (cdf + pre * density).astype(BF)
        for k in range(4):
            wide_ref[k, here, :] = hidden[:, k * 512 : (k + 1) * 512]
            wide_ref[4 + k, here, :] = slope[:, k * 512 : (k + 1) * 512]
        feed = dot(hidden, w12_ref[1], 1, 1)
        out, n2, recip = norm_forward(dmid_ref[here, :] * gain[0:1] + bias[0:1] + feed, gain[1:2], bias[1:2])
        dual_ref[here, :] = dual_ref[here, :] + feed
        d_out = jnp.where(kept(t), pc_ref[here, :].astype(F32), 0.0)
        d_dual = jnp.where(kept(t), dc_ref[here, :].astype(F32), 0.0)
        pc_ref[here, :] = out.astype(BF)
        store(0, t).start()
        store(1, t).start()
        d_pre = norm_back(d_out, n2, recip, gain[1:2])
        dpre_ref[here, :] = d_pre
        d_feed = (d_pre + d_dual).astype(BF)
        post_ref[here, :] = d_feed
        dft_ref[:, :, here] = d_feed.T.reshape(batches, rows, block)
        norm_send[0] = norm_send[0] + jnp.concatenate([zero, over_tokens(d_out * n2), zero, over_tokens(d_out)], axis=0)

    def in_slots(ref):
        return jnp.concatenate([ref[owner_ref[j]] for j in range(batches)], axis=0)

    def weight_piece(k):
        left = in_slots(dft_ref if k < groups else mbt_ref)
        for device in range(heads):
            h = device * groups + k % groups
            held = wide_ref[4 * (k // groups) + h // 2, :, (h % 2) * PART : (h % 2 + 1) * PART]
            grad = dot(left, held, 1, 0).astype(BF)
            gb_ref[k, device % 2, device // 2] = grad.reshape(Z, Y, rows, PART)
        pieces[k].hop0()

    sends.drain(place)
    for k in range(groups):
        weight_piece(k)
    p_fetch(0).start()
    p_fetch(1).start()

    @pl.loop(0, MID_STEPS, unroll=UNROLL)
    def _(t):
        here = block_of(t)
        d_hidden = dot(post_ref[here, :], w12_ref[1], 1, 0)
        slope = jnp.concatenate([wide_ref[4 + k, here, :] for k in range(4)], axis=1)
        d_hidden_pre = (d_hidden * slope.astype(F32)).astype(BF)
        for k in range(4):
            wide_ref[4 + k, here, :] = d_hidden_pre[:, k * 512 : (k + 1) * 512]
        d_middle = dpre_ref[here, :] + dot(d_hidden_pre, w12_ref[0], 1, 1)
        n1 = dmid_ref[here, :]
        d_mid = norm_back(d_middle, n1, recip_ref[here, :], gain[0:1])
        dmid_ref[here, :] = d_mid
        d_branch = (d_mid + jnp.where(kept(t), dc_ref[here, :].astype(F32), 0.0)).astype(BF)
        dbt_ref[:, :, here] = d_branch.T.reshape(batches, rows, block)
        dat_ref[:, :, here] = dot(wo_ref[...], d_branch, 0, 1).astype(BF).reshape(NHEADS, DH, block)
        norm_send[0] = norm_send[0] + jnp.concatenate(
            [over_tokens(d_middle * n1), zero, over_tokens(d_middle), zero], axis=0
        )
        for k in range(groups):
            pl.when(t == k)(pieces[k].hop1)

    norm_push(0)
    for k in range(groups, parts):
        weight_piece(k)
    dwo = dot(in_slots(dbt_ref), at_ref[...].reshape(D, SEQ_LEN), 1, 1).astype(BF)
    empty = jnp.zeros((D, DH), BF)
    for h in range(NHEADS):
        dwo_ref[h] = jnp.concatenate([empty, dwo[:, h * DH : (h + 1) * DH]], axis=1)

    half = parts // 2
    todo = [[] for _ in range(NHEADS + 1)]
    early, late = pieces[:half], pieces[half:]
    for n, chunk in enumerate(chunks):
        todo[n].append(chunk.hop0)
        if n + 1 < len(chunks):
            todo[n + 1].append(chunk.hop1)
    for k in range(4):
        todo[2 * k] += [functools.partial(norm_pull, k), functools.partial(norm_push, k + 1)]
    for t, hop, some in REDUCE_PLAN:
        todo[t] += [getattr(p, hop) for p in (early, late)[some]]

    def backward_transfers(t):
        for act in todo[t]:
            act()

    backward_transfers(-1)

    @pl.loop(0, NHEADS)
    def _(i):
        p_fetch(i).wait()
        g, r = i // heads, i % heads
        cc, xx = r % 2, lax.rem(x + X - 1 - r // 2, X)
        head = (xx * 2 + cc) * groups + g
        lane = lax.broadcasted_iota(jnp.int32, (SEQ_LEN, 128), 1)
        row = lax.broadcasted_iota(jnp.int32, (DH, SEQ_LEN), 0)
        qk, vx = qk_ref[head], vx_ref[head]
        do = dat_ref[head].astype(F32) * linv_ref[head]
        inner = -jnp.sum(do * at_ref[head].astype(F32), axis=0, keepdims=True)
        coarse = inner.astype(BF).astype(F32)
        tail = jnp.where(row == 0, coarse, jnp.where(row == 1, inner - coarse, 0.0))
        et = jnp.concatenate([do, tail], axis=0).astype(BF)
        e = et.T
        kt = qk.T[DH:]
        kq = jnp.concatenate([qk[:, DH:], qk[:, :DH]], axis=1)
        dk = jnp.zeros((SEQ_LEN, 128), F32)
        dv = jnp.zeros((SEQ_LEN, 128), F32)
        dqs = []
        slot = lax.rem(i, 2)
        for b in range(2):
            sl = slice(b * (SEQ_LEN // 2), (b + 1) * (SEQ_LEN // 2))
            p = wide_ref[2 * slot + b]
            ds = (p.astype(F32) * dot(vx, et[:, sl], 1, 0)).astype(BF)
            dv = dv + dot(p, e[sl], 1, 0)
            dk = dk + dot(ds, kq[sl], 1, 0)
            dqs.append(dot(kt, ds, 1, 0))
        dqt = jnp.concatenate(dqs, axis=1) * F32(DH**-0.5)
        dq = jnp.concatenate([dqt, jnp.zeros_like(dqt)], axis=0).T
        d_proj = jnp.concatenate([jnp.where(lane < DH, dq, dk), jnp.where(lane < DH, dv, 0.0)], axis=1).astype(BF)
        cols = pl.ds(pl.multiple_of(head * PART, PART), PART)
        w12_ref[0, :, cols] = d_proj[: SEQ_LEN // 2]
        w12_ref[1, :, cols] = d_proj[SEQ_LEN // 2 :]
        dw = dot(xst_ref[...], d_proj, 1, 0)
        dw = jnp.concatenate([dw[:, :128], dw[:, 128:] + dwo_ref[head].astype(F32)], axis=1).astype(BF)
        dqkv_ref[g, cc, xx] = dw.reshape(dqkv_ref.shape[3:])

        @pl.when(i + 2 < NHEADS)
        def _():
            p_fetch(i + 2).start()

        for t in range(NHEADS):
            pl.when(i == t)(functools.partial(backward_transfers, t))

    for k in range(4, len(partners)):
        norm_pull(k)
        if k + 1 < len(partners):
            norm_push(k + 1)
    norm_out[...] = norm_send[len(partners)]
    chunks[-1].hop1()
    table = []
    for h in range(NHEADS):
        g, xx, cc = h % groups, (h // groups) // 2, (h // groups) % 2
        table.append(ga_ref[cc, xx, :, :, g].reshape(D, PART))
    table = jnp.concatenate(table, axis=1)
    dpost = []
    for k in range(2):
        here = slice(k * (SEQ_LEN // 2), (k + 1) * (SEQ_LEN // 2))
        ordered = dot(w12_ref[k], table, 1, 1).astype(BF)
        dmid_ref[here, :] = dmid_ref[here, :] + dot(ordered, pick_ref[...], 1, 1)
        dpost.append(pltpu.make_async_copy(dmid_ref.at[here], dpost_out.at[here], in_sems.at[k]))
        dpost[k].start()
    for piece in pieces[len(pieces) // 2 :]:
        piece.hop4()
    for g in range(groups):
        low = g * GROUPW
        grad_ref[:, low + PART : low + 2 * PART] = final[groups + g]
        grad_ref[:, low + 2 * PART : low + 3 * PART] = final[g]
        grad_ref[:, low : low + PART] = collect(place, dqkv_ref.at[g], qr2.at[g], recv_q.at[g], send_r.at[0])
    for copy in dpost:
        copy.wait()
    for n in range(len(outs)):
        for t in range(MID_STEPS):
            store(n, t).wait()
    reduce_sends.drain(place)


def layer_call(owner, lengths, gain, bias, post, weights, dual, pc, dc, batches, heads):
    groups, rows = NHEADS // heads, D // batches
    parts = 2 * groups
    X = Y = heads // 2
    Z = batches // Y
    tokens = post.shape[0]
    assert tokens == SEQ_LEN
    stages = 1 + sum(len(bits(v)) for v in (X, Y, Z))
    smem, vmem = pl.BlockSpec(memory_space=pltpu.SMEM), pl.BlockSpec(memory_space=pltpu.VMEM)
    far = pl.BlockSpec(memory_space=pl.ANY)
    outs = [
        jax.ShapeDtypeStruct((tokens, D), BF),
        jax.ShapeDtypeStruct((tokens, D), F32),
        jax.ShapeDtypeStruct((tokens, D), F32),
        jax.ShapeDtypeStruct((rows, groups * GROUPW), F32),
        jax.ShapeDtypeStruct((4, D), F32),
        jax.ShapeDtypeStruct((NHEADS, 2, tokens, tokens // 2), BF),
    ]
    dma = pltpu.SemaphoreType.DMA
    x_parts = sum(k < parts for k in X_FIRST)
    return pl.pallas_call(
        functools.partial(layer_kernel, batches, heads),
        in_specs=[smem, smem, vmem, vmem] + [far] * 5,
        out_specs=[far, far, far, vmem, vmem, far],
        out_shape=outs,
        scratch_shapes=[
            pltpu.VMEM((tokens, D), BF),
            pltpu.VMEM(weights.shape, F32),
            pltpu.VMEM((tokens, D), F32),
            pltpu.VMEM((tokens, D), BF),
            pltpu.VMEM((tokens, D), F32),
            pltpu.VMEM((tokens, D), F32),
            pltpu.VMEM((tokens, 1), F32),
            pltpu.VMEM((D, D), BF),
            pltpu.VMEM((tokens, D), BF),
            pltpu.VMEM((D, tokens), BF),
            pltpu.VMEM((2, X, Z, Y, groups, rows, PART), BF),
            pltpu.VMEM((parts, 2, X, Z, Y, rows, PART), BF),
            pltpu.VMEM((NHEADS, tokens, 128), BF),
            pltpu.VMEM((NHEADS, tokens, 128), BF),
            pltpu.VMEM((8, tokens, tokens // 2), BF),
            pltpu.VMEM((NHEADS, 1, tokens), F32),
            pltpu.VMEM((NHEADS, DH, tokens), BF),
            pltpu.VMEM((NHEADS, DH, tokens), BF),
            pltpu.VMEM((2, D, FF), BF),
            pltpu.VMEM((D, D), BF),
            pltpu.VMEM((batches, rows, tokens), BF),
            pltpu.VMEM((batches, rows, tokens), BF),
            pltpu.VMEM((batches, rows, tokens), BF),
            pltpu.VMEM((NHEADS, D, 128), BF),
            pltpu.VMEM((groups, 2, X, batches, rows, PART), BF),
            pltpu.VMEM((parts, X, Z, Y, rows, PART), BF),
            pltpu.VMEM((x_parts, X - 1, Z, Y, rows, PART), BF),
            pltpu.VMEM((parts - x_parts, Y - 1, X, Z, rows, PART), BF),
            pltpu.VMEM((x_parts, Z, Y, rows, PART), BF),
            pltpu.VMEM((parts - x_parts, X, Z, rows, PART), BF),
            pltpu.VMEM((parts, X - 1, Z, rows, PART), BF),
            pltpu.VMEM((parts, Z, rows, PART), BF),
            pltpu.VMEM((parts, Z - 1, rows, PART), BF),
            pltpu.VMEM((parts, rows, PART), F32),
            pltpu.VMEM((groups, X, batches, rows, PART), BF),
            pltpu.VMEM((groups, X - 1, batches, rows, PART), BF),
            pltpu.VMEM((groups, batches - 1, rows, PART), BF),
            pltpu.VMEM((stages + 1, 4, D), F32),
            pltpu.VMEM((stages, 4, D), F32),
            dma((groups, Z)),
            dma((groups, Z, Y)),
            dma((X, Z + Y)),
            dma((X,)),
            dma((2, X, Z, Y)),
            dma((forward_sends(X, Y, Z, groups),)),
            dma((parts, 2 * X + Z)),
            dma((groups, 2 * X + batches)),
            dma((stages,)),
            dma((backward_sends(X, Y, Z, groups),)),
            dma((4,)),
            dma((5,)),
            dma((2, MID_STEPS)),
        ],
        name="layer",
        compiler_params=pltpu.CompilerParams(
            collective_id=1, has_side_effects=True, vmem_limit_bytes=VMEM_BYTES
        ),
    )(owner, lengths, gain, bias, post, weights, dual, pc, dc)


def update_kernel(
    post_in, dual_in, dpost_in, grad_ref, weight_ref, first_ref, second_ref,
    ngrad_ref, gain_ref, bias_ref, nfirst_ref, nsecond_ref,
    post_out, dual_out, dpost_out, first_out, second_out, weight_out, nfirst_out, nsecond_out, nparam_out,
):
    post_out[...] = post_in[...]
    dual_out[...] = dual_in[...]
    dpost_out[...] = dpost_in[...]
    first_out[...], second_out[...], weight_out[...] = adam_update(
        weight_ref[...], grad_ref[...], first_ref[...], second_ref[...], WEIGHT_RATE, WEIGHT_DECAY
    )
    nparam = jnp.concatenate([gain_ref[...], bias_ref[...]], axis=0)
    nfirst_out[...], nsecond_out[...], nparam_out[...] = adam_update(
        nparam, ngrad_ref[...], nfirst_ref[...], nsecond_ref[...], NORM_RATE, 0.0
    )


def update_call(post, dual, dpost, grad, weights, first, second, ngrad, gain, bias, nfirst, nsecond):
    steps = 2
    cut = lambda a: pl.BlockSpec((a.shape[0] // steps, a.shape[1]), lambda i: (i, 0))
    same = lambda a: pl.BlockSpec(a.shape, lambda i: (0, 0))
    outs = [post, dual, dpost, weights, weights, weights, nfirst, nfirst, nfirst]
    return pl.pallas_call(
        update_kernel,
        grid=(steps,),
        in_specs=[cut(a) for a in (post, dual, dpost, grad, weights, first, second)]
        + [same(a) for a in (ngrad, gain, bias, nfirst, nsecond)],
        out_specs=[cut(a) for a in outs[:6]] + [same(a) for a in outs[6:]],
        out_shape=[jax.ShapeDtypeStruct(a.shape, a.dtype) for a in outs],
        name="update",
        compiler_params=pltpu.CompilerParams(vmem_limit_bytes=VMEM_BYTES),
    )(post, dual, dpost, grad, weights, first, second, ngrad, gain, bias, nfirst, nsecond)


def shards(
    post_stream,
    dual_stream,
    post_cotangent,
    dual_cotangent,
    seq_lengths,
    owner_slots,
    weights,
    first_moment,
    second_moment,
    norm_gain,
    norm_bias,
    norm_first,
    norm_second,
):
    batches, heads = lax.axis_size("batch"), lax.axis_size("head")
    post, dual, dpost, grad, norm_grad, _ = layer_call(
        owner_slots, seq_lengths, norm_gain, norm_bias, post_stream, weights, dual_stream, post_cotangent,
        dual_cotangent, batches, heads,
    )
    return update_call(
        post, dual, dpost, grad, weights, first_moment, second_moment,
        norm_grad, norm_gain, norm_bias, norm_first, norm_second,
    )


def solution(mesh):
    tokens, table, copied = P(("batch", "head"), None), P("batch", "head"), P()
    in_specs = (tokens,) * 4 + (P("batch"), copied) + (table,) * 3 + (copied,) * 4
    out_specs = (tokens,) * 3 + (table,) * 3 + (copied,) * 3
    return jax.shard_map(shards, mesh=mesh, in_specs=in_specs, out_specs=out_specs, check_vma=False)
```
